32 devices in a mesh: dp: 8 (over z, y), seq: 4 (over x, core).
Axes of the slice: x: 2, y: 2, z: 4, core: 2. Of those that a mesh axis runs over, the one named last changes fastest.
Arguments:
- tokens: bfloat16 [16, 768, 1152], P('dp', 'seq'), may hold values from -12 to 12
- cotangent: bfloat16 [16, 768, 1152], P('dp', 'seq'), may hold values from -6 to 6
- condition: bfloat16 [16, 3, 1152], P('dp'), may hold values from -6 to 6
- item_lengths: int32 [16, 3], P('dp'), may hold values from 48 to 672, as said below
- item_widths: int32 [16, 3], P('dp'), may hold values from 4 to 32
- qkv_weight: float32 [1152, 3456], P('dp', 'seq'), may hold values from -0.1875 to 0.1875
- qkv_first: float32 [1152, 3456], P('dp', 'seq'), may hold values from -0.00030517578 to 0.00030517578
- qkv_second: float32 [1152, 3456], P('dp', 'seq'), may hold values from 2.2019542e-09 to 8.791072e-09
- out_weight: float32 [1152, 1152], P('dp', 'seq'), may hold values from -1.25 to 1.25
- out_first: float32 [1152, 1152], P('dp', 'seq'), may hold values from -0.00030517578 to 0.00030517578
- out_second: float32 [1152, 1152], P('dp', 'seq'), may hold values from 2.2019542e-09 to 8.791072e-09
- gateup_weight: float32 [1152, 6144], P('dp', 'seq'), may hold values from -0.1875 to 0.1875
- gateup_first: float32 [1152, 6144], P('dp', 'seq'), may hold values from -0.00030517578 to 0.00030517578
- gateup_second: float32 [1152, 6144], P('dp', 'seq'), may hold values from 2.2019542e-09 to 8.791072e-09
- down_weight: float32 [3072, 1152], P('dp', 'seq'), may hold values from -0.109375 to 0.109375
- down_first: float32 [3072, 1152], P('dp', 'seq'), may hold values from -0.00030517578 to 0.00030517578
- down_second: float32 [3072, 1152], P('dp', 'seq'), may hold values from 2.2019542e-09 to 8.791072e-09
- mod_weight: float32 [1152, 6912], P('dp', 'seq'), may hold values from -0.1875 to 0.1875
- mod_first: float32 [1152, 6912], P('dp', 'seq'), may hold values from -0.00030517578 to 0.00030517578
- mod_second: float32 [1152, 6912], P('dp', 'seq'), may hold values from 2.2019542e-09 to 8.791072e-09
- mod_bias: float32 [6912], P('seq'), may hold values from -0.6 to 0.6
- bias_first: float32 [6912], P('seq'), may hold values from -0.0012207031 to 0.0012207031
- bias_second: float32 [6912], P('seq'), may hold values from 3.524801e-08 to 1.4107577e-07
- qk_gains: float32 [2, 72], replicated, may hold values from -0.4 to 0.4
- gains_first: float32 [2, 72], replicated, may hold values from -0.0012207031 to 0.0012207031
- gains_second: float32 [2, 72], replicated, may hold values from 3.524801e-08 to 1.4107577e-07
Outputs:
- layer_out: bfloat16 [16, 768, 1152], P('dp', 'seq')
- tokens_grad: bfloat16 [16, 768, 1152], P('dp', 'seq')
- grad_norm: float32 [], replicated
- qkv_master: float32 [1152, 3456], P('dp', 'seq')
- qkv_moment: float32 [1152, 3456], P('dp', 'seq')
- qkv_square: float32 [1152, 3456], P('dp', 'seq')
- out_master: float32 [1152, 1152], P('dp', 'seq')
- out_moment: float32 [1152, 1152], P('dp', 'seq')
- out_square: float32 [1152, 1152], P('dp', 'seq')
- gateup_master: float32 [1152, 6144], P('dp', 'seq')
- gateup_moment: float32 [1152, 6144], P('dp', 'seq')
- gateup_square: float32 [1152, 6144], P('dp', 'seq')
- down_master: float32 [3072, 1152], P('dp', 'seq')
- down_moment: float32 [3072, 1152], P('dp', 'seq')
- down_square: float32 [3072, 1152], P('dp', 'seq')
- mod_master: float32 [1152, 6912], P('dp', 'seq')
- mod_moment: float32 [1152, 6912], P('dp', 'seq')
- mod_square: float32 [1152, 6912], P('dp', 'seq')
- bias_master: float32 [6912], P('seq')
- bias_moment: float32 [6912], P('seq')
- bias_square: float32 [6912], P('seq')
- gains_master: float32 [2, 72], replicated
- gains_moment: float32 [2, 72], replicated
- gains_square: float32 [2, 72], replicated
The draws below stay inside these ranges and needn't reach their ends.
Inputs may be any that keep to these rules, and one draw needn't show every extreme that they name: `item_lengths`: each pack holds 3 images in order; the first and the last hold fewer than a quarter of 768 tokens each, the middle one the rest.
All inputs are finite; a program needn't handle non-finite values.
Results may differ from the reference program's by a relative error of at most 0.01.
Values may be sent and summed in bfloat16 or wider, within the bound.
A program may use at most 256 MiB of HBM per device.

```python
import math
import jax
import jax.numpy as jnp
from jax import lax

D = 1152
HEADS = 16
FF = 3072
HD = 72
PACK_LEN = 768
ITEMS = 3
OPT_STEP = 10
PACKS = 16


def draw_tokens(key, part):
    key = jax.random.fold_in(key, 11)
    ramp_scale = jnp.arange(D, dtype=jnp.float32) / (D - 1)
    base_draw = jnp.clip(jax.random.normal(key, (PACKS, PACK_LEN, D), jnp.float32), -4.0, 4.0)
    feature_scale = 1.0 + 2.0 * ramp_scale
    return (base_draw * feature_scale).astype(jnp.bfloat16)


def draw_item_lengths(key, part):
    key = jax.random.fold_in(key, 23)
    quarter = PACK_LEN // 4
    shortest = PACK_LEN // 16
    first_key, last_key = jax.random.split(key)
    first_len = jax.random.randint(first_key, (PACKS,), shortest, quarter, dtype=jnp.int32)
    last_len = jax.random.randint(last_key, (PACKS,), shortest, quarter, dtype=jnp.int32)
    leading = jnp.arange(PACKS, dtype=jnp.int32) == 0
    first_len = jnp.where(leading, shortest, first_len).astype(jnp.int32)
    last_len = jnp.where(leading, shortest, last_len).astype(jnp.int32)
    middle = (PACK_LEN - first_len - last_len).astype(jnp.int32)
    return jnp.stack([first_len, middle, last_len], axis=1).astype(jnp.int32)


def place_ends(entries, stream_key, least, top_value):
    spot = [jax.random.randint(jax.random.fold_in(stream_key, axis), (), 0, length) for axis, length in enumerate(entries.shape)]
    longest = entries.shape.index(max(entries.shape))
    neighbour = spot[:longest] + [(spot[longest] + 1) % entries.shape[longest]] + spot[longest + 1:]
    return entries.at[tuple(spot)].set(least).at[tuple(neighbour)].set(top_value)


def levels(rng, dims, pieces, smallest, high):
    def one(position, parts):
        steps = jax.random.uniform(jax.random.fold_in(jax.random.fold_in(rng, 6), position), (parts,), jnp.float32, smallest / len(pieces), high / len(pieces))
        return jnp.repeat(jnp.exp(steps), dims[position] // parts).reshape((-1,) + (1,) * (len(dims) - position - 1))

    factor_of = one(*pieces[0])
    for cut in pieces[1:]:
        factor_of = factor_of * one(*cut)
    return factor_of


def normal_values(own_key, shape, scale, most, shards=(), kind=jnp.bfloat16):
    values = scale * jax.random.normal(own_key, shape, jnp.float32)
    if shards:
        values = values * levels(own_key, shape, shards, -0.22, 0.18)
    return jnp.clip(values, -most, most).astype(kind)


def setup_inputs(seed: int = 0) -> dict:
    key_of = jax.random.split(jax.random.key(seed), 27)
    return {
        "tokens": draw_tokens(jax.random.fold_in(key_of[26], 71), 0),
        "cotangent": normal_values(key_of[1], (PACKS, PACK_LEN, D), 1.0, 6.0, ((0, 8), (1, 4))),
        "condition": normal_values(key_of[2], (PACKS, ITEMS, D), 1.0, 6.0, ((0, 8),)),
        "item_lengths": draw_item_lengths(jax.random.fold_in(key_of[26], 71), 0),
        "item_widths": place_ends(jax.random.randint(key_of[4], (PACKS, ITEMS), 4, 33), jax.random.fold_in(key_of[4], 1), 4, 32).astype(jnp.int32),
        "qkv_weight": normal_values(key_of[5], (D, 3 * D), D ** -0.5, 0.1875, ((0, 8), (1, 4)), jnp.float32),
        "qkv_first": normal_values(key_of[6], (D, 3 * D), (0.111 * (10 * D * D + 3 * D * FF) ** -0.5), 0.00030517578, ((0, 8), (1, 4)), jnp.float32),
        "qkv_second": jnp.clip(jnp.exp(math.log(8.79107187046202e-09) - 1.3843914 * jax.random.uniform(key_of[7], (D, 3 * D), jnp.float32) ** levels(key_of[7], (D, 3 * D), ((0, 8), (1, 4)), -0.2, 0.2)), 2.2019541745521565e-09, 8.79107187046202e-09),
        "out_weight": normal_values(key_of[8], (D, D), (D * 16 // PACK_LEN) ** -0.5, 1.25, ((0, 8), (1, 4)), jnp.float32),
        "out_first": normal_values(key_of[9], (D, D), (0.111 * (10 * D * D + 3 * D * FF) ** -0.5), 0.00030517578, ((0, 8), (1, 4)), jnp.float32),
        "out_second": jnp.clip(jnp.exp(math.log(8.79107187046202e-09) - 1.3843914 * jax.random.uniform(key_of[10], (D, D), jnp.float32) ** levels(key_of[10], (D, D), ((0, 8), (1, 4)), -0.2, 0.2)), 2.2019541745521565e-09, 8.79107187046202e-09),
        "gateup_weight": normal_values(key_of[11], (D, 2 * FF), D ** -0.5, 0.1875, ((0, 8), (1, 4)), jnp.float32),
        "gateup_first": normal_values(key_of[12], (D, 2 * FF), (0.111 * (10 * D * D + 3 * D * FF) ** -0.5), 0.00030517578, ((0, 8), (1, 4)), jnp.float32),
        "gateup_second": jnp.clip(jnp.exp(math.log(8.79107187046202e-09) - 1.3843914 * jax.random.uniform(key_of[13], (D, 2 * FF), jnp.float32) ** levels(key_of[13], (D, 2 * FF), ((0, 8), (1, 4)), -0.2, 0.2)), 2.2019541745521565e-09, 8.79107187046202e-09),
        "down_weight": normal_values(key_of[14], (FF, D), FF ** -0.5, 0.109375, ((0, 8), (1, 4)), jnp.float32),
        "down_first": normal_values(key_of[15], (FF, D), (0.111 * (10 * D * D + 3 * D * FF) ** -0.5), 0.00030517578, ((0, 8), (1, 4)), jnp.float32),
        "down_second": jnp.clip(jnp.exp(math.log(8.79107187046202e-09) - 1.3843914 * jax.random.uniform(key_of[16], (FF, D), jnp.float32) ** levels(key_of[16], (FF, D), ((0, 8), (1, 4)), -0.2, 0.2)), 2.2019541745521565e-09, 8.79107187046202e-09),
        "mod_weight": normal_values(key_of[17], (D, 6 * D), D ** -0.5, 0.1875, ((0, 8), (1, 4)), jnp.float32),
        "mod_first": normal_values(key_of[18], (D, 6 * D), (0.111 * (10 * D * D + 3 * D * FF) ** -0.5), 0.00030517578, ((0, 8), (1, 4)), jnp.float32),
        "mod_second": jnp.clip(jnp.exp(math.log(8.79107187046202e-09) - 1.3843914 * jax.random.uniform(key_of[19], (D, 6 * D), jnp.float32) ** levels(key_of[19], (D, 6 * D), ((0, 8), (1, 4)), -0.2, 0.2)), 2.2019541745521565e-09, 8.79107187046202e-09),
        "mod_bias": normal_values(key_of[20], (6 * D,), 0.15, 0.6, ((0, 4),), jnp.float32),
        "bias_first": normal_values(key_of[21], (6 * D,), (0.444 * (10 * D * D + 3 * D * FF) ** -0.5), 0.0012207031, ((0, 4),), jnp.float32),
        "bias_second": jnp.clip(jnp.exp(math.log(1.4107577328559273e-07) - 1.386888 * jax.random.uniform(key_of[22], (6 * D,), jnp.float32) ** levels(key_of[22], (6 * D,), ((0, 4),), -0.2, 0.2)), 3.524801073240269e-08, 1.4107577328559273e-07),
        "qk_gains": normal_values(key_of[23], (2, HD), 0.1, 0.4, (), jnp.float32),
        "gains_first": normal_values(key_of[24], (2, HD), (0.444 * (10 * D * D + 3 * D * FF) ** -0.5), 0.0012207031, (), jnp.float32),
        "gains_second": jnp.clip(jnp.exp(jax.random.uniform(key_of[25], (2, HD), jnp.float32, math.log(3.524801073240269e-08), math.log(1.4107577328559273e-07))), 3.524801073240269e-08, 1.4107577328559273e-07),
    }


@jax.custom_vjp
def low(v):
    return lax.optimization_barrier(v.astype(jnp.bfloat16)).astype(jnp.float32)

@jax.custom_vjp
def low_back(v):
    return v

def low_keep(v):
    return (low(v), None)

def low_pass(kept, grad):
    return (grad,)

def back_keep(v):
    return (v, None)

def back_low(kept, grad):
    return (low(grad),)
low.defvjp(low_keep, low_pass)
low_back.defvjp(back_keep, back_low)
highest = lax.Precision.HIGHEST
norm_eps = 1e-06
clip_limit = 1.0
beta_one = 0.9
beta_two = 0.95
adam_eps = 1e-08
learn_rate = 0.06
decay_rate = 0.01
masked_score = -1e+30

def pack_layout(lengths, widths):
    lengths = lengths.astype(jnp.int32)
    widths = widths.astype(jnp.int32)
    item_ends = jnp.cumsum(lengths).astype(jnp.int32)
    starts = (item_ends - lengths).astype(jnp.int32)
    places = jnp.arange(PACK_LEN, dtype=jnp.int32)
    item_ids = lax.optimization_barrier(jnp.sum((places[:, None] >= item_ends[None, :]).astype(jnp.int32), axis=1)).astype(jnp.int32)
    chosen = (item_ids[:, None] == jnp.arange(ITEMS, dtype=jnp.int32)[None, :]).astype(jnp.int32)
    offsets = (places - lax.optimization_barrier(jnp.sum(chosen * starts[None, :], axis=1))).astype(jnp.int32)
    span_width = lax.optimization_barrier(jnp.sum(chosen * widths[None, :], axis=1)).astype(jnp.int32)
    return (item_ids, (offsets // span_width).astype(jnp.int32), (offsets % span_width).astype(jnp.int32))

def rotary_tables(row_pos, col_pos):
    quarter = HD // 4
    frequency = 10000.0 ** (-jnp.arange(quarter, dtype=jnp.float32) / quarter)
    angle_row = row_pos.astype(jnp.float32)[..., None] * frequency
    angle_col = col_pos.astype(jnp.float32)[..., None] * frequency
    return (jnp.cos(angle_row)[..., None, :], jnp.sin(angle_row)[..., None, :], jnp.cos(angle_col)[..., None, :], jnp.sin(angle_col)[..., None, :])

def rotate(half_vec, cos_table, sin_table):
    quarter = half_vec.shape[-1] // 2
    leading = half_vec[..., :quarter]
    trailing = half_vec[..., quarter:]
    return jnp.concatenate([leading * cos_table - trailing * sin_table, trailing * cos_table + leading * sin_table], axis=-1)

def rotary(vectors, tables):
    half_width = vectors.shape[-1] // 2
    return jnp.concatenate([rotate(vectors[..., :half_width], tables[0], tables[1]), rotate(vectors[..., half_width:], tables[2], tables[3])], axis=-1)

def head_norm(vectors, gain_row):
    return vectors * lax.rsqrt(lax.optimization_barrier(jnp.mean(vectors * vectors, axis=-1, keepdims=True)) + norm_eps) * (1.0 + gain_row)

def layer_norm(activations):
    centered = activations - lax.optimization_barrier(jnp.mean(activations, axis=-1, keepdims=True))
    return centered * lax.rsqrt(lax.optimization_barrier(jnp.mean(centered * centered, axis=-1, keepdims=True)) + norm_eps)

def pack_forward(params, tokens, condition, item_ids, tables):
    qkv_weight, out_weight, gateup_weight, down_weight, mod_weight, mod_bias, qk_gains = params
    length = tokens.shape[0]
    cond_act = low(jax.nn.silu(condition))
    modulation = low(jnp.dot(cond_act, low(mod_weight), precision=highest) + mod_bias)
    chosen = (item_ids[:, None] == jnp.arange(ITEMS, dtype=jnp.int32)[None, :]).astype(jnp.float32)
    per_token = jnp.dot(chosen, modulation, precision=highest)
    shift_attn, scale_attn, gate_attn, shift_ffn, scale_ffn, gate_ffn = jnp.split(per_token, 6, axis=1)
    normed = low(layer_norm(tokens) * (1.0 + scale_attn) + shift_attn)
    projected = low_back(jnp.dot(normed, low(qkv_weight), precision=highest)).reshape(length, 3, HEADS, HD)
    queries = low(rotary(head_norm(projected[:, 0], qk_gains[0]), tables) * (1.0 / math.sqrt(HD)))
    key_rows = low(rotary(head_norm(projected[:, 1], qk_gains[1]), tables))
    value_rows = low(projected[:, 2])
    raw_scores = low_back(jnp.einsum('qhd,khd->hqk', queries, key_rows, precision=highest))
    same_item = (item_ids[:, None] == item_ids[None, :])[None]
    scores = jnp.where(same_item, raw_scores, masked_score)
    top_score = lax.optimization_barrier(jnp.max(scores, axis=-1, keepdims=True))
    exp_scores = jnp.exp(scores - top_score)
    attention = exp_scores / lax.optimization_barrier(jnp.sum(exp_scores, axis=-1, keepdims=True))
    mixed_heads = low(low_back(jnp.einsum('hqk,khd->qhd', low(attention), value_rows, precision=highest))).reshape(length, D)
    attended = low_back(jnp.dot(mixed_heads, low(out_weight), precision=highest))
    middle = tokens + gate_attn * attended
    normed_ffn = low(layer_norm(middle) * (1.0 + scale_ffn) + shift_ffn)
    gate_up = low_back(jnp.dot(normed_ffn, low(gateup_weight), precision=highest))
    hidden = low(jax.nn.silu(gate_up[:, :FF]) * gate_up[:, FF:])
    branch = low_back(jnp.dot(hidden, low(down_weight), precision=highest))
    return middle + gate_ffn * branch

def adam_update(master, moment, square, gradient, factor):
    clipped = gradient * factor
    moment_new = beta_one * moment + (1.0 - beta_one) * clipped
    square_new = beta_two * square + (1.0 - beta_two) * clipped * clipped
    moment_hat = moment_new / (1.0 - beta_one ** OPT_STEP)
    square_hat = square_new / (1.0 - beta_two ** OPT_STEP)
    master_new = master - learn_rate * (moment_hat / (jnp.sqrt(square_hat) + adam_eps) + decay_rate * master)
    return (master_new, moment_new, square_new)

def reference(tokens, cotangent, condition, item_lengths, item_widths, qkv_weight, qkv_first, qkv_second, out_weight, out_first, out_second, gateup_weight, gateup_first, gateup_second, down_weight, down_first, down_second, mod_weight, mod_first, mod_second, mod_bias, bias_first, bias_second, qk_gains, gains_first, gains_second):
    params = (qkv_weight, out_weight, gateup_weight, down_weight, mod_weight, mod_bias, qk_gains)

    def one_pack(totals, pack_data):
        pack_tokens, pack_cot, pack_cond, lengths, widths = pack_data
        item_ids, row_pos, col_pos = pack_layout(lengths, widths)
        tables = rotary_tables(row_pos, col_pos)

        def forward(weights, inputs):
            return pack_forward(weights, inputs, pack_cond.astype(jnp.float32), item_ids, tables)
        output, pullback = jax.vjp(forward, params, pack_tokens.astype(jnp.float32))
        gradients, input_grad = pullback(pack_cot.astype(jnp.float32))
        totals = jax.tree.map(lambda running, addend: running + addend, totals, gradients)
        return (totals, (output.astype(jnp.bfloat16), input_grad.astype(jnp.bfloat16)))
    zero_grads = jax.tree.map(jnp.zeros_like, params)
    gradients, outputs = lax.scan(one_pack, zero_grads, (tokens, cotangent, condition, item_lengths, item_widths))
    layer_out, tokens_grad = outputs
    square_sum = jnp.float32(0.0)
    for gradient in gradients:
        square_sum = square_sum + jnp.sum(gradient * gradient)
    grad_norm = jnp.sqrt(square_sum)
    factor = clip_limit / jnp.maximum(grad_norm, clip_limit)
    qkv_new = adam_update(qkv_weight, qkv_first, qkv_second, gradients[0], factor)
    out_new = adam_update(out_weight, out_first, out_second, gradients[1], factor)
    gateup_new = adam_update(gateup_weight, gateup_first, gateup_second, gradients[2], factor)
    down_new = adam_update(down_weight, down_first, down_second, gradients[3], factor)
    mod_new = adam_update(mod_weight, mod_first, mod_second, gradients[4], factor)
    bias_new = adam_update(mod_bias, bias_first, bias_second, gradients[5], factor)
    gains_new = adam_update(qk_gains, gains_first, gains_second, gradients[6], factor)
    return (layer_out, tokens_grad, grad_norm, qkv_new[0], qkv_new[1], qkv_new[2], out_new[0], out_new[1], out_new[2], gateup_new[0], gateup_new[1], gateup_new[2], down_new[0], down_new[1], down_new[2], mod_new[0], mod_new[1], mod_new[2], bias_new[0], bias_new[1], bias_new[2], gains_new[0], gains_new[1], gains_new[2])
```

```python
from functools import partial
import math

import jax
import jax.numpy as jnp
from jax import lax
from jax.sharding import PartitionSpec as P

HEADS = 16
OPT_STEP = 10


highest = lax.Precision.HIGHEST
norm_eps = 1e-06
clip_limit = 1.0
beta_one = 0.9
beta_two = 0.95
adam_eps = 1e-08
learn_rate = 0.06
decay_rate = 0.01
masked_score = -1e30


def pack_layout(lengths, widths, span):
    item_count = lengths.shape[0]
    item_ends = jnp.cumsum(lengths)
    starts = item_ends - lengths
    places = jnp.arange(span, dtype=jnp.int32)
    item_ids = jnp.sum((places[:, None] >= item_ends[None, :]).astype(jnp.int32), axis=1)
    chosen = (item_ids[:, None] == jnp.arange(item_count, dtype=jnp.int32)[None, :]).astype(
        jnp.int32
    )
    offsets = places - jnp.sum(chosen * starts[None, :], axis=1)
    span_width = jnp.sum(chosen * widths[None, :], axis=1)
    return (item_ids, offsets // span_width, offsets % span_width)


def rotary_tables(row_pos, col_pos, quarter):
    frequency = 10000.0 ** (-jnp.arange(quarter, dtype=jnp.float32) / quarter)
    angle_row = row_pos.astype(jnp.float32)[..., None] * frequency
    angle_col = col_pos.astype(jnp.float32)[..., None] * frequency
    return (
        jnp.cos(angle_row)[..., None, :],
        jnp.sin(angle_row)[..., None, :],
        jnp.cos(angle_col)[..., None, :],
        jnp.sin(angle_col)[..., None, :],
    )


def rotate(half_vec, cos_table, sin_table):
    quarter = half_vec.shape[-1] // 2
    leading = half_vec[..., :quarter]
    trailing = half_vec[..., quarter:]
    return jnp.concatenate(
        [leading * cos_table - trailing * sin_table, trailing * cos_table + leading * sin_table],
        axis=-1,
    )


def rotary(vectors, tables):
    half_width = vectors.shape[-1] // 2
    return jnp.concatenate(
        [
            rotate(vectors[..., :half_width], tables[0], tables[1]),
            rotate(vectors[..., half_width:], tables[2], tables[3]),
        ],
        axis=-1,
    )


def head_norm(vectors, gain_row):
    return (
        vectors
        * lax.rsqrt(jnp.mean(vectors * vectors, axis=-1, keepdims=True) + norm_eps)
        * (1.0 + gain_row)
    )


def norm_back(raw_rows, gain_row, incoming):
    inverse = lax.rsqrt(jnp.mean(raw_rows * raw_rows, axis=-1, keepdims=True) + norm_eps)
    unit_rows = raw_rows * inverse
    scaled = incoming * (1.0 + gain_row)
    grad_raw = inverse * (scaled - unit_rows * jnp.mean(scaled * unit_rows, axis=-1, keepdims=True))
    grad_gain = jnp.sum(incoming * unit_rows, axis=(0, 1, 2))
    return (grad_raw, grad_gain)


def layer_stats(activations):
    centered = activations - jnp.mean(activations, axis=-1, keepdims=True)
    inverse = lax.rsqrt(jnp.mean(centered * centered, axis=-1, keepdims=True) + norm_eps)
    return (centered * inverse, inverse)


def layer_back(normal, inverse, incoming):
    return inverse * (
        incoming
        - jnp.mean(incoming, axis=-1, keepdims=True)
        - normal * jnp.mean(incoming * normal, axis=-1, keepdims=True)
    )


def adam_update(master, moment, square, gradient, factor):
    clipped = gradient * factor
    moment_new = beta_one * moment + (1.0 - beta_one) * clipped
    square_new = beta_two * square + (1.0 - beta_two) * clipped * clipped
    moment_hat = moment_new / (1.0 - beta_one**OPT_STEP)
    square_hat = square_new / (1.0 - beta_two**OPT_STEP)
    master_new = master - learn_rate * (
        moment_hat / (jnp.sqrt(square_hat) + adam_eps) + decay_rate * master
    )
    return (master_new, moment_new, square_new)


def cube_order(count):
    order, step = [0], count // 2
    while step:
        order = order + [place ^ step for place in order]
        step //= 2
    return order


def swap(values, axis, step):
    count = lax.axis_size(axis)
    return lax.ppermute(values, axis, [(rank, rank ^ step) for rank in range(count)])


def cube_gather(values, axis):
    step = lax.axis_size(axis) // 2
    while step:
        values = jnp.concatenate([values, swap(values, axis, step)], axis=0)
        step //= 2
    return values


def cube_reduce(values, axis, wire):
    count, step = lax.axis_size(axis), 1
    while step < count:
        half = values.shape[0] // 2
        arrived = swap(values[half:].astype(wire), axis, step)
        values = values[:half] + arrived.astype(jnp.float32)
        step *= 2
    return values


def cube_total(values, axes):
    for axis in axes:
        step = 1
        while step < lax.axis_size(axis):
            values = values + swap(values, axis, step)
            step *= 2
    return values


def by_rank(blocks, axis):
    count = lax.axis_size(axis)
    order = cube_order(count)
    places = jnp.asarray([order.index(offset) for offset in range(count)], dtype=jnp.int32)
    return jnp.take(blocks, places[lax.axis_index(axis) ^ jnp.arange(count)], axis=0)


def by_offset(blocks, axis):
    order = jnp.asarray(cube_order(lax.axis_size(axis)), dtype=jnp.int32)
    return jnp.take(blocks, lax.axis_index(axis) ^ order, axis=0)


def trade(blocks, axis):
    order = cube_order(lax.axis_size(axis))
    return jnp.stack(
        [blocks[0]] + [swap(blocks[place], axis, order[place]) for place in range(1, len(order))]
    )


def head_places(index):
    count, rank = lax.axis_size("seq"), lax.axis_index("seq")
    inverse = pow(3, -1, count)
    owner = (inverse * (rank - index)) % count
    return (3 * owner + index) // count, [
        (place, (inverse * (place - index)) % count) for place in range(count)
    ]


def to_heads(block):
    rows, columns = block.shape
    count, rank = lax.axis_size("seq"), lax.axis_index("seq")
    parts = block.reshape(rows, 3, columns // 3)
    arrived = jnp.stack(
        [
            lax.ppermute(
                parts[:, index], "seq", [(place, (3 * place + index) % count) for place in range(count)]
            )
            for index in range(3)
        ]
    )
    chosen = [
        lax.dynamic_index_in_dim(arrived, (slot * count + rank) % 3, 0, keepdims=False)
        for slot in range(3)
    ]
    return jnp.concatenate(chosen, axis=1)


def from_heads(block):
    rows, columns = block.shape
    parts = block.reshape(rows, 3, columns // 3)
    arrived = []
    for index in range(3):
        slot, moves = head_places(index)
        sent = lax.dynamic_index_in_dim(parts, slot, 1, keepdims=False)
        arrived.append(lax.ppermute(sent, "seq", moves))
    return jnp.concatenate(arrived, axis=1)


def to_pairs(block):
    half = block.shape[1] // 2
    low = lax.axis_index("seq") < lax.axis_size("seq") // 2
    left, right = block[:, :half], block[:, half:]
    kept, sent = jnp.where(low, left, right), jnp.where(low, right, left)
    arrived = swap(sent, "seq", lax.axis_size("seq") // 2)
    return jnp.concatenate([jnp.where(low, kept, arrived), jnp.where(low, arrived, kept)], axis=1)


def from_pairs(block):
    half = block.shape[1] // 2
    low = lax.axis_index("seq") < lax.axis_size("seq") // 2
    gate, up = block[:, :half], block[:, half:]
    kept, sent = jnp.where(low, gate, up), jnp.where(low, up, gate)
    arrived = swap(sent, "seq", lax.axis_size("seq") // 2)
    return jnp.concatenate([jnp.where(low, kept, arrived), jnp.where(low, arrived, kept)], axis=1)


def pair_index(rank):
    half = lax.axis_size("seq") // 2
    return 2 * (rank % half) + rank // half


def mm(left, right):
    return jnp.dot(left, right, preferred_element_type=jnp.float32)


def mm_t(left, right):
    return lax.dot_general(left, right, (((1,), (1,)), ((), ())), preferred_element_type=jnp.float32)


def t_mm(left, right):
    return lax.dot_general(left, right, (((0,), (0,)), ((), ())), preferred_element_type=jnp.float32)


def on_device(
    tokens,
    cotangent,
    condition,
    item_lengths,
    item_widths,
    qkv_weight,
    qkv_first,
    qkv_second,
    out_weight,
    out_first,
    out_second,
    gateup_weight,
    gateup_first,
    gateup_second,
    down_weight,
    down_first,
    down_second,
    mod_weight,
    mod_first,
    mod_second,
    mod_bias,
    bias_first,
    bias_second,
    qk_gains,
    gains_first,
    gains_second,
):
    packs, length, width = tokens.shape
    items = condition.shape[1]
    head_size = width // HEADS
    rank, count = lax.axis_index("seq"), lax.axis_size("seq")
    row_rank, row_count = lax.axis_index("dp"), lax.axis_size("dp")
    total = length * count
    heads = HEADS // count
    slab = heads * head_size
    rows = qkv_weight.shape[0]
    order = cube_order(count)
    low = jnp.bfloat16

    qkv_w = lax.all_gather(to_heads(qkv_weight.astype(low)), "dp", axis=0, tiled=True)
    pair_w = lax.all_gather(to_pairs(gateup_weight.astype(low)), "dp", axis=0, tiled=True)
    out_cols = lax.all_gather(out_weight.astype(low), "dp", axis=0, tiled=True)
    down_cols = lax.all_gather(down_weight.astype(low), "dp", axis=0, tiled=True)
    out_w = jnp.moveaxis(
        by_rank(cube_gather(out_cols[None], "seq"), "seq"), 0, 1
    ).reshape(width, width)
    down_rows = down_cols.shape[0] // count
    down_parts = down_cols.reshape(count, down_rows, slab)
    pair_of = jnp.asarray([2 * (r % (count // 2)) + r // (count // 2) for r in range(count)])
    order_ranks = rank ^ jnp.asarray(order, dtype=jnp.int32)
    down_w = jnp.moveaxis(
        by_rank(trade(jnp.take(down_parts, pair_of[order_ranks], axis=0), "seq"), "seq"), 0, 1
    ).reshape(down_rows, width)
    gate_w, up_w = pair_w[:, :down_rows], pair_w[:, down_rows:]

    item_ids, row_pos, col_pos = jax.vmap(partial(pack_layout, span=total))(
        item_lengths, item_widths
    )

    def reorder(values):
        return jnp.take(values.reshape(packs, count, length), order_ranks, axis=1).reshape(
            packs, total
        )

    item_ids, row_pos, col_pos = reorder(item_ids), reorder(row_pos), reorder(col_pos)
    tables = rotary_tables(row_pos, col_pos, head_size // 4)
    back_tables = (tables[0], -tables[1], tables[2], -tables[3])

    cond_act = jax.nn.silu(condition.astype(jnp.float32)).astype(low).reshape(packs * items, width)
    cond_all = cube_gather(cond_act, "dp")
    cond_rows = lax.dynamic_slice_in_dim(cond_all, row_rank * rows, rows, 1)
    mod_part = cube_reduce(mm(cond_rows, mod_weight.astype(low)), "dp", jnp.float32)
    mod_part = (mod_part + mod_bias).astype(low)
    modulation = jnp.moveaxis(by_rank(cube_gather(mod_part[None], "seq"), "seq"), 0, 1)
    modulation = modulation.reshape(packs, items, 6, width).astype(jnp.float32)

    def pick(pack, which, ids):
        choice = modulation[pack, items - 1, which][None]
        for item in range(items - 2, -1, -1):
            choice = jnp.where((ids == item)[:, None], modulation[pack, item, which][None], choice)
        return choice

    saved, outputs = [], []
    for pack in range(packs):
        ids = item_ids[pack]
        own = ids[:length]
        table = tuple(entry[pack] for entry in tables)
        tok_all = cube_gather(tokens[pack], "seq").astype(jnp.float32)
        cot_all = cube_gather(cotangent[pack], "seq")
        normal_attn, inverse_attn = layer_stats(tok_all)
        normed = (normal_attn * (1.0 + pick(pack, 1, ids)) + pick(pack, 0, ids)).astype(low)
        projected = mm(normed, qkv_w).reshape(total, 3, heads, head_size)
        query_raw, key_raw = projected[:, 0], projected[:, 1]
        queries = (
            rotary(head_norm(query_raw, qk_gains[0]), table) * (1.0 / math.sqrt(head_size))
        ).astype(low)
        keys = rotary(head_norm(key_raw, qk_gains[1]), table).astype(low)
        values = projected[:, 2].astype(low)
        same = (ids[:, None] == ids[None, :])[None]
        scores = jnp.where(
            same,
            jnp.einsum("qhd,khd->hqk", queries, keys, preferred_element_type=jnp.float32),
            masked_score,
        )
        top_score = jnp.max(scores, axis=-1, keepdims=True)
        exp_scores = jnp.exp(scores - top_score)
        exp_total = jnp.sum(exp_scores, axis=-1, keepdims=True)
        attention = exp_scores / exp_total
        log_total = top_score + jnp.log(exp_total)
        mixed = jnp.einsum(
            "hqk,khd->qhd", attention.astype(low), values, preferred_element_type=jnp.float32
        ).astype(low)
        mixed = by_rank(trade(mixed.reshape(count, length, slab), "seq"), "seq")
        mixed = jnp.moveaxis(mixed, 0, 1).reshape(length, width)
        attended = mm(mixed, out_w)
        tok_own = tokens[pack].astype(jnp.float32)
        middle = tok_own + pick(pack, 2, own) * attended
        normal_ffn, inverse_ffn = layer_stats(middle)
        normed_ffn = (normal_ffn * (1.0 + pick(pack, 4, own)) + pick(pack, 3, own)).astype(low)
        normed_ffn = cube_gather(normed_ffn, "seq")
        gate, up = mm(normed_ffn, gate_w), mm(normed_ffn, up_w)
        hidden = (jax.nn.silu(gate) * up).astype(low)
        branch = cube_reduce(mm(hidden, down_w), "seq", low)
        layer_out = (middle + pick(pack, 5, own) * branch).astype(low)
        outputs.append(layer_out)
        saved.append(
            (
                ids, own, cot_all, normal_attn[:length], inverse_attn[:length], normed, query_raw,
                key_raw, queries, keys, values, same, log_total, mixed, attended, normal_ffn,
                inverse_ffn, normed_ffn, gate, up, hidden, branch,
            )
        )

    grads, token_grads, mod_grads = [], [], []
    for pack in range(packs):
        (
            ids, own, cot_all, normal_attn, inverse_attn, normed, query_raw,
            key_raw, queries, keys, values, same, log_total, mixed, attended, normal_ffn,
            inverse_ffn, normed_ffn, gate, up, hidden, branch,
        ) = saved[pack]
        back_table = tuple(entry[pack] for entry in back_tables)
        cot_own = cotangent[pack].astype(jnp.float32)
        grad_branch = (cot_all.astype(jnp.float32) * pick(pack, 5, ids)).astype(low)
        grad_gate_ffn = cot_own * branch
        grad_hidden = mm_t(grad_branch, down_w)
        grad_down = t_mm(hidden, grad_branch)
        sigmoid = jax.nn.sigmoid(gate)
        grad_gate = (grad_hidden * up * sigmoid * (1.0 + gate * (1.0 - sigmoid))).astype(low)
        grad_up = (grad_hidden * gate * sigmoid).astype(low)
        grad_normed_ffn = cube_reduce(mm_t(grad_gate, gate_w) + mm_t(grad_up, up_w), "seq", low)
        grad_pair = jnp.concatenate([t_mm(normed_ffn, grad_gate), t_mm(normed_ffn, grad_up)], axis=1)
        grad_scale_ffn = grad_normed_ffn * normal_ffn
        grad_middle = cot_own + layer_back(
            normal_ffn, inverse_ffn, grad_normed_ffn * (1.0 + pick(pack, 4, own))
        )
        grad_attended = (grad_middle * pick(pack, 2, own)).astype(low)
        grad_gate_attn = grad_middle * attended
        grad_out = t_mm(mixed, grad_attended)
        grad_mixed = mm_t(grad_attended, out_w).astype(low)
        grad_mixed = jnp.moveaxis(grad_mixed.reshape(length, count, slab), 1, 0)
        grad_mixed = trade(by_offset(grad_mixed, "seq"), "seq")
        grad_mixed = grad_mixed.reshape(total, heads, head_size)
        scores = jnp.where(
            same,
            jnp.einsum("qhd,khd->hqk", queries, keys, preferred_element_type=jnp.float32),
            masked_score,
        )
        attention = jnp.exp(scores - log_total)
        grad_attention = jnp.einsum(
            "qhd,khd->hqk", grad_mixed, values, preferred_element_type=jnp.float32
        )
        inner = jnp.sum(attention * grad_attention, axis=-1, keepdims=True)
        grad_scores = (attention * (grad_attention - inner)).astype(low)
        grad_queries = jnp.einsum(
            "hqk,khd->qhd", grad_scores, keys, preferred_element_type=jnp.float32
        )
        grad_keys = jnp.einsum(
            "hqk,qhd->khd", grad_scores, queries, preferred_element_type=jnp.float32
        )
        grad_values = jnp.einsum(
            "hqk,qhd->khd", attention.astype(low), grad_mixed, preferred_element_type=jnp.float32
        )
        grad_query_norm = rotary(grad_queries * (1.0 / math.sqrt(head_size)), back_table)
        grad_key_norm = rotary(grad_keys, back_table)
        grad_query_raw, gain_query = norm_back(query_raw[None], qk_gains[0], grad_query_norm[None])
        grad_key_raw, gain_key = norm_back(key_raw[None], qk_gains[1], grad_key_norm[None])
        grad_projected = jnp.stack([grad_query_raw[0], grad_key_raw[0], grad_values], axis=1)
        grad_projected = grad_projected.reshape(total, 3 * slab).astype(low)
        grad_normed = cube_reduce(mm_t(grad_projected, qkv_w), "seq", low)
        grad_qkv = t_mm(normed, grad_projected)
        grad_scale_attn = grad_normed * normal_attn
        token_grads.append(
            (
                grad_middle
                + layer_back(normal_attn, inverse_attn, grad_normed * (1.0 + pick(pack, 1, own)))
            ).astype(low)
        )
        chosen = (own[:, None] == jnp.arange(items, dtype=jnp.int32)).astype(jnp.float32)
        per_token = jnp.concatenate(
            [
                grad_normed, grad_scale_attn, grad_gate_attn,
                grad_normed_ffn, grad_scale_ffn, grad_gate_ffn,
            ],
            axis=1,
        )
        mod_grads.append(jnp.einsum("ti,tc->ic", chosen, per_token, precision=highest))
        grads.append((grad_qkv, grad_out, grad_pair, grad_down, jnp.stack([gain_query, gain_key])))
    grad_qkv, grad_out, grad_pair, grad_down, gain_part = [sum(parts) for parts in zip(*grads)]

    def split_rows(gradient):
        return lax.psum_scatter(
            gradient.astype(low), "dp", scatter_dimension=0, tiled=True
        ).astype(jnp.float32)

    down_parts = jnp.moveaxis(grad_down.astype(low).reshape(down_rows, count, slab), 1, 0)
    down_parts = trade(by_offset(down_parts, "seq"), "seq")
    back_of = jnp.asarray(
        [[2 * (r % (count // 2)) + r // (count // 2) for r in range(count)].index(place) for place in range(count)]
    )
    place_of = jnp.asarray([order.index(offset) for offset in range(count)])
    down_parts = jnp.take(down_parts, place_of[back_of ^ rank], axis=0)
    out_parts = by_offset(jnp.moveaxis(grad_out.reshape(width, count, slab), 1, 0), "seq")
    down_sum = split_rows(down_parts.reshape(count * down_rows, slab))
    pair_sum = split_rows(grad_pair)
    out_sum = split_rows(cube_reduce(out_parts, "seq", low)[0])
    qkv_sum = split_rows(grad_qkv)
    gateup_sum = from_pairs(pair_sum)
    qkv_sum = from_heads(qkv_sum)

    gain_total = cube_total(gain_part, ("seq", "dp"))
    mod_grads = jnp.concatenate(mod_grads, axis=0)
    mod_grads = by_offset(
        jnp.moveaxis(mod_grads.reshape(packs * items, count, -1), 1, 0), "seq"
    )
    mod_grads = cube_gather(cube_reduce(mod_grads, "seq", jnp.float32)[0], "dp")
    mod_sum = lax.dot_general(
        cond_rows.astype(jnp.float32), mod_grads, (((0,), (0,)), ((), ())), precision=highest
    )
    bias_local = jnp.sum(mod_grads, axis=0)

    local_square = (
        jnp.sum(qkv_sum * qkv_sum) + jnp.sum(out_sum * out_sum) + jnp.sum(gateup_sum * gateup_sum)
    )
    local_square = local_square + jnp.sum(down_sum * down_sum) + jnp.sum(mod_sum * mod_sum)
    local_square = local_square + jnp.sum(bias_local * bias_local) / row_count
    square_total = cube_total(local_square, ("seq", "dp")) + jnp.sum(gain_total * gain_total)
    grad_norm = jnp.sqrt(square_total)
    factor = clip_limit / jnp.maximum(grad_norm, clip_limit)
    results = [jnp.stack(outputs), jnp.stack(token_grads), grad_norm]
    results += adam_update(qkv_weight, qkv_first, qkv_second, qkv_sum, factor)
    results += adam_update(out_weight, out_first, out_second, out_sum, factor)
    results += adam_update(gateup_weight, gateup_first, gateup_second, gateup_sum, factor)
    results += adam_update(down_weight, down_first, down_second, down_sum, factor)
    results += adam_update(mod_weight, mod_first, mod_second, mod_sum, factor)
    results += adam_update(mod_bias, bias_first, bias_second, bias_local, factor)
    results += adam_update(qk_gains, gains_first, gains_second, gain_total, factor)
    return tuple(results)


def solution(mesh):
    return jax.shard_map(
        on_device,
        mesh=mesh,
        in_specs=(
            P("dp", "seq", None),
            P("dp", "seq", None),
            P("dp", None, None),
            P("dp", None),
            P("dp", None),
            P("dp", "seq"),
            P("dp", "seq"),
            P("dp", "seq"),
            P("dp", "seq"),
            P("dp", "seq"),
            P("dp", "seq"),
            P("dp", "seq"),
            P("dp", "seq"),
            P("dp", "seq"),
            P("dp", "seq"),
            P("dp", "seq"),
            P("dp", "seq"),
            P("dp", "seq"),
            P("dp", "seq"),
            P("dp", "seq"),
            P("seq"),
            P("seq"),
            P("seq"),
            P(),
            P(),
            P(),
        ),
        out_specs=(
            P("dp", "seq", None),
            P("dp", "seq", None),
            P(),
            P("dp", "seq"),
            P("dp", "seq"),
            P("dp", "seq"),
            P("dp", "seq"),
            P("dp", "seq"),
            P("dp", "seq"),
            P("dp", "seq"),
            P("dp", "seq"),
            P("dp", "seq"),
            P("dp", "seq"),
            P("dp", "seq"),
            P("dp", "seq"),
            P("dp", "seq"),
            P("dp", "seq"),
            P("dp", "seq"),
            P("seq"),
            P("seq"),
            P("seq"),
            P(),
            P(),
            P(),
        ),
        check_vma=False,
    )
```

```python
from functools import partial
import math

import jax
import jax.numpy as jnp
import numpy as np
from jax import lax
from jax.experimental import pallas as pl
from jax.experimental.pallas import tpu as pltpu
from jax.sharding import PartitionSpec as P

HEADS = 16
OPT_STEP = 10


norm_eps = 1e-06
clip_limit = 1.0
beta_one = 0.9
beta_two = 0.95
adam_eps = 1e-08
learn_rate = 0.06
decay_rate = 0.01


def adam_update(master, moment, square, gradient, factor):
    clipped = gradient * factor
    moment_new = beta_one * moment + (1.0 - beta_one) * clipped
    square_new = beta_two * square + (1.0 - beta_two) * clipped * clipped
    moment_hat = moment_new / (1.0 - beta_one**OPT_STEP)
    square_hat = square_new / (1.0 - beta_two**OPT_STEP)
    master_new = master - learn_rate * (
        moment_hat / (jnp.sqrt(square_hat) + adam_eps) + decay_rate * master
    )
    return (master_new, moment_new, square_new)


LANE = 128


def fit(total, wanted):
    size = min(total, wanted)
    while total % size:
        size -= 8
    return size


def spread_matrix(heads, size):
    row = lax.broadcasted_iota(jnp.int32, (heads * size, heads * LANE), 0)
    column = lax.broadcasted_iota(jnp.int32, (heads * size, heads * LANE), 1)
    hit = row < 0
    for head in range(heads):
        inside = (column >= head * LANE) & (column < head * LANE + size)
        hit = hit | (inside & (row - column == head * (size - LANE)))
    return jnp.where(hit, 1.0, 0.0).astype(jnp.bfloat16)


def cube_slot(offset, count):
    bits = count.bit_length() - 1
    return sum(((offset // 2**bit) % 2) * 2 ** (bits - 1 - bit) for bit in range(bits))


def chosen(ids, rows_ref, which, pack, items):
    first = items * pack
    choice = rows_ref[which, first + items - 1 : first + items]
    for item in range(items - 2, -1, -1):
        choice = jnp.where(ids == item, rows_ref[which, first + item : first + item + 1], choice)
    return choice


def dot(left, right):
    return jnp.dot(left, right, preferred_element_type=jnp.float32)


def dot_t(left, right):
    return lax.dot_general(left, right, (((1,), (1,)), ((), ())), preferred_element_type=jnp.float32)


def t_dot(left, right):
    return lax.dot_general(left, right, (((0,), (0,)), ((), ())), preferred_element_type=jnp.float32)


def normalized(values):
    centered = values - jnp.mean(values, axis=-1, keepdims=True)
    inverse = lax.rsqrt(jnp.mean(centered * centered, axis=-1, keepdims=True) + norm_eps)
    return centered * inverse, inverse


def normalized_back(normal, inverse, incoming):
    return inverse * (
        incoming
        - jnp.mean(incoming, axis=-1, keepdims=True)
        - normal * jnp.mean(incoming * normal, axis=-1, keepdims=True)
    )


def gain_row(gains_ref, part, size):
    return jnp.concatenate(
        [1.0 + gains_ref[part : part + 1], jnp.zeros((1, LANE - size), jnp.float32)], axis=1
    )


def flip(rank, step):
    return rank + step - 2 * step * ((rank // step) % 2)


def xor(rank, offset):
    step = 1
    while step <= offset:
        if offset & step:
            rank = flip(rank, step)
        step *= 2
    return rank


def cube_order(count):
    order, step = [0], count // 2
    while step:
        order = order + [place ^ step for place in order]
        step //= 2
    return order


def ring_place(rank, count):
    side = rank % 2
    return (rank // 2) * (1 - 2 * side) + (count - 1) * side


def ring_rank(place, count):
    place = (place + count) % count
    side = place // (count // 2)
    return 2 * place * (1 - side) + (2 * (count - 1 - place) + 1) * side


def send(source, target, send_sem, recv_sem, where):
    copy = pltpu.make_async_remote_copy(
        src_ref=source, dst_ref=target, send_sem=send_sem, recv_sem=recv_sem,
        device_id=where, device_id_type=pl.DeviceIdType.MESH,
    )
    copy.start()
    return copy


def greet(targets):
    barrier = pltpu.get_barrier_semaphore()
    for target in targets:
        pl.semaphore_signal(
            barrier, inc=1, device_id=target, device_id_type=pl.DeviceIdType.MESH
        )
    pl.semaphore_wait(barrier, len(targets))


def seq_peers(rank, count):
    return [{"seq": xor(rank, offset)} for offset in range(1, count)]


def far_peers(rank, count):
    return [{"dp": (rank + offset) % count} for offset in range(1, count)]


def ring_peers(rank, count):
    place = ring_place(rank, count)
    return [{"dp": ring_rank(place + 1, count)}, {"dp": ring_rank(place - 1, count)}]


def far_part(index, lead, way):
    if lead == 1:
        return (0, 1) if index % 2 == way else (0, 0)
    cut = (lead + 1) // 2
    return (cut, lead) if way else (0, cut)


class RingGather:
    def __init__(self, buffers, rank, count, send_sems, recv_sems, use=None):
        self.buffers, self.count, self.use = buffers, count, use
        self.place = ring_place(rank, count)
        self.send_sems, self.recv_sems = send_sems, recv_sems
        self.steps = count // 2
        self.sent, self.going = [], []
        self.step = 0

    def advance(self):
        for copy in self.going:
            copy.wait_recv()
        self.sent += self.going
        self.going = []
        step = self.step
        if step > self.steps:
            return
        self.step += 1
        if step < self.steps:
            self.launch(step)
        if self.use is not None:
            self.use(ring_rank(self.place - step, self.count))
            if 0 < step < self.steps:
                self.use(ring_rank(self.place + step, self.count))

    def launch(self, step):
        for way in range(2):
            sign = 1 - 2 * way
            block = ring_rank(self.place - sign * step, self.count)
            where = {"dp": ring_rank(self.place + sign, self.count)}
            for index, buffer in enumerate(self.buffers):
                low, high = 0, buffer.shape[0]
                if step == self.steps - 1:
                    low, high = far_part(index, high, way)
                    if low == high:
                        continue
                view = buffer.at[pl.ds(low, high - low), block]
                self.going.append(
                    send(
                        view, view, self.send_sems.at[way, step, index],
                        self.recv_sems.at[way, step, index], where,
                    )
                )

    def finish(self):
        while self.step <= self.steps:
            self.advance()
        for copy in self.sent:
            copy.wait_send()


class RingReduce:
    def __init__(self, sources, results, totals, landed, rank, count, send_sems, recv_sems):
        self.sources, self.results, self.totals, self.landed = sources, results, totals, landed
        self.count, self.steps = count, count // 2
        self.place = ring_place(rank, count)
        self.send_sems, self.recv_sems = send_sems, recv_sems
        self.sent, self.going = [], []
        self.step = 0

    def advance(self):
        for copy in self.going:
            copy.wait_recv()
        self.sent += self.going
        self.going = []
        step = self.step
        self.step += 1
        if step > self.steps:
            return
        if step == self.steps:
            for index, source in enumerate(self.sources):
                mine = ring_rank(self.place, self.count)
                for lead in range(source.shape[0]):
                    total = source[lead, mine].astype(jnp.float32)
                    for way in range(2):
                        total += self.landed[index][way, step - 1, lead].astype(jnp.float32)
                    self.results[index][lead] = total
            return
        for way in range(2):
            sign = 1 - 2 * way
            block = ring_rank(self.place + sign * (self.steps - step), self.count)
            where = {"dp": ring_rank(self.place + sign, self.count)}
            for index, source in enumerate(self.sources):
                size = source.shape[0]
                low, high = far_part(index, size, way)
                if step == 0:
                    if low == high:
                        continue
                    view = source.at[pl.ds(low, high - low), block]
                    target = self.landed[index].at[way, step, pl.ds(low, high - low)]
                else:
                    for lead in range(size):
                        total = source[lead, block]
                        if step > 1 or low <= lead < high:
                            total = (
                                total.astype(jnp.float32)
                                + self.landed[index][way, step - 1, lead].astype(jnp.float32)
                            ).astype(total.dtype)
                        self.totals[index][way, step - 1, lead] = total
                    view = self.totals[index].at[way, step - 1]
                    target = self.landed[index].at[way, step]
                self.going.append(
                    send(
                        view, target, self.send_sems.at[way, step, index],
                        self.recv_sems.at[way, step, index], where,
                    )
                )

    def finish(self):
        while self.step <= self.steps:
            self.advance()
        for copy in self.sent:
            copy.wait_send()


class CubeGather:
    def __init__(self, source, target, rank, count, send_sems, recv_sems):
        self.source, self.target, self.rank = source, target, rank
        self.length = source.shape[0]
        self.send_sems, self.recv_sems = send_sems, recv_sems
        self.steps = [count >> (level + 1) for level in range(count.bit_length() - 1)]
        self.copies = {}
        self.level = 0
        for level in range(len(self.steps)):
            self.launch(0, level)

    def launch(self, slot, level):
        landing = slot + 2**level
        view = self.source
        if slot:
            view = self.target.at[pl.ds(slot * self.length, self.length)]
        self.copies[slot, level] = send(
            view, self.target.at[pl.ds(landing * self.length, self.length)],
            self.send_sems.at[landing - 1], self.recv_sems.at[landing - 1],
            {"seq": flip(self.rank, self.steps[level])},
        )

    def advance(self):
        level = self.level
        if level >= len(self.steps):
            return
        self.level += 1
        for slot in range(2**level):
            self.copies[slot, level].wait_recv()
        for later in range(level + 1, len(self.steps)):
            for slot in range(2**level, 2 ** (level + 1)):
                self.launch(slot, later)

    def finish(self):
        while self.level < len(self.steps):
            self.advance()

    def settle(self):
        for copy in self.copies.values():
            copy.wait_send()


class CubeReduce:
    def __init__(self, parts, landed, total, rank, count, send_sems, recv_sems):
        self.parts, self.landed, self.total, self.rank = parts, landed, total, rank
        self.length = parts.shape[0] // count
        self.half = parts.shape[0] // 2
        self.send_sems, self.recv_sems = send_sems, recv_sems
        self.copies = []

    def near(self):
        view = self.parts.at[pl.ds(self.half, self.half)]
        self.copies.append(
            send(
                view, self.landed.at[pl.ds(0, self.half)], self.send_sems.at[0],
                self.recv_sems.at[0], {"seq": flip(self.rank, 1)},
            )
        )

    def across(self):
        self.copies[0].wait_recv()
        here = pl.ds(self.length, self.length)
        self.total[...] = (
            self.parts[here].astype(jnp.float32) + self.landed[here].astype(jnp.float32)
        ).astype(self.total.dtype)
        self.copies.append(
            send(
                self.total, self.landed.at[pl.ds(self.half, self.length)], self.send_sems.at[1],
                self.recv_sems.at[1], {"seq": flip(self.rank, 2)},
            )
        )

    def result(self):
        self.copies[1].wait_recv()
        own = pl.ds(0, self.length)
        return (
            self.parts[own].astype(jnp.float32)
            + self.landed[own].astype(jnp.float32)
            + self.landed[pl.ds(self.half, self.length)].astype(jnp.float32)
        )

    def settle(self):
        for copy in self.copies:
            copy.wait_send()


def token_layout(pack, slot_rank, length, lengths_ref, widths_ref):
    items = lengths_ref.shape[1]
    place = lax.broadcasted_iota(jnp.int32, (length, 1), 0) + slot_rank * length
    ids = jnp.zeros_like(place)
    start = jnp.zeros_like(place)
    width = jnp.zeros_like(place) + widths_ref[pack, 0]
    end = 0
    for item in range(1, items):
        end = end + lengths_ref[pack, item - 1]
        inside = place >= end
        ids = jnp.where(inside, item, ids)
        start = jnp.where(inside, end, start)
        width = jnp.where(inside, widths_ref[pack, item], width)
    offset = (place - start).astype(jnp.float32)
    width = width.astype(jnp.float32)
    row = jnp.floor((offset + 0.5) / width)
    return ids, row, offset - row * width


def frequencies(size):
    quarter = size // 4
    lane = np.arange(LANE)
    table = np.where(lane < size, 10000.0 ** (-(lane % quarter) / quarter), 0.0)
    return table.astype(np.float32)[None]


def open_kernel(
    heads, size, items,
    lengths_ref, widths_ref, tok_ref, cond_ref, qkv_ref, out_ref, pair_ref, down_ref, modw_ref,
    bias_ref, freq_ref,
    tok_all_ref, ids_ref, cos_ref, lead_ref, trail_ref, mod_ref, cond_all_ref, wide_ref,
    out_all_ref, pair_x_ref, down_own_ref,
    cond_own_ref, part_ref, sums_ref, mod_own_ref, mod_all_ref, head_src_ref, head_x_ref,
    ring_a_ref, ring_b_ref, pair_src_ref, down_src_ref, down_x_ref,
    tok_send, tok_recv, far_send, far_recv, near_send, near_recv, ring_send, ring_recv,
    head_send, head_recv,
):
    rank, count = lax.axis_index("seq"), lax.axis_size("seq")
    row_rank, row_count = lax.axis_index("dp"), lax.axis_size("dp")
    packs, length, width = tok_ref.shape
    rows = qkv_ref.shape[0]
    slab = heads * size
    low = jnp.bfloat16
    far, near = far_peers(row_rank, row_count), seq_peers(rank, count)
    greet(far + near)

    cond = cond_ref[...].astype(jnp.float32)
    act = (cond / (1.0 + jnp.exp(-cond))).astype(low).astype(jnp.float32)
    for index in range(row_count):
        cond_own_ref[index] = act[:, index * rows : (index + 1) * rows]
    conds = []
    for offset, peer in enumerate(far):
        conds.append(
            send(
                cond_own_ref.at[peer["dp"]], cond_all_ref.at[row_rank],
                far_send.at[0, offset], far_recv.at[0, offset], peer,
            )
        )
    cond_all_ref[row_rank] = cond_own_ref[row_rank]

    def head_copy(index, slot, peer):
        return pltpu.make_async_remote_copy(
            src_ref=head_src_ref.at[index], dst_ref=head_x_ref.at[slot],
            send_sem=head_send.at[index], recv_sem=head_recv.at[slot],
            device_id={"seq": peer}, device_id_type=pl.DeviceIdType.MESH,
        )

    for index in range(3):
        head_src_ref[index] = qkv_ref[:, index * slab : (index + 1) * slab].astype(low)
    moves = []
    for index in range(3):
        peer, slot = (3 * rank + index) % count, (3 * rank + index) // count
        owner = (pow(3, -1, count) * (rank - index + 3 * count)) % count
        moves.append((peer, slot, owner, (3 * owner + index) // count))

        @pl.when(peer != rank)
        def _():
            head_copy(index, slot, peer).start()

        @pl.when(peer == rank)
        def _():
            head_x_ref[slot] = head_src_ref[index]

    toks = [
        CubeGather(
            tok_ref.at[pack], tok_all_ref.at[pack], rank, count, tok_send.at[pack],
            tok_recv.at[pack],
        )
        for pack in range(packs)
    ]
    for pack in range(packs):
        tok_all_ref[pack, :length] = tok_ref[pack]
    hidden_rows = down_ref.shape[0] // count
    groups = pair_ref.shape[1] // (count * hidden_rows)
    for target in range(count):
        pieces = []
        for group in range(groups):
            start = (group * count + target) * hidden_rows
            pieces.append(pair_ref[:, start : start + hidden_rows])
        pair_src_ref[target] = jnp.concatenate(pieces, axis=1).astype(low)
        down_src_ref[target] = down_ref[
            target * hidden_rows : (target + 1) * hidden_rows
        ].astype(low)
    weights = []
    for offset, peer in enumerate(near):
        weights.append(
            send(
                pair_src_ref.at[peer["seq"]], pair_x_ref.at[rank], near_send.at[0, offset],
                near_recv.at[0, offset], peer,
            )
        )
        weights.append(
            send(
                down_src_ref.at[peer["seq"]], down_x_ref.at[rank], near_send.at[1, offset],
                near_recv.at[1, offset], peer,
            )
        )
    pair_x_ref[rank] = pair_src_ref[rank]
    down_x_ref[rank] = down_src_ref[rank]

    for index, (peer, slot, owner, landed) in enumerate(moves):
        @pl.when(peer != rank)
        def _():
            head_copy(index, slot, peer).wait_send()

        @pl.when(owner != rank)
        def _():
            head_copy(index, landed, owner).wait_recv()

    cut = ring_a_ref.shape[3]
    block = jnp.concatenate([head_x_ref[0], head_x_ref[1], head_x_ref[2], out_ref[...].astype(low)], axis=1)
    ring_a_ref[0, row_rank] = block[:, :cut]
    ring_b_ref[0, row_rank] = block[:, cut:]
    spread = spread_matrix(heads, size)

    def use(index):
        whole_block = jnp.concatenate([ring_a_ref[0, index], ring_b_ref[0, index]], axis=1)
        for part in range(3):
            wide_ref[index, :, part * heads * LANE : (part + 1) * heads * LANE] = jnp.dot(
                whole_block[:, part * slab : (part + 1) * slab], spread,
                preferred_element_type=jnp.float32,
            ).astype(low)
        out_all_ref[index] = whole_block[:, 3 * slab :]

    ring = RingGather([ring_a_ref, ring_b_ref], row_rank, row_count, ring_send, ring_recv, use)
    ring.advance()
    modw = modw_ref[...].astype(low)
    for copy in conds:
        copy.wait_recv()
    lines = cond_all_ref.shape[1]
    conditions = cond_all_ref[...].reshape(row_count * lines, rows).astype(low)
    products = jnp.dot(conditions, modw, preferred_element_type=jnp.float32)
    part_ref[...] = products.reshape(part_ref.shape)
    parts = []
    for offset, peer in enumerate(far):
        parts.append(
            send(
                part_ref.at[peer["dp"]], sums_ref.at[row_rank], far_send.at[1, offset],
                far_recv.at[1, offset], peer,
            )
        )
    sums_ref[row_rank] = part_ref[row_rank]

    order = cube_order(count)
    lane = lax.broadcasted_iota(jnp.int32, (length, LANE), 1)
    quarter = size // 4
    leading = (lane < quarter) | ((lane >= 2 * quarter) & (lane < 3 * quarter))

    def tables(pack):
        for slot in range(count):
            here = slice(slot * length, (slot + 1) * length)
            ids, row, col = token_layout(
                pack, xor(rank, order[slot]), length, lengths_ref, widths_ref
            )
            ids_ref[pack, here] = ids
            angle = jnp.where(lane < 2 * quarter, row, col) * freq_ref[...]
            sine = jnp.where(lane < size, jnp.sin(angle), 0.0)
            cos_ref[pack, here] = jnp.where(lane < size, jnp.cos(angle), 0.0)
            lead_ref[pack, here] = jnp.where(leading, -sine, 0.0)
            trail_ref[pack, here] = jnp.where(leading, 0.0, sine)

    tables(0)
    ring.advance()
    for copy in parts:
        copy.wait_recv()
    total = bias_ref[...] + sums_ref[0]
    for index in range(1, row_count):
        total += sums_ref[index]
    mod_own_ref[...] = total.astype(low).astype(jnp.float32)
    mods = []
    for offset, peer in enumerate(near):
        mods.append(
            send(
                mod_own_ref, mod_all_ref.at[rank], near_send.at[2, offset],
                near_recv.at[2, offset], peer,
            )
        )
    mod_all_ref[rank] = mod_own_ref[...]
    for gather in toks:
        gather.advance()
    for pack in range(1, packs):
        tables(pack)
    ring.advance()
    for copy in mods:
        copy.wait_recv()
    everything = jnp.concatenate([mod_all_ref[index] for index in range(count)], axis=1)
    for which in range(6):
        mod_ref[which] = everything[:, which * width : (which + 1) * width]
    for copy in weights:
        copy.wait_recv()
    down_own_ref[...] = jnp.concatenate([down_x_ref[index] for index in range(count)], axis=1)
    ring.finish()
    for gather in toks:
        gather.finish()
    for gather in toks:
        gather.settle()
    for copy in conds + parts + weights + mods:
        copy.wait_send()


def opening(lengths, widths, tok, cond, qkv, out, pair, down, modw, bias, heads, size):
    packs, length, width = tok.shape
    items = lengths.shape[1]
    lines = cond.shape[0]
    count, row_count = lax.axis_size("seq"), lax.axis_size("dp")
    total = count * length
    low, full = jnp.bfloat16, jnp.float32
    rows, slab = out.shape
    columns = modw.shape[1]
    hidden_rows = down.shape[0] // count
    chunk = pair.shape[1] // count
    block = 4 * slab
    cut = -(-block // (2 * LANE)) * LANE
    table = jax.ShapeDtypeStruct((packs, total, LANE), full)
    shapes = [
        jax.ShapeDtypeStruct((packs, total, width), low),
        jax.ShapeDtypeStruct((packs, total, 1), jnp.int32),
        table, table, table,
        jax.ShapeDtypeStruct((6, lines, width), full),
        jax.ShapeDtypeStruct((row_count, lines, rows), full),
        jax.ShapeDtypeStruct((row_count, rows, 3 * heads * LANE), low),
        jax.ShapeDtypeStruct((row_count, rows, slab), low),
        jax.ShapeDtypeStruct((count, rows, chunk), low),
        jax.ShapeDtypeStruct((hidden_rows, count * slab), low),
    ]
    inside = pl.BlockSpec(memory_space=pltpu.VMEM)
    scalars = pl.BlockSpec(memory_space=pltpu.SMEM)
    dma = pltpu.SemaphoreType.DMA
    return pl.pallas_call(
        partial(open_kernel, heads, size, items),
        out_shape=shapes,
        in_specs=[scalars] * 2 + [inside] * 9,
        out_specs=[inside] * len(shapes),
        scratch_shapes=[
            pltpu.VMEM((row_count, lines, rows), full),
            pltpu.VMEM((row_count, lines, columns), full),
            pltpu.VMEM((row_count, lines, columns), full),
            pltpu.VMEM((lines, columns), full),
            pltpu.VMEM((count, lines, columns), full),
            pltpu.VMEM((3, rows, slab), low),
            pltpu.VMEM((3, rows, slab), low),
            pltpu.VMEM((1, row_count, rows, cut), low),
            pltpu.VMEM((1, row_count, rows, block - cut), low),
            pltpu.VMEM((count, rows, chunk), low),
            pltpu.VMEM((count, hidden_rows, slab), low),
            pltpu.VMEM((count, hidden_rows, slab), low),
            dma((packs, count - 1)), dma((packs, count - 1)),
            dma((2, row_count - 1)), dma((2, row_count - 1)),
            dma((3, count - 1)), dma((3, count - 1)),
            dma((2, row_count // 2, 2)), dma((2, row_count // 2, 2)),
            dma((3,)), dma((3,)),
        ],
        compiler_params=pltpu.CompilerParams(
            collective_id=0, has_side_effects=True, vmem_limit_bytes=48 * 1024 * 1024
        ),
        name="opening",
    )(lengths, widths, tok, cond, qkv, out, pair, down, modw, bias, frequencies(size))


def attend_pack(
    heads, size, items, pack, hook, tok_ref, ids_ref, rows_ref, cos_ref, lead_ref, trail_ref,
    gains_ref, wide_ref, normed_ref, raw_ref, query_ref, key_ref, value_ref, inverse_ref, mixed_ref,
    value_t_ref, out_ref,
):
    total, width = tok_ref.shape
    span = heads * LANE
    tile = fit(total, 192)
    lane = lax.broadcasted_iota(jnp.int32, (tile, LANE), 1)

    def project(index, carry):
        start = pl.multiple_of(index * tile, tile)
        here = pl.ds(start, tile)
        ids = ids_ref[here]
        normal, _ = normalized(tok_ref[here].astype(jnp.float32))
        normed = (
            normal * (1.0 + chosen(ids, rows_ref, 1, pack, items))
            + chosen(ids, rows_ref, 0, pack, items)
        ).astype(jnp.bfloat16)
        normed_ref[here] = normed
        cos, lead, trail = cos_ref[here], lead_ref[here], trail_ref[here]
        query_mark = jnp.where((lane >= size) & (lane < size + 8) & (lane - size != ids), -200.0, 0.0)
        key_mark = jnp.where(lane - size == ids, 1.0, 0.0)
        for part in range(3):
            projected = dot(normed, wide_ref[:, part * span : (part + 1) * span])
            for head in range(heads):
                raw = projected[:, head * LANE : (head + 1) * LANE]
                slot = slice(head * LANE, (head + 1) * LANE)
                if part == 2:
                    value_ref[here, slot] = raw.astype(jnp.bfloat16)
                    continue
                raw_ref[here, part * span + head * LANE : part * span + (head + 1) * LANE] = raw
                square = jnp.sum(raw * raw, axis=-1, keepdims=True) * (1.0 / size)
                unit = raw * lax.rsqrt(square + norm_eps) * gain_row(gains_ref, part, size)
                turned = (
                    unit * cos
                    + pltpu.roll(unit, LANE - size // 4, 1) * lead
                    + pltpu.roll(unit, size // 4, 1) * trail
                )
                if part == 0:
                    turned = turned * (1.0 / math.sqrt(size))
                    query_ref[here, slot] = (turned + query_mark).astype(jnp.bfloat16)
                else:
                    key_ref[here, slot] = (turned + key_mark).astype(jnp.bfloat16)
        return carry

    lax.fori_loop(0, total // tile, project, 0)
    hook()
    block = fit(total, 256)
    value_lane = lax.broadcasted_iota(jnp.int32, (total, LANE), 1)
    for head in range(heads):
        slot = slice(head * LANE, (head + 1) * LANE)
        marked = jnp.where(value_lane == size, 1.0, value_ref[:, slot].astype(jnp.float32))
        value_t_ref[...] = marked.T.astype(jnp.bfloat16)

        def score(index, carry):
            here = pl.ds(pl.multiple_of(index * block, block), block)
            weights = jnp.exp(dot_t(key_ref[:, slot], query_ref[here, slot])).astype(jnp.bfloat16)
            mixed = dot(value_t_ref[...], weights)
            inverse = 1.0 / mixed[size : size + 1]
            inverse_ref[head : head + 1, here] = inverse
            out_ref[here, slot] = (mixed * inverse).T.astype(jnp.bfloat16)
            return carry

        lax.fori_loop(0, total // block, score, 0)
        hook()
    spread = spread_matrix(heads, size)

    def narrow(index, carry):
        here = pl.ds(pl.multiple_of(index * tile, tile), tile)
        mixed_ref[here] = dot_t(out_ref[here], spread).astype(jnp.bfloat16)
        return carry

    lax.fori_loop(0, total // tile, narrow, 0)


def attend_kernel(
    heads, size, items, tok_ref, ids_ref, rows_ref, cos_ref, lead_ref, trail_ref, gains_ref,
    wide_ref, out_ref, pair_ref, cot_ref,
    normed_ref, raw_ref, query_ref, key_ref, value_ref, inverse_ref,
    mixed_ref, out_full_ref, pair_all_ref, cot_all_ref,
    value_t_ref, wide_out_ref, own_mixed_ref, out_slots_ref,
    ring_send, ring_recv, mixed_send, mixed_recv, out_send, out_recv, cot_send, cot_recv,
):
    rank, count = lax.axis_index("seq"), lax.axis_size("seq")
    row_rank, row_count = lax.axis_index("dp"), lax.axis_size("dp")
    packs, total, width = tok_ref.shape
    length = total // count
    order = cube_order(count)
    greet(ring_peers(row_rank, row_count) + seq_peers(rank, count))
    for lead in range(pair_ref.shape[0]):
        pair_all_ref[lead, row_rank] = pair_ref[lead]
    ring = RingGather([pair_all_ref], row_rank, row_count, ring_send, ring_recv)
    ring.advance()
    outs = CubeGather(out_ref, out_slots_ref, rank, count, out_send, out_recv)
    cots = [
        CubeGather(
            cot_ref.at[pack], cot_all_ref.at[pack], rank, count, cot_send.at[pack],
            cot_recv.at[pack],
        )
        for pack in range(packs)
    ]
    out_slots_ref[:row_count] = out_ref[...]
    for pack in range(packs):
        cot_all_ref[pack, :length] = cot_ref[pack]
    marks = [0]
    stride = max(1, (packs * (heads + 1) - 1) // (row_count // 2))

    def hook():
        marks[0] += 1
        if marks[0] % stride == 0 and ring.going:
            ring.advance()
        if marks[0] == (packs * (heads + 1)) * 2 // 3:
            for gather in [outs] + cots:
                gather.advance()

    sends = []
    for pack in range(packs):
        attend_pack(
            heads, size, items, pack, hook, tok_ref.at[pack], ids_ref.at[pack], rows_ref,
            cos_ref.at[pack], lead_ref.at[pack], trail_ref.at[pack], gains_ref, wide_ref,
            normed_ref.at[pack], raw_ref.at[pack], query_ref.at[pack], key_ref.at[pack],
            value_ref.at[pack], inverse_ref.at[pack], own_mixed_ref.at[pack],
            value_t_ref, wide_out_ref,
        )
        for slot in range(1, count):
            sends.append(
                send(
                    own_mixed_ref.at[pack, pl.ds(slot * length, length)],
                    mixed_ref.at[pack, rank], mixed_send.at[pack, slot - 1],
                    mixed_recv.at[pack, slot - 1], {"seq": xor(rank, order[slot])},
                )
            )
        mixed_ref[pack, rank] = own_mixed_ref[pack, :length]
    outs.finish()
    for index in range(row_count):
        out_full_ref[index] = jnp.concatenate(
            [
                out_slots_ref[cube_slot(xor(rank, owner), count) * row_count + index]
                for owner in range(count)
            ],
            axis=1,
        )
    ring.finish()
    for gather in cots:
        gather.finish()
    for copy in sends:
        copy.wait_recv()
    for gather in [outs] + cots:
        gather.settle()
    for copy in sends:
        copy.wait_send()


def attend(tok, ids, rows, turns, gains, wide, out, pair, cot, items, heads, size):
    packs, total, width = tok.shape
    count, row_count = lax.axis_size("seq"), lax.axis_size("dp")
    span, slab = heads * LANE, heads * size
    length = total // count
    low = jnp.bfloat16
    shapes = [
        jax.ShapeDtypeStruct((packs, total, width), low),
        jax.ShapeDtypeStruct((packs, total, 2 * span), jnp.float32),
        jax.ShapeDtypeStruct((packs, total, span), low),
        jax.ShapeDtypeStruct((packs, total, span), low),
        jax.ShapeDtypeStruct((packs, total, span), low),
        jax.ShapeDtypeStruct((packs, heads, total), jnp.float32),
        jax.ShapeDtypeStruct((packs, count, length, slab), low),
        jax.ShapeDtypeStruct(out.shape[:2] + (count * slab,), low),
        jax.ShapeDtypeStruct((pair.shape[0], row_count) + pair.shape[1:], low),
        jax.ShapeDtypeStruct((packs, total, width), low),
    ]
    inside = pl.BlockSpec(memory_space=pltpu.VMEM)
    dma = pltpu.SemaphoreType.DMA
    return pl.pallas_call(
        partial(attend_kernel, heads, size, items),
        out_shape=shapes,
        in_specs=[inside] * 11,
        out_specs=[inside] * 10,
        scratch_shapes=[
            pltpu.VMEM((LANE, total), low), pltpu.VMEM((total, span), low),
            pltpu.VMEM((packs, total, slab), low),
            pltpu.VMEM((count * row_count,) + out.shape[1:], low),
            dma((2, row_count // 2, 1)), dma((2, row_count // 2, 1)),
            dma((packs, count - 1)), dma((packs, count - 1)),
            dma((count - 1,)), dma((count - 1,)),
            dma((packs, count - 1)), dma((packs, count - 1)),
        ],
        compiler_params=pltpu.CompilerParams(
            collective_id=1, has_side_effects=True, vmem_limit_bytes=60 * 1024 * 1024
        ),
        name="attend",
    )(tok, ids, rows, *turns, gains, wide, out, pair, cot)


def middle_kernel(
    items, mixed_ref, tok_ref, ids_ref, rows_ref, cot_ref, out_ref, pair_ref, down_ref,
    layer_ref, grad_mixed_ref, grad_middle_ref, part_ref, pair_grad_ref, down_grad_ref, out_grad_ref,
    down_a_ref, down_b_ref, own_ref, attended_ref, middle_ref, normed_ref, hidden_ref, gated_ref,
    branch_in_ref, partial_ref, landed_ref, total_ref, branch_ref, branch_landed_ref,
    branch_total_ref, gmix_ref, coming_ref,
    ring_send, ring_recv, norm_send, norm_recv, grad_send, grad_recv, branch_send, branch_recv,
    mix_send, mix_recv,
):
    rank, count = lax.axis_index("seq"), lax.axis_size("seq")
    row_rank, row_count = lax.axis_index("dp"), lax.axis_size("dp")
    packs, total, width = cot_ref.shape
    length = total // count
    slab = width // count
    chunk = pair_ref.shape[2]
    half = count // 2
    cut = down_a_ref.shape[3]
    hidden = row_count * down_ref.shape[0]
    order = cube_order(count)
    low, full = jnp.bfloat16, jnp.float32
    greet(ring_peers(row_rank, row_count) + seq_peers(rank, count))
    down_a_ref[0, row_rank] = down_ref[:, :cut]
    down_b_ref[0, row_rank] = down_ref[:, cut:]
    ring = RingGather([down_a_ref, down_b_ref], row_rank, row_count, ring_send, ring_recv)
    ring.advance()
    part_ref[...] = jnp.zeros_like(part_ref)

    def own_ids(pack):
        return ids_ref[pack, :length]

    def pick(pack, which):
        return chosen(own_ids(pack), rows_ref, which, pack, items)

    def by_item(pack, which, values):
        for item in range(items):
            line = items * pack + item
            part_ref[which - 2, line : line + 1] = jnp.sum(
                jnp.where(own_ids(pack) == item, values, 0.0), axis=0, keepdims=True
            )

    gathers = []
    for pack in range(packs):
        own = jnp.concatenate([mixed_ref[pack, index] for index in range(count)], axis=1)
        own_ref[pack] = own
        attended = dot(own, out_ref[...])
        attended_ref[pack] = attended.astype(low)
        middle = tok_ref[pack].astype(full) + pick(pack, 2) * attended
        middle_ref[pack] = middle
        normal, _ = normalized(middle)
        coming_ref[pack] = (normal * (1.0 + pick(pack, 4)) + pick(pack, 3)).astype(low)
        normed_ref[pack, :length] = coming_ref[pack]
        gathers.append(
            CubeGather(
                coming_ref.at[pack], normed_ref.at[pack], rank, count, norm_send.at[pack],
                norm_recv.at[pack],
            )
        )
        ring.advance()
    tile = fit(total, 2 * length)

    def scale_cotangent(pack):
        def step(index, carry):
            here = pl.ds(pl.multiple_of(index * length, length), length)
            gate = chosen(ids_ref[pack, here], rows_ref, 5, pack, items)
            branch_in_ref[pack, here] = (cot_ref[pack, here].astype(full) * gate).astype(low)
            return carry

        lax.fori_loop(0, count, step, 0)

    for pack in range(packs):
        scale_cotangent(pack)
        ring.advance()
    ring.finish()

    def down_part(which):
        ref = (down_a_ref, down_b_ref)[which]
        return ref[0].reshape(hidden, ref.shape[3])

    def feed(pack, start):
        here = pl.ds(start, tile)
        normed, coming = normed_ref[pack, here], branch_in_ref[pack, here]
        grad_hidden = dot_t(coming[:, :cut], down_part(0)) + dot_t(coming[:, cut:], down_part(1))
        back = None
        for index in range(half):
            columns = slice(index * chunk, (index + 1) * chunk)
            gate, up = dot(normed, pair_ref[index]), dot(normed, pair_ref[index + half])
            grad = grad_hidden[:, columns]
            sigmoid = 1.0 / (1.0 + jnp.exp(-gate))
            silu = gate * sigmoid
            hidden_ref[pack, here, columns] = (silu * up).astype(low)
            grad_gate = (grad * up * sigmoid * (1.0 + gate * (1.0 - sigmoid))).astype(low)
            grad_up = (grad * silu).astype(low)
            gated_ref[pack, here, columns] = grad_gate
            gated_ref[pack, here, (index + half) * chunk : (index + half + 1) * chunk] = grad_up
            term = dot_t(grad_gate, pair_ref[index]) + dot_t(grad_up, pair_ref[index + half])
            back = term if back is None else back + term
        partial_ref[pack, here] = back.astype(low)

    reduces, branches = [], []
    for pack in range(packs):
        gathers[pack].finish()
        reduces.append(
            CubeReduce(
                partial_ref.at[pack], landed_ref.at[pack], total_ref.at[pack], rank, count,
                grad_send.at[pack], grad_recv.at[pack],
            )
        )
        feed(pack, total // 2)
        reduces[pack].near()
        feed(pack, 0)
        reduces[pack].across()

    def branch_part(pack, start):
        here = pl.ds(start, tile)
        values = hidden_ref[pack, here]
        branch_ref[here, :cut] = dot(values, down_part(0)).astype(low)
        branch_ref[here, cut:] = dot(values, down_part(1)).astype(low)

    def middle_back(pack):
        normal, inverse = normalized(middle_ref[pack])
        grad_normed = reduces[pack].result()
        grad_middle = cot_ref[pack, :length].astype(full) + normalized_back(
            normal, inverse, grad_normed * (1.0 + pick(pack, 4))
        )
        grad_middle_ref[pack] = grad_middle
        by_item(pack, 2, grad_middle * attended_ref[pack].astype(full))
        by_item(pack, 3, grad_normed)
        by_item(pack, 4, grad_normed * normal)
        grad_attended = (grad_middle * pick(pack, 2)).astype(low)
        coming_ref[pack] = grad_attended
        grad_mixed = dot_t(grad_attended, out_ref[...]).astype(low)
        for index in range(count):
            gmix_ref[index] = grad_mixed[:, index * slab : (index + 1) * slab]
        copies = []
        for slot in range(1, count):
            peer = xor(rank, order[slot])
            copies.append(
                send(
                    gmix_ref.at[peer],
                    grad_mixed_ref.at[pack, pl.ds(slot * length, length)],
                    mix_send.at[pack, slot - 1], mix_recv.at[pack, slot - 1], {"seq": peer},
                )
            )
        grad_mixed_ref[pack, :length] = gmix_ref[rank]
        return copies

    def branch_start(pack):
        branches.append(
            CubeReduce(
                branch_ref, branch_landed_ref.at[pack], branch_total_ref.at[pack], rank, count,
                branch_send.at[pack], branch_recv.at[pack],
            )
        )
        branch_part(pack, total // 2)
        branches[pack].near()
        branch_part(pack, 0)

    def branch_finish(pack):
        branch = branches[pack].result()
        layer_ref[pack] = (middle_ref[pack] + pick(pack, 5) * branch).astype(low)
        by_item(pack, 5, cot_ref[pack, :length].astype(full) * branch)
        branches[pack].settle()

    mixes = []
    branch_start(0)
    for pack in range(packs):
        gathers[pack].settle()
    mixes += middle_back(0)
    branches[0].across()
    strip = fit(width, 384)
    for start in range(0, width, strip):
        left = [normed_ref[pack, :, start : start + strip].T for pack in range(packs)]
        for index in range(count):
            columns = slice(index * chunk, (index + 1) * chunk)
            pair_grad_ref[index, start : start + strip] = sum(
                dot(left[pack], gated_ref[pack, :, columns]) for pack in range(packs)
            ).astype(low)
    for pack in range(1, packs):
        branch_finish(pack - 1)
        branch_start(pack)
        for copy in mixes[-(count - 1) :]:
            copy.wait_send()
        mixes += middle_back(pack)
        branches[pack].across()
    for start in range(0, hidden, chunk):
        left = [hidden_ref[pack, :, start : start + chunk].T for pack in range(packs)]
        for column in range(0, width, strip):
            down_grad_ref[start : start + chunk, column : column + strip] = sum(
                dot(left[pack], branch_in_ref[pack, :, column : column + strip])
                for pack in range(packs)
            ).astype(low)
    branch_finish(packs - 1)
    for start in range(0, width, strip):
        left = [own_ref[pack, :, start : start + strip].T for pack in range(packs)]
        grad = sum(dot(left[pack], coming_ref[pack]) for pack in range(packs)).astype(low)
        for index in range(count):
            out_grad_ref[index, start : start + strip] = grad[:, index * slab : (index + 1) * slab]
    for copy in mixes:
        copy.wait_recv()
    for group in reduces:
        group.settle()
    for copy in mixes[-(count - 1) :]:
        copy.wait_send()


def middle(mixed, tok, ids, rows, cot, out, pair, down, items):
    packs, total, width = cot.shape
    count, row_count = lax.axis_size("seq"), lax.axis_size("dp")
    length, slab = total // count, width // count
    hidden_rows = down.shape[0]
    hidden = row_count * hidden_rows
    low, full = jnp.bfloat16, jnp.float32
    lines = rows.shape[1]
    cut = -(-width // (2 * LANE)) * LANE
    half = total // 2
    shapes = [
        jax.ShapeDtypeStruct((packs, length, width), low),
        jax.ShapeDtypeStruct((packs, total, slab), low),
        jax.ShapeDtypeStruct((packs, length, width), full),
        jax.ShapeDtypeStruct((4, lines, width), full),
        jax.ShapeDtypeStruct(pair.shape, low),
        jax.ShapeDtypeStruct((hidden, width), low),
        jax.ShapeDtypeStruct((count, width, slab), low),
    ]
    inside = pl.BlockSpec(memory_space=pltpu.VMEM)
    dma = pltpu.SemaphoreType.DMA
    return pl.pallas_call(
        partial(middle_kernel, items),
        out_shape=shapes,
        in_specs=[inside] * 8,
        out_specs=[inside] * len(shapes),
        scratch_shapes=[
            pltpu.VMEM((1, row_count, hidden_rows, cut), low),
            pltpu.VMEM((1, row_count, hidden_rows, width - cut), low),
            pltpu.VMEM((packs, length, width), low),
            pltpu.VMEM((packs, length, width), low),
            pltpu.VMEM((packs, length, width), full),
            pltpu.VMEM((packs, total, width), low),
            pltpu.VMEM((packs, total, hidden), low),
            pltpu.VMEM((packs, total, 2 * hidden), low),
            pltpu.VMEM((packs, total, width), low),
            pltpu.VMEM((packs, total, width), low),
            pltpu.VMEM((packs, half + length, width), low),
            pltpu.VMEM((packs, length, width), low),
            pltpu.VMEM((total, width), low),
            pltpu.VMEM((packs, half + length, width), low),
            pltpu.VMEM((packs, length, width), low),
            pltpu.VMEM((count, length, slab), low),
            pltpu.VMEM((packs, length, width), low),
            dma((2, row_count // 2, 2)), dma((2, row_count // 2, 2)),
            dma((packs, count - 1)), dma((packs, count - 1)),
            dma((packs, 2)), dma((packs, 2)), dma((packs, 2)), dma((packs, 2)),
            dma((packs, count - 1)), dma((packs, count - 1)),
        ],
        compiler_params=pltpu.CompilerParams(
            collective_id=2, has_side_effects=True, vmem_limit_bytes=62 * 1024 * 1024
        ),
        name="middle",
    )(mixed, tok, ids, rows, cot, out, pair, down)


def attend_back_pack(
    heads, size, hook, mixed_ref, raw_ref, query_ref, key_ref, value_ref, inverse_ref,
    cos_ref, lead_ref, trail_ref, gains_ref, wide_ref,
    grad_ref, normed_ref, gain_ref,
    wide_mixed_ref, key_t_ref, dq_ref, dk_ref, dv_ref,
):
    total = mixed_ref.shape[0]
    span = heads * LANE
    tile = fit(total, 128)
    block = fit(total, 256)
    spread = spread_matrix(heads, size)

    def widen(index, carry):
        here = pl.ds(pl.multiple_of(index * tile, tile), tile)
        wide_mixed_ref[here] = jnp.dot(
            mixed_ref[here], spread, preferred_element_type=jnp.float32
        ).astype(jnp.bfloat16)
        return carry

    lax.fori_loop(0, total // tile, widen, 0)
    for head in range(heads):
        slot = slice(head * LANE, (head + 1) * LANE)
        key_t_ref[...] = key_ref[:, slot].astype(jnp.float32).T.astype(jnp.bfloat16)
        dk_ref[...] = jnp.zeros_like(dk_ref)
        dv_ref[...] = jnp.zeros_like(dv_ref)

        def score(index, carry):
            start = pl.multiple_of(index * block, block)
            here = pl.ds(start, block)
            query, coming = query_ref[here, slot], wide_mixed_ref[here, slot]
            scores = lax.dot_general(
                key_ref[:, slot], query, (((1,), (1,)), ((), ())),
                preferred_element_type=jnp.float32,
            )
            probs = jnp.exp(scores) * inverse_ref[head : head + 1, here]
            grad_probs = lax.dot_general(
                value_ref[:, slot], coming, (((1,), (1,)), ((), ())),
                preferred_element_type=jnp.float32,
            )
            inner = jnp.sum(probs * grad_probs, axis=0, keepdims=True)
            grad_scores = (probs * (grad_probs - inner)).astype(jnp.bfloat16)
            dv_ref[...] += jnp.dot(
                probs.astype(jnp.bfloat16), coming, preferred_element_type=jnp.float32
            )
            dk_ref[...] += jnp.dot(grad_scores, query, preferred_element_type=jnp.float32)
            dq_ref[here] = jnp.dot(
                key_t_ref[...], grad_scores, preferred_element_type=jnp.float32
            ).T
            return carry

        lax.fori_loop(0, total // block, score, 0)

        def unturn(index, carry):
            here = pl.ds(pl.multiple_of(index * tile, tile), tile)
            cos, lead, trail = cos_ref[here], lead_ref[here], trail_ref[here]
            for part, source in ((0, dq_ref), (1, dk_ref)):
                coming = source[here]
                if part == 0:
                    coming = coming * (1.0 / math.sqrt(size))
                coming = (
                    coming * cos
                    - pltpu.roll(coming, LANE - size // 4, 1) * lead
                    - pltpu.roll(coming, size // 4, 1) * trail
                )
                start = part * span + head * LANE
                raw = raw_ref[here, start : start + LANE]
                square = jnp.sum(raw * raw, axis=-1, keepdims=True) * (1.0 / size)
                inverse = lax.rsqrt(square + norm_eps)
                unit = raw * inverse
                scaled = coming * gain_row(gains_ref, part, size)
                slope = jnp.sum(scaled * unit, axis=-1, keepdims=True) * (1.0 / size)
                grad_ref[here, start : start + LANE] = (
                    inverse * (scaled - unit * slope)
                ).astype(jnp.bfloat16)
                gain_ref[part : part + 1] += jnp.sum(coming * unit, axis=0, keepdims=True)
            start = 2 * span + head * LANE
            grad_ref[here, start : start + LANE] = dv_ref[here].astype(jnp.bfloat16)
            return carry

        lax.fori_loop(0, total // tile, unturn, 0)
        hook()

    def project(index, carry):
        here = pl.ds(pl.multiple_of(index * tile, tile), tile)
        normed_ref[here] = lax.dot_general(
            grad_ref[here], wide_ref[...], (((1,), (1,)), ((), ())),
            preferred_element_type=jnp.float32,
        ).astype(jnp.bfloat16)
        return carry

    lax.fori_loop(0, total // tile, project, 0)


def attend_back_kernel(
    heads, size, mixed_ref, raw_ref, query_ref, key_ref, value_ref, inverse_ref,
    cos_ref, lead_ref, trail_ref, gains_ref, wide_ref, pair_ref, down_ref, out_ref,
    grad_ref, normed_ref, gain_ref, pair_sum_ref, down_sum_ref, out_sum_ref,
    wide_mixed_ref, key_t_ref, dq_ref, dk_ref, dv_ref,
    pair_total_ref, down_total_ref, out_total_ref, pair_land_ref, down_land_ref, out_land_ref,
    out_near_ref, out_move_ref, out_far_ref, out_own_ref,
    ring_send, ring_recv, late_send, late_recv, out_send, out_recv,
):
    rank, count = lax.axis_index("seq"), lax.axis_size("seq")
    row_rank, row_count = lax.axis_index("dp"), lax.axis_size("dp")
    packs = mixed_ref.shape[0]
    greet(ring_peers(row_rank, row_count) + seq_peers(rank, count))
    ring = RingReduce(
        [pair_ref, down_ref], [pair_sum_ref, down_sum_ref], [pair_total_ref, down_total_ref],
        [pair_land_ref, down_land_ref], row_rank, row_count, ring_send, ring_recv,
    )
    ring.advance()
    mate, across = flip(rank, 1), flip(rank, 2)
    near = [
        send(
            out_ref.at[flip(mate, 2) if index else mate], out_near_ref.at[index],
            out_send.at[index], out_recv.at[index], {"seq": mate},
        )
        for index in range(2)
    ]
    late = RingReduce(
        [out_own_ref], [out_sum_ref], [out_total_ref], [out_land_ref], row_rank, row_count,
        late_send, late_recv,
    )
    marks, moved = [0], []
    stride = max(1, packs * heads // (row_count // 2))

    def hook():
        marks[0] += 1
        if marks[0] == 1:
            near[1].wait_recv()
            out_move_ref[...] = (
                out_ref[across].astype(jnp.float32) + out_near_ref[1].astype(jnp.float32)
            ).astype(jnp.bfloat16)
            moved.append(
                send(out_move_ref, out_far_ref, out_send.at[2], out_recv.at[2], {"seq": across})
            )
        if marks[0] == packs * heads // 2:
            near[0].wait_recv()
            moved[0].wait_recv()
            own = (
                out_ref[rank].astype(jnp.float32)
                + out_near_ref[0].astype(jnp.float32)
                + out_far_ref[...].astype(jnp.float32)
            )
            out_own_ref[0] = own.astype(jnp.bfloat16).reshape(out_own_ref.shape[1:])
            late.advance()
        elif marks[0] > packs * heads // 2 and late.going:
            late.advance()
        if marks[0] % stride == 0 and ring.going:
            ring.advance()

    gain_ref[...] = jnp.zeros_like(gain_ref)
    for pack in range(packs):
        attend_back_pack(
            heads, size, hook, mixed_ref.at[pack], raw_ref.at[pack], query_ref.at[pack],
            key_ref.at[pack], value_ref.at[pack], inverse_ref.at[pack], cos_ref.at[pack],
            lead_ref.at[pack], trail_ref.at[pack], gains_ref, wide_ref, grad_ref.at[pack],
            normed_ref.at[pack], gain_ref, wide_mixed_ref, key_t_ref, dq_ref, dk_ref, dv_ref,
        )
    ring.finish()
    late.finish()
    for copy in near + moved:
        copy.wait_send()


def attend_back(mixed, saved, turns, gains, wide, pair, down, out, heads, size):
    packs, total, slab = mixed.shape
    count, row_count = lax.axis_size("seq"), lax.axis_size("dp")
    steps = row_count // 2
    span = heads * LANE
    width = wide.shape[0]
    rows = width // row_count
    low, full = jnp.bfloat16, jnp.float32
    blocks = [
        (pair.shape[0],) + pair.shape[2:], (down.shape[0],) + down.shape[2:], (1, rows, slab)
    ]
    inside = pl.BlockSpec(memory_space=pltpu.VMEM)
    dma = pltpu.SemaphoreType.DMA
    return pl.pallas_call(
        partial(attend_back_kernel, heads, size),
        out_shape=[
            jax.ShapeDtypeStruct((packs, total, 3 * span), low),
            jax.ShapeDtypeStruct((packs, total, width), low),
            jax.ShapeDtypeStruct((2, LANE), full),
        ] + [jax.ShapeDtypeStruct(block, full) for block in blocks],
        in_specs=[inside] * 14,
        out_specs=[inside] * 6,
        scratch_shapes=[
            pltpu.VMEM((total, span), low),
            pltpu.VMEM((LANE, total), low),
            pltpu.VMEM((total, LANE), full),
            pltpu.VMEM((total, LANE), full),
            pltpu.VMEM((total, LANE), full),
        ]
        + [pltpu.VMEM((2, steps - 1) + block, low) for block in blocks]
        + [pltpu.VMEM((2, steps) + block, low) for block in blocks]
        + [
            pltpu.VMEM((2, width, slab), low), pltpu.VMEM((width, slab), low),
            pltpu.VMEM((width, slab), low), pltpu.VMEM((1, row_count, rows, slab), low),
            dma((2, steps, 2)), dma((2, steps, 2)), dma((2, steps, 1)), dma((2, steps, 1)),
            dma((3,)), dma((3,)),
        ],
        compiler_params=pltpu.CompilerParams(
            collective_id=3, has_side_effects=True, vmem_limit_bytes=62 * 1024 * 1024
        ),
        name="attend_back",
    )(mixed, *saved, *turns, gains, wide, pair, down, out)


def closing_kernel(
    heads, size, items, normed_ref, wide_ref, part_ref, tok_ref, ids_ref, rows_ref, middle_ref,
    mods_ref, cond_ref, gain_ref, pair_ref, down_ref, out_ref,
    tokens_ref, qkv_sum_ref, gateup_sum_ref, down_sum_ref, mod_sum_ref, bias_sum_ref,
    gain_sum_ref, square_ref,
    landed_ref, total_ref, grad_a_ref, grad_b_ref, sum_a_ref, sum_b_ref, tot_a_ref, tot_b_ref,
    land_a_ref, land_b_ref, head_src_ref, head_x_ref, pair_x_ref, down_src_ref, down_x_ref,
    first_ref, mod_src_ref, mod_x_ref, mod_own_ref, mod_all_ref, norm_own_ref, norm_x_ref,
    norm_mid_ref, norm_all_ref,
    part_send, part_recv, ring_send, ring_recv, head_send, head_recv, near_send, near_recv,
    far_send, far_recv,
):
    rank, count = lax.axis_index("seq"), lax.axis_size("seq")
    row_rank, row_count = lax.axis_index("dp"), lax.axis_size("dp")
    packs, total, width = normed_ref.shape
    length = total // count
    slab = heads * size
    span = heads * LANE
    rows = width // row_count
    low, full = jnp.bfloat16, jnp.float32
    far, near = far_peers(row_rank, row_count), seq_peers(rank, count)
    greet(far + near)

    def exchange(kind, source, target):
        return [
            send(
                source(peer["seq"]), target.at[rank], near_send.at[kind, offset],
                near_recv.at[kind, offset], peer,
            )
            for offset, peer in enumerate(near)
        ]

    reduces = [
        CubeReduce(
            part_ref.at[pack], landed_ref.at[pack], total_ref.at[pack], rank, count,
            part_send.at[pack], part_recv.at[pack],
        )
        for pack in range(packs)
    ]
    for reduce in reduces:
        reduce.near()
    copies = exchange(0, lambda peer: pair_ref.at[peer], pair_x_ref)
    pair_x_ref[rank] = pair_ref[rank]
    for index in range(count):
        down_src_ref[index] = down_ref[0, :, index * slab : (index + 1) * slab]
    copies += exchange(1, lambda peer: down_src_ref.at[peer], down_x_ref)
    down_x_ref[rank] = down_src_ref[rank]

    strip = 2 * rows
    cut = grad_a_ref.shape[3]
    for index in range(width // strip):
        start = index * strip
        left = [normed_ref[pack, :, start : start + strip].T for pack in range(packs)]
        pieces = []
        for part in range(3):
            grad = sum(
                dot(left[pack], wide_ref[pack, :, part * span : (part + 1) * span])
                for pack in range(packs)
            ).astype(low)
            pieces += [grad[:, head * LANE : head * LANE + size] for head in range(heads)]
        grad = jnp.concatenate(pieces, axis=1)
        for side in range(2):
            here = slice(side * rows, (side + 1) * rows)
            grad_a_ref[0, 2 * index + side] = grad[here, :cut]
            grad_b_ref[0, 2 * index + side] = grad[here, cut:]
        if index < packs:
            reduces[index].across()
    ring = RingReduce(
        [grad_a_ref, grad_b_ref], [sum_a_ref, sum_b_ref], [tot_a_ref, tot_b_ref],
        [land_a_ref, land_b_ref], row_rank, row_count, ring_send, ring_recv,
    )
    ring.advance()

    first_ref[...] = jnp.zeros_like(first_ref)
    for pack in range(packs):
        ids = ids_ref[pack, :length]
        normal, inverse = normalized(tok_ref[pack].astype(full))
        grad_normed = reduces[pack].result()
        scale = chosen(ids, rows_ref, 1, pack, items)
        tokens_ref[pack] = (
            middle_ref[pack] + normalized_back(normal, inverse, grad_normed * (1.0 + scale))
        ).astype(low)
        for which, values in enumerate((grad_normed, grad_normed * normal)):
            for item in range(items):
                line = items * pack + item
                first_ref[which, line : line + 1] = jnp.sum(
                    jnp.where(ids == item, values, 0.0), axis=0, keepdims=True
                )
    used = items * packs
    columns = mod_src_ref.shape[2]
    full_rows = jnp.concatenate(
        [first_ref[0], first_ref[1]] + [mods_ref[index] for index in range(4)], axis=1
    )
    for index in range(count):
        mod_src_ref[index] = full_rows[:, index * columns : (index + 1) * columns]
        mod_src_ref[index, used : used + 2, :LANE] = gain_ref[...]
    mod_near = exchange(2, lambda peer: mod_src_ref.at[peer], mod_x_ref)
    mod_x_ref[rank] = mod_src_ref[rank]
    ring.advance()
    for copy in mod_near:
        copy.wait_recv()
    mod_own_ref[...] = sum(mod_x_ref[index] for index in range(count))
    mod_far = [
        send(
            mod_own_ref, mod_all_ref.at[row_rank], far_send.at[0, offset], far_recv.at[0, offset],
            peer,
        )
        for offset, peer in enumerate(far)
    ]
    mod_all_ref[row_rank] = mod_own_ref[...]
    ring.advance()
    for copy in copies:
        copy.wait_recv()
    hidden_rows = down_src_ref.shape[1]
    groups = pair_ref.shape[2] // hidden_rows
    pieces = []
    for group in range(groups):
        for index in range(count):
            pieces.append(pair_x_ref[index, :, group * hidden_rows : (group + 1) * hidden_rows])
    gateup = jnp.concatenate(pieces, axis=1)
    gateup_sum_ref[...] = gateup
    square = jnp.sum(gateup * gateup)
    for index in range(count):
        block = down_x_ref[index]
        down_sum_ref[index * hidden_rows : (index + 1) * hidden_rows] = block
        square += jnp.sum(block * block)
    square += jnp.sum(out_ref[...] * out_ref[...])
    for copy in mod_far:
        copy.wait_recv()
    lines = mod_all_ref.shape[1]
    every = mod_all_ref[...].reshape(row_count * lines, columns)
    conditions = cond_ref[...].reshape(row_count * lines, rows).astype(low)
    high = every.astype(low)
    mod_sum = t_dot(conditions, high) + t_dot(conditions, (every - high.astype(full)).astype(low))
    mod_sum_ref[...] = mod_sum
    square += jnp.sum(mod_sum * mod_sum)
    gains, bias = 0.0, 0.0
    for index in range(row_count):
        gains += mod_all_ref[index, used : used + 2, :LANE]
        bias += jnp.sum(mod_all_ref[index, :used], axis=0, keepdims=True)
    gain_sum_ref[...] = gains
    bias_sum_ref[...] = bias
    square += jnp.sum(bias * bias) * (1.0 / row_count)
    ring.finish()
    summed = jnp.concatenate([sum_a_ref[0], sum_b_ref[0]], axis=1)
    square += jnp.sum(summed * summed)
    norm_own_ref[...] = jnp.full(norm_own_ref.shape, square, full)
    norm_near = exchange(3, lambda peer: norm_own_ref, norm_x_ref)
    norm_x_ref[rank] = norm_own_ref[...]
    for slot in range(3):
        head_src_ref[slot] = summed[:, slot * slab : (slot + 1) * slab]

    def head_copy(slot, index, peer):
        return pltpu.make_async_remote_copy(
            src_ref=head_src_ref.at[slot], dst_ref=head_x_ref.at[index],
            send_sem=head_send.at[slot], recv_sem=head_recv.at[index],
            device_id={"seq": peer}, device_id_type=pl.DeviceIdType.MESH,
        )

    moves = []
    for slot in range(3):
        peer, index = (slot * count + rank) // 3, (slot * count + rank) % 3
        moves.append((peer, index))

        @pl.when(peer != rank)
        def _():
            head_copy(slot, index, peer).start()

        @pl.when(peer == rank)
        def _():
            head_x_ref[index] = head_src_ref[slot]

    for copy in norm_near:
        copy.wait_recv()
    norm_mid_ref[...] = sum(norm_x_ref[index] for index in range(count))
    norm_far = [
        send(
            norm_mid_ref, norm_all_ref.at[row_rank], far_send.at[1, offset],
            far_recv.at[1, offset], peer,
        )
        for offset, peer in enumerate(far)
    ]
    norm_all_ref[row_rank] = norm_mid_ref[...]
    for index in range(3):
        source = (3 * rank + index) % count

        @pl.when(source != rank)
        def _():
            head_copy(index, index, source).wait_recv()

    qkv_sum_ref[...] = jnp.concatenate([head_x_ref[index] for index in range(3)], axis=1)
    for copy in norm_far:
        copy.wait_recv()
    squares = sum(norm_all_ref[index] for index in range(row_count))
    square_ref[...] = squares + jnp.sum(gains * gains)
    for slot, (peer, index) in enumerate(moves):
        @pl.when(peer != rank)
        def _():
            head_copy(slot, index, peer).wait_send()

    for reduce in reduces:
        reduce.settle()
    for copy in copies + mod_near + mod_far + norm_near + norm_far:
        copy.wait_send()


def closing(
    normed, wide, part, tok, ids, rows, middle_grad, mods, cond, gain, pair, down, out, items,
    heads, size,
):
    packs, total, width = normed.shape
    count, row_count = lax.axis_size("seq"), lax.axis_size("dp")
    length, slab = total // count, heads * size
    my_rows = width // row_count
    steps = row_count // 2
    low, full = jnp.bfloat16, jnp.float32
    lines = rows.shape[1]
    columns = 6 * width // count
    hidden_rows = down.shape[1]
    cut = -(-3 * slab // (2 * LANE)) * LANE
    sides = [(1, my_rows, cut), (1, my_rows, 3 * slab - cut)]
    shapes = [
        jax.ShapeDtypeStruct((packs, length, width), low),
        jax.ShapeDtypeStruct((my_rows, 3 * slab), full),
        jax.ShapeDtypeStruct((my_rows, pair.shape[0] * pair.shape[2]), full),
        jax.ShapeDtypeStruct((count * hidden_rows, slab), full),
        jax.ShapeDtypeStruct((my_rows, columns), full),
        jax.ShapeDtypeStruct((1, columns), full),
        jax.ShapeDtypeStruct((2, LANE), full),
        jax.ShapeDtypeStruct((8, LANE), full),
    ]
    inside = pl.BlockSpec(memory_space=pltpu.VMEM)
    dma = pltpu.SemaphoreType.DMA
    return pl.pallas_call(
        partial(closing_kernel, heads, size, items),
        out_shape=shapes,
        in_specs=[inside] * 13,
        out_specs=[inside] * len(shapes),
        scratch_shapes=[
            pltpu.VMEM((packs, total // 2 + length, width), low),
            pltpu.VMEM((packs, length, width), low),
        ]
        + [pltpu.VMEM((1, row_count) + side[1:], low) for side in sides]
        + [pltpu.VMEM(side, full) for side in sides]
        + [pltpu.VMEM((2, steps - 1) + side, low) for side in sides]
        + [pltpu.VMEM((2, steps) + side, low) for side in sides]
        + [
            pltpu.VMEM((3, my_rows, slab), full),
            pltpu.VMEM((3, my_rows, slab), full),
            pltpu.VMEM(pair.shape, full),
            pltpu.VMEM((count, hidden_rows, slab), full),
            pltpu.VMEM((count, hidden_rows, slab), full),
            pltpu.VMEM((2, lines, width), full),
            pltpu.VMEM((count, lines, columns), full),
            pltpu.VMEM((count, lines, columns), full),
            pltpu.VMEM((lines, columns), full),
            pltpu.VMEM((row_count, lines, columns), full),
            pltpu.VMEM((8, LANE), full),
            pltpu.VMEM((count, 8, LANE), full),
            pltpu.VMEM((8, LANE), full),
            pltpu.VMEM((row_count, 8, LANE), full),
            dma((packs, 2)), dma((packs, 2)),
            dma((2, steps, 2)), dma((2, steps, 2)),
            dma((3,)), dma((3,)), dma((4, count - 1)), dma((4, count - 1)),
            dma((2, row_count - 1)), dma((2, row_count - 1)),
        ],
        compiler_params=pltpu.CompilerParams(
            collective_id=4, has_side_effects=True, vmem_limit_bytes=60 * 1024 * 1024
        ),
        name="closing",
    )(normed, wide, part, tok, ids, rows, middle_grad, mods, cond, gain, pair, down, out)


def on_device(
    tokens,
    cotangent,
    condition,
    item_lengths,
    item_widths,
    qkv_weight,
    qkv_first,
    qkv_second,
    out_weight,
    out_first,
    out_second,
    gateup_weight,
    gateup_first,
    gateup_second,
    down_weight,
    down_first,
    down_second,
    mod_weight,
    mod_first,
    mod_second,
    mod_bias,
    bias_first,
    bias_second,
    qk_gains,
    gains_first,
    gains_second,
):
    packs, length, width = tokens.shape
    items = condition.shape[1]
    size = width // HEADS
    count, row_count = lax.axis_size("seq"), lax.axis_size("dp")
    heads = HEADS // count
    rows = qkv_weight.shape[0]

    lines = -(-(packs * items + 2) // 8) * 8
    cond = jnp.pad(condition.reshape(packs * items, width), ((0, lines - packs * items), (0, 0)))
    (
        tok_all, ids, cos, lead, trail, mod_rows, cond_rows, wide, out_all, pair_own, down_own,
    ) = opening(
        item_lengths, item_widths, tokens, cond, qkv_weight, out_weight, gateup_weight,
        down_weight, mod_weight, mod_bias[None], heads, size,
    )
    turns = (cos, lead, trail)
    wide = wide.reshape(width, wide.shape[2])
    normed, raw, query, key, value, inverse, mixed, out_full, pair_all, cot_all = attend(
        tok_all, ids, mod_rows, turns, qk_gains, wide, out_all, pair_own, cotangent, items, heads,
        size,
    )
    layer_out, grad_mixed, grad_middle, mod_part, pair_grad, down_grad, out_grad = middle(
        mixed, tokens, ids, mod_rows, cot_all, out_full.reshape(width, width),
        pair_all.reshape(count, width, -1), down_own, items,
    )
    grad_wide, grad_part, gain_part, pair_sum, down_sum, out_sum = attend_back(
        grad_mixed, (raw, query, key, value, inverse), turns, qk_gains, wide,
        pair_grad.reshape(count, row_count, rows, -1),
        down_grad.reshape(1, row_count, -1, width), out_grad, heads, size,
    )
    tokens_grad, qkv_sum, gateup_sum, down_sum, mod_sum, bias_sum, gain_sum, square = closing(
        normed, grad_wide, grad_part, tokens, ids, mod_rows, grad_middle, mod_part, cond_rows,
        gain_part, pair_sum, down_sum, out_sum, items, heads, size,
    )
    grad_norm = jnp.sqrt(square[0, 0])
    factor = clip_limit / jnp.maximum(grad_norm, clip_limit)
    results = [layer_out, tokens_grad, grad_norm]
    results += adam_update(qkv_weight, qkv_first, qkv_second, qkv_sum, factor)
    results += adam_update(out_weight, out_first, out_second, out_sum[0], factor)
    results += adam_update(gateup_weight, gateup_first, gateup_second, gateup_sum, factor)
    results += adam_update(down_weight, down_first, down_second, down_sum, factor)
    results += adam_update(mod_weight, mod_first, mod_second, mod_sum, factor)
    results += adam_update(mod_bias, bias_first, bias_second, bias_sum[0], factor)
    results += adam_update(qk_gains, gains_first, gains_second, gain_sum[:, :size], factor)
    return tuple(results)


def solution(mesh):
    return jax.shard_map(
        on_device,
        mesh=mesh,
        in_specs=(
            P("dp", "seq", None),
            P("dp", "seq", None),
            P("dp", None, None),
            P("dp", None),
            P("dp", None),
            P("dp", "seq"),
            P("dp", "seq"),
            P("dp", "seq"),
            P("dp", "seq"),
            P("dp", "seq"),
            P("dp", "seq"),
            P("dp", "seq"),
            P("dp", "seq"),
            P("dp", "seq"),
            P("dp", "seq"),
            P("dp", "seq"),
            P("dp", "seq"),
            P("dp", "seq"),
            P("dp", "seq"),
            P("dp", "seq"),
            P("seq"),
            P("seq"),
            P("seq"),
            P(),
            P(),
            P(),
        ),
        out_specs=(
            P("dp", "seq", None),
            P("dp", "seq", None),
            P(),
            P("dp", "seq"),
            P("dp", "seq"),
            P("dp", "seq"),
            P("dp", "seq"),
            P("dp", "seq"),
            P("dp", "seq"),
            P("dp", "seq"),
            P("dp", "seq"),
            P("dp", "seq"),
            P("dp", "seq"),
            P("dp", "seq"),
            P("dp", "seq"),
            P("dp", "seq"),
            P("dp", "seq"),
            P("dp", "seq"),
            P("seq"),
            P("seq"),
            P("seq"),
            P(),
            P(),
            P(),
        ),
        check_vma=False,
    )
```

```python
from functools import partial
import math

import jax
import jax.numpy as jnp
import numpy as np
from jax import lax
from jax.experimental import pallas as pl
from jax.experimental.pallas import tpu as pltpu
from jax.sharding import PartitionSpec as P

HEADS = 16
OPT_STEP = 10


norm_eps = 1e-06
clip_limit = 1.0
beta_one = 0.9
beta_two = 0.95
adam_eps = 1e-08
learn_rate = 0.06
decay_rate = 0.01


def adam_update(master, moment, square, gradient, factor):
    clipped = gradient * factor
    moment_new = beta_one * moment + (1.0 - beta_one) * clipped
    square_new = beta_two * square + (1.0 - beta_two) * clipped * clipped
    moment_hat = moment_new / (1.0 - beta_one**OPT_STEP)
    square_hat = square_new / (1.0 - beta_two**OPT_STEP)
    master_new = master - learn_rate * (
        moment_hat / (jnp.sqrt(square_hat) + adam_eps) + decay_rate * master
    )
    return (master_new, moment_new, square_new)


LANE = 128
PROJECT_TILE = 384
SCORE_TILE = 768
BACK_TILE = 384
BACK_SCORE_TILE = 768


def fit(total, wanted):
    size = min(total, wanted)
    while total % size:
        size -= 8
    return size


def spread_matrix(heads, size):
    row = lax.broadcasted_iota(jnp.int32, (heads * size, heads * LANE), 0)
    column = lax.broadcasted_iota(jnp.int32, (heads * size, heads * LANE), 1)
    hit = row < 0
    for head in range(heads):
        inside = (column >= head * LANE) & (column < head * LANE + size)
        hit = hit | (inside & (row - column == head * (size - LANE)))
    return jnp.where(hit, 1.0, 0.0).astype(jnp.bfloat16)


def cube_slot(offset, count):
    bits = count.bit_length() - 1
    return sum(((offset // 2**bit) % 2) * 2 ** (bits - 1 - bit) for bit in range(bits))


def chosen(ids, rows_ref, which, pack, items):
    first = items * pack
    choice = rows_ref[which, first + items - 1 : first + items]
    for item in range(items - 2, -1, -1):
        choice = jnp.where(ids == item, rows_ref[which, first + item : first + item + 1], choice)
    return choice


def dot(left, right):
    return jnp.dot(left, right, preferred_element_type=jnp.float32)


def dot_t(left, right):
    return lax.dot_general(left, right, (((1,), (1,)), ((), ())), preferred_element_type=jnp.float32)


def t_dot(left, right):
    return lax.dot_general(left, right, (((0,), (0,)), ((), ())), preferred_element_type=jnp.float32)


def normalized(values):
    centered = values - jnp.mean(values, axis=-1, keepdims=True)
    inverse = lax.rsqrt(jnp.mean(centered * centered, axis=-1, keepdims=True) + norm_eps)
    return centered * inverse, inverse


def normalized_back(normal, inverse, incoming):
    return inverse * (
        incoming
        - jnp.mean(incoming, axis=-1, keepdims=True)
        - normal * jnp.mean(incoming * normal, axis=-1, keepdims=True)
    )


def gain_row(gains_ref, part, size):
    return jnp.concatenate(
        [1.0 + gains_ref[part : part + 1], jnp.zeros((1, LANE - size), jnp.float32)], axis=1
    )


def flip(rank, step):
    return rank + step - 2 * step * ((rank // step) % 2)


def xor(rank, offset):
    step = 1
    while step <= offset:
        if offset & step:
            rank = flip(rank, step)
        step *= 2
    return rank


def cube_order(count):
    order, step = [0], count // 2
    while step:
        order = order + [place ^ step for place in order]
        step //= 2
    return order


def ring_place(rank, count):
    side = rank % 2
    return (rank // 2) * (1 - 2 * side) + (count - 1) * side


def ring_rank(place, count):
    place = (place + count) % count
    side = place // (count // 2)
    return 2 * place * (1 - side) + (2 * (count - 1 - place) + 1) * side


def send(source, target, send_sem, recv_sem, where):
    copy = pltpu.make_async_remote_copy(
        src_ref=source, dst_ref=target, send_sem=send_sem, recv_sem=recv_sem,
        device_id=where, device_id_type=pl.DeviceIdType.MESH,
    )
    copy.start()
    return copy


def greet(targets):
    barrier = pltpu.get_barrier_semaphore()
    for target in targets:
        pl.semaphore_signal(
            barrier, inc=1, device_id=target, device_id_type=pl.DeviceIdType.MESH
        )
    pl.semaphore_wait(barrier, len(targets))


def seq_peers(rank, count):
    return [{"seq": xor(rank, offset)} for offset in range(1, count)]


def far_peers(rank, count):
    return [{"dp": (rank + offset) % count} for offset in range(1, count)]


def ring_peers(rank, count):
    place = ring_place(rank, count)
    return [{"dp": ring_rank(place + 1, count)}, {"dp": ring_rank(place - 1, count)}]


def far_part(index, lead, way):
    if lead == 1:
        return (0, 1) if index % 2 == way else (0, 0)
    cut = (lead + 1) // 2
    return (cut, lead) if way else (0, cut)


class RingGather:
    def __init__(self, buffers, rank, count, send_sems, recv_sems, use=None):
        self.buffers, self.count, self.use = buffers, count, use
        self.place = ring_place(rank, count)
        self.send_sems, self.recv_sems = send_sems, recv_sems
        self.steps = count // 2
        self.sent, self.going = [], []
        self.step = 0

    def launch_first(self):
        self.advance_links()

    def use_first(self):
        self.use(ring_rank(self.place, self.count))

    def advance_links(self):
        step = self.step
        if step > self.steps:
            return
        self.step += 1
        arriving, self.going = self.going, []
        for index in range(len(self.buffers)):
            for place, copy in arriving:
                if place == index:
                    copy.wait_recv()
                    self.sent.append(copy)
            if step < self.steps:
                self.launch(step, index)

    def advance(self):
        step = self.step
        self.advance_links()
        if self.use is not None and step <= self.steps:
            self.use(ring_rank(self.place - step, self.count))
            if 0 < step < self.steps:
                self.use(ring_rank(self.place + step, self.count))

    def launch(self, step, index):
        buffer = self.buffers[index]
        for way in range(2):
            sign = 1 - 2 * way
            block = ring_rank(self.place - sign * step, self.count)
            where = {"dp": ring_rank(self.place + sign, self.count)}
            low, high = 0, buffer.shape[0]
            if step == self.steps - 1:
                low, high = far_part(index, high, way)
                if low == high:
                    continue
            view = buffer.at[pl.ds(low, high - low), block]
            copy = send(
                view, view, self.send_sems.at[way, step, index],
                self.recv_sems.at[way, step, index], where,
            )
            self.going.append((index, copy))

    def finish(self):
        while self.step <= self.steps:
            self.advance()
        for copy in self.sent:
            copy.wait_send()


class RingReduce:
    def __init__(self, sources, results, totals, landed, rank, count, send_sems, recv_sems):
        self.sources, self.results, self.totals, self.landed = sources, results, totals, landed
        self.count, self.steps = count, count // 2
        self.place = ring_place(rank, count)
        self.send_sems, self.recv_sems = send_sems, recv_sems
        self.sent, self.going = [], []
        self.step = 0

    def advance(self):
        step = self.step
        if step > self.steps:
            return
        self.step += 1
        arriving, self.going = self.going, []
        for index in range(len(self.sources)):
            for place, copy in arriving:
                if place == index:
                    copy.wait_recv()
                    self.sent.append(copy)
            if step < self.steps:
                self.launch(step, index)
            else:
                self.total(step, index)

    def total(self, step, index):
        source = self.sources[index]
        mine = ring_rank(self.place, self.count)
        for lead in range(source.shape[0]):
            total = source[lead, mine].astype(jnp.float32)
            for way in range(2):
                total += self.landed[index][way, step - 1, lead].astype(jnp.float32)
            self.results[index][lead] = total

    def launch(self, step, index):
        source = self.sources[index]
        size = source.shape[0]
        for way in range(2):
            sign = 1 - 2 * way
            block = ring_rank(self.place + sign * (self.steps - step), self.count)
            where = {"dp": ring_rank(self.place + sign, self.count)}
            low, high = far_part(index, size, way)
            if step == 0:
                if low == high:
                    continue
                view = source.at[pl.ds(low, high - low), block]
                target = self.landed[index].at[way, step, pl.ds(low, high - low)]
            else:
                for lead in range(size):
                    total = source[lead, block]
                    if step > 1 or low <= lead < high:
                        total = (
                            total.astype(jnp.float32)
                            + self.landed[index][way, step - 1, lead].astype(jnp.float32)
                        ).astype(total.dtype)
                    self.totals[index][way, step - 1, lead] = total
                view = self.totals[index].at[way, step - 1]
                target = self.landed[index].at[way, step]
            copy = send(
                view, target, self.send_sems.at[way, step, index],
                self.recv_sems.at[way, step, index], where,
            )
            self.going.append((index, copy))

    def finish(self):
        while self.step <= self.steps:
            self.advance()
        for copy in self.sent:
            copy.wait_send()


class CubeGather:
    def __init__(self, source, target, rank, count, send_sems, recv_sems):
        self.source, self.target, self.rank = source, target, rank
        self.length = source.shape[0]
        self.send_sems, self.recv_sems = send_sems, recv_sems
        self.steps = [count >> (level + 1) for level in range(count.bit_length() - 1)]
        self.copies = {}
        self.level = 0
        for level in range(len(self.steps)):
            self.launch(0, level)

    def launch(self, slot, level):
        landing = slot + 2**level
        view = self.source
        if slot:
            view = self.target.at[pl.ds(slot * self.length, self.length)]
        self.copies[slot, level] = send(
            view, self.target.at[pl.ds(landing * self.length, self.length)],
            self.send_sems.at[landing - 1], self.recv_sems.at[landing - 1],
            {"seq": flip(self.rank, self.steps[level])},
        )

    def advance(self):
        level = self.level
        if level >= len(self.steps):
            return
        self.level += 1
        for slot in range(2**level):
            self.copies[slot, level].wait_recv()
        for later in range(level + 1, len(self.steps)):
            for slot in range(2**level, 2 ** (level + 1)):
                self.launch(slot, later)

    def finish(self):
        while self.level < len(self.steps):
            self.advance()

    def settle(self):
        for copy in self.copies.values():
            copy.wait_send()


class CubeReduce:
    def __init__(self, parts, landed, total, rank, count, send_sems, recv_sems):
        self.parts, self.landed, self.total, self.rank = parts, landed, total, rank
        self.length = parts.shape[0] // count
        self.half = parts.shape[0] // 2
        self.send_sems, self.recv_sems = send_sems, recv_sems
        self.copies = []

    def near(self):
        view = self.parts.at[pl.ds(self.half, self.half)]
        self.copies.append(
            send(
                view, self.landed.at[pl.ds(0, self.half)], self.send_sems.at[0],
                self.recv_sems.at[0], {"seq": flip(self.rank, 1)},
            )
        )

    def across(self):
        self.copies[0].wait_recv()
        here = pl.ds(self.length, self.length)
        self.total[...] = (
            self.parts[here].astype(jnp.float32) + self.landed[here].astype(jnp.float32)
        ).astype(self.total.dtype)
        self.copies.append(
            send(
                self.total, self.landed.at[pl.ds(self.half, self.length)], self.send_sems.at[1],
                self.recv_sems.at[1], {"seq": flip(self.rank, 2)},
            )
        )

    def result(self):
        self.copies[1].wait_recv()
        own = pl.ds(0, self.length)
        return (
            self.parts[own].astype(jnp.float32)
            + self.landed[own].astype(jnp.float32)
            + self.landed[pl.ds(self.half, self.length)].astype(jnp.float32)
        )

    def settle(self):
        for copy in self.copies:
            copy.wait_send()


class Mover:
    def __init__(self, sems):
        self.sems, self.used, self.stores = sems, 0, []

    def load(self, source, target):
        copy = pltpu.make_async_copy(source, target, self.sems.at[self.used])
        self.used += 1
        copy.start()
        return copy

    def store(self, source, target):
        self.stores.append(self.load(source, target))

    def finish(self):
        for copy in self.stores:
            copy.wait()


def narrow_parts(values):
    slab = values.shape[1]
    cut = slab // LANE * LANE
    per = LANE // (slab - cut)
    step = values.shape[0] // per
    tail = [values[index * step : (index + 1) * step, cut:] for index in range(per)]
    return values[:, :cut], jnp.concatenate(tail, axis=1)


def join_parts(wide, packed):
    per = wide.shape[0] // packed.shape[0]
    rest = LANE // per
    tail = [packed[:, index * rest : (index + 1) * rest] for index in range(per)]
    return jnp.concatenate([wide, jnp.concatenate(tail, axis=0)], axis=1)


def token_layout(pack, slot_rank, length, lengths_ref, widths_ref):
    items = lengths_ref.shape[1]
    place = lax.broadcasted_iota(jnp.int32, (length, 1), 0) + slot_rank * length
    ids = jnp.zeros_like(place)
    start = jnp.zeros_like(place)
    width = jnp.zeros_like(place) + widths_ref[pack, 0]
    end = 0
    for item in range(1, items):
        end = end + lengths_ref[pack, item - 1]
        inside = place >= end
        ids = jnp.where(inside, item, ids)
        start = jnp.where(inside, end, start)
        width = jnp.where(inside, widths_ref[pack, item], width)
    offset = (place - start).astype(jnp.float32)
    width = width.astype(jnp.float32)
    row = jnp.floor((offset + 0.5) / width)
    return ids, row, offset - row * width


def frequencies(size):
    quarter = size // 4
    lane = np.arange(LANE)
    table = np.where(lane < size, 10000.0 ** (-(lane % quarter) / quarter), 0.0)
    return table.astype(np.float32)[None]


def open_kernel(
    heads, size, items,
    lengths_ref, widths_ref, cond_ref, bias_ref, freq_ref, qkv_any, out_any, tok_any, cot_any, pair_any,
    down_any, modw_any,
    tok_all_any, cot_all_any, ids_ref, cos_any, lead_any, trail_any, mod_ref, cond_all_ref,
    wide_any, out_a_ref, out_b_ref, pair_x_ref, down_own_ref,
    qkv_ref, out_ref, tok_ref, cot_ref, pair_ref, down_ref, modw_ref,
    tok_all_ref, cot_all_ref, cos_ref, lead_ref, trail_ref, wide_ref, out_tail_ref,
    act_ref, cond_own_ref, part_ref, half_ref, half_own_ref, sums_ref, mod_own_ref, mod_all_ref, head_src_ref, head_x_ref,
    ring_a_ref, ring_b_ref, pair_src_ref, down_src_ref, down_x_ref,
    tok_send, tok_recv, far_send, far_recv, near_send, near_recv, ring_send, ring_recv,
    head_send, head_recv, local,
):
    rank, count = lax.axis_index("seq"), lax.axis_size("seq")
    row_rank, row_count = lax.axis_index("dp"), lax.axis_size("dp")
    packs = ids_ref.shape[0]
    length, width = tok_ref.shape
    rows = qkv_ref.shape[0]
    slab = heads * size
    low = jnp.bfloat16
    mover = Mover(local)
    qkv_load, out_load = mover.load(qkv_any, qkv_ref), mover.load(out_any, out_ref)
    modw_load = mover.load(modw_any, modw_ref)
    down_load, pair_load = mover.load(down_any, down_ref), mover.load(pair_any, pair_ref)
    tok_loads = [mover.load(tok_any.at[0], tok_ref), mover.load(cot_any.at[0], cot_ref)]
    far, near = far_peers(row_rank, row_count), seq_peers(rank, count)
    act_ref[...] = jnp.zeros_like(act_ref)
    for item in range(items):
        cond = cond_ref[item].astype(jnp.float32)
        act = (cond / (1.0 + jnp.exp(-cond))).astype(low).astype(jnp.float32)
        for pack in range(packs):
            line = items * pack + item
            act_ref[line : line + 1] = act[pack : pack + 1]
    for index in range(row_count):
        cond_own_ref[index] = act_ref[:, index * rows : (index + 1) * rows]
    cond_all_ref[row_rank] = cond_own_ref[row_rank]
    qkv_load.wait()
    for index in range(3):
        head_src_ref[index] = qkv_ref[:, index * slab : (index + 1) * slab].astype(low)
    greet(far + near)

    def head_copy(index, slot, peer):
        return pltpu.make_async_remote_copy(
            src_ref=head_src_ref.at[index], dst_ref=head_x_ref.at[slot],
            send_sem=head_send.at[index], recv_sem=head_recv.at[slot],
            device_id={"seq": peer}, device_id_type=pl.DeviceIdType.MESH,
        )

    moves = []
    for index in range(3):
        peer, slot = (3 * rank + index) % count, (3 * rank + index) // count
        owner = (pow(3, -1, count) * (rank - index + 3 * count)) % count
        moves.append((peer, slot, owner, (3 * owner + index) // count))

        @pl.when(peer != rank)
        def _():
            head_copy(index, slot, peer).start()

        @pl.when(peer == rank)
        def _():
            head_x_ref[slot] = head_src_ref[index]

    conds = []
    for offset, peer in enumerate(far):
        conds.append(
            send(
                cond_own_ref.at[peer["dp"]], cond_all_ref.at[row_rank],
                far_send.at[0, offset], far_recv.at[0, offset], peer,
            )
        )
    hidden_rows = down_ref.shape[1] // count
    groups = pair_ref.shape[1] // (count * hidden_rows)
    down_load.wait()
    down = down_ref[...].T.astype(low)
    pair_load.wait()
    for target in range(count):
        pieces = []
        for group in range(groups):
            start = (group * count + target) * hidden_rows
            pieces.append(pair_ref[:, start : start + hidden_rows])
        pair_src_ref[target] = jnp.concatenate(pieces, axis=1).astype(low)
        down_src_ref[target] = down[target * hidden_rows : (target + 1) * hidden_rows]
    pair_x_ref[rank] = pair_src_ref[rank]
    down_x_ref[rank] = down_src_ref[rank]

    for index, (peer, slot, owner, landed) in enumerate(moves):
        @pl.when(peer != rank)
        def _():
            head_copy(index, slot, peer).wait_send()

        @pl.when(owner != rank)
        def _():
            head_copy(index, landed, owner).wait_recv()

    cut = ring_a_ref.shape[3]
    out_load.wait()
    block = jnp.concatenate(
        [head_x_ref[index] for index in range(3)] + [out_ref[...].astype(low)], axis=1
    )
    ring_a_ref[0, row_rank] = block[:, :cut]
    ring_b_ref[0, row_rank] = block[:, cut:]
    spread = spread_matrix(heads, size)
    main = slab // LANE * LANE

    def use(index):
        whole_block = jnp.concatenate([ring_a_ref[0, index], ring_b_ref[0, index]], axis=1)
        for part in range(3):
            wide_ref[index, :, part * heads * LANE : (part + 1) * heads * LANE] = jnp.dot(
                whole_block[:, part * slab : (part + 1) * slab], spread,
                preferred_element_type=jnp.float32,
            ).astype(low)
        mover.store(wide_ref.at[index], wide_any.at[index])
        out_a_ref[index] = whole_block[:, 3 * slab : 3 * slab + main]
        out_tail_ref[index] = whole_block[:, 3 * slab + main :]

    ring = RingGather([ring_a_ref, ring_b_ref], row_rank, row_count, ring_send, ring_recv, use)
    ring.launch_first()
    for copy in tok_loads:
        copy.wait()
    toks = [CubeGather(tok_ref, tok_all_ref, rank, count, tok_send.at[0], tok_recv.at[0])]
    tok_all_ref[:length] = tok_ref[...]
    cot_all_ref[:length] = cot_ref[...]
    weights = []
    for offset, peer in enumerate(near):
        weights.append(
            send(
                pair_src_ref.at[peer["seq"]], pair_x_ref.at[rank], near_send.at[0, offset],
                near_recv.at[0, offset], peer,
            )
        )
        weights.append(
            send(
                down_src_ref.at[peer["seq"]], down_x_ref.at[rank], near_send.at[1, offset],
                near_recv.at[1, offset], peer,
            )
        )
    toks.append(CubeGather(cot_ref, cot_all_ref, rank, count, tok_send.at[1], tok_recv.at[1]))
    modw_load.wait()
    modw = modw_ref[...].astype(low)
    for copy in conds:
        copy.wait_recv()
    lines = cond_all_ref.shape[1]
    conditions = cond_all_ref[...].reshape(row_count * lines, rows).astype(low)
    products = jnp.dot(conditions, modw, preferred_element_type=jnp.float32)
    part_ref[...] = products.reshape(part_ref.shape)
    side, group = row_rank % 2, row_rank // 2
    paired = send(
        part_ref.at[:, 1 - side], half_ref, far_send.at[1, row_count - 2],
        far_recv.at[1, row_count - 2], {"dp": flip(row_rank, 1)},
    )
    ring.use_first()
    ring.advance()

    order = cube_order(count)
    lane = lax.broadcasted_iota(jnp.int32, (length, LANE), 1)
    quarter = size // 4
    leading = (lane < quarter) | ((lane >= 2 * quarter) & (lane < 3 * quarter))

    def tables(pack):
        for slot in range(count):
            here = slice(slot * length, (slot + 1) * length)
            ids, row, col = token_layout(
                pack, xor(rank, order[slot]), length, lengths_ref, widths_ref
            )
            ids_ref[pack, here] = ids
            angle = jnp.where(lane < 2 * quarter, row, col) * freq_ref[...]
            sine = jnp.where(lane < size, jnp.sin(angle), 0.0)
            cos_ref[pack, here] = jnp.where(lane < size, jnp.cos(angle), 0.0)
            lead_ref[pack, here] = jnp.where(leading, -sine, 0.0)
            trail_ref[pack, here] = jnp.where(leading, 0.0, sine)
        mover.store(cos_ref.at[pack], cos_any.at[pack])
        mover.store(lead_ref.at[pack], lead_any.at[pack])
        mover.store(trail_ref.at[pack], trail_any.at[pack])

    paired.wait_recv()
    half_own_ref[...] = part_ref[:, side] + half_ref[...]
    parts = []
    for offset in range(1, row_count // 2):
        target = (group + offset) % (row_count // 2)
        parts.append(
            send(
                half_own_ref.at[target], sums_ref.at[group], far_send.at[1, offset - 1],
                far_recv.at[1, offset - 1], {"dp": 2 * target + side},
            )
        )
    sums_ref[group] = half_own_ref[group]
    tables(0)
    ring.advance()
    for copy in parts:
        copy.wait_recv()
    total = bias_ref[...].reshape(1, -1) + sums_ref[0]
    for index in range(1, row_count // 2):
        total += sums_ref[index]
    mod_own_ref[...] = total.astype(low).astype(jnp.float32)
    mods = []
    for offset, peer in enumerate(near):
        mods.append(
            send(
                mod_own_ref, mod_all_ref.at[rank], near_send.at[2, offset],
                near_recv.at[2, offset], peer,
            )
        )
    mod_all_ref[rank] = mod_own_ref[...]
    for pack in range(1, packs):
        tables(pack)
    ring.advance()
    for gather in toks:
        gather.advance()
    for copy in mods:
        copy.wait_recv()
    everything = jnp.concatenate([mod_all_ref[index] for index in range(count)], axis=1)
    for which in range(6):
        mod_ref[which] = everything[:, which * width : (which + 1) * width]
    for copy in weights:
        copy.wait_recv()
    down_own_ref[...] = jnp.concatenate([down_x_ref[index] for index in range(count)], axis=1)
    ring.finish()
    for gather, source, target in zip(
        toks, (tok_all_ref, cot_all_ref), (tok_all_any, cot_all_any)
    ):
        gather.finish()
        mover.store(source, target)
    per = LANE // (slab - main)
    for index in range(row_count // per):
        out_b_ref[index] = jnp.concatenate(
            [out_tail_ref[per * index + place] for place in range(per)], axis=1
        )
    for gather in toks:
        gather.settle()
    for copy in conds + [paired] + parts + weights + mods:
        copy.wait_send()
    mover.finish()


def opening(
    lengths, widths, tok, cot, cond, qkv, out, pair, down, modw, bias, lines, heads, size
):
    packs, length, width = tok.shape
    items = lengths.shape[1]
    count, row_count = lax.axis_size("seq"), lax.axis_size("dp")
    total = count * length
    low, full = jnp.bfloat16, jnp.float32
    rows, slab = qkv.shape[0], heads * size
    columns = modw.shape[1]
    hidden_rows = down.shape[1] // count
    chunk = pair.shape[1] // count
    block = 4 * slab
    main = slab // LANE * LANE
    per = LANE // (slab - main)
    cut = -(-block // (2 * LANE)) * LANE
    table = jax.ShapeDtypeStruct((packs, total, LANE), full)
    shapes = [
        jax.ShapeDtypeStruct((total, width), low),
        jax.ShapeDtypeStruct((total, width), low),
        jax.ShapeDtypeStruct((packs, total, 1), jnp.int32),
        table, table, table,
        jax.ShapeDtypeStruct((6, lines, width), full),
        jax.ShapeDtypeStruct((row_count, lines, rows), full),
        jax.ShapeDtypeStruct((row_count, rows, 3 * heads * LANE), low),
        jax.ShapeDtypeStruct((row_count, rows, main), low),
        jax.ShapeDtypeStruct((row_count // per, rows, LANE), low),
        jax.ShapeDtypeStruct((count, rows, chunk), low),
        jax.ShapeDtypeStruct((hidden_rows, count * slab), low),
    ]
    inside = pl.BlockSpec(memory_space=pltpu.VMEM)
    anywhere = pl.BlockSpec(memory_space=pl.ANY)
    scalars = pl.BlockSpec(memory_space=pltpu.SMEM)
    dma = pltpu.SemaphoreType.DMA
    return pl.pallas_call(
        partial(open_kernel, heads, size, items),
        out_shape=shapes,
        in_specs=[scalars] * 2 + [inside] * 3 + [anywhere] * 7,
        out_specs=[anywhere] * 2 + [inside] + [anywhere] * 3 + [inside] * 2 + [anywhere]
        + [inside] * 4,
        scratch_shapes=[
            pltpu.VMEM(qkv.shape, full), pltpu.VMEM(out.shape, full),
            pltpu.VMEM((length, width), low),
            pltpu.VMEM((length, width), low), pltpu.VMEM(pair.shape, full),
            pltpu.VMEM(down.shape, full), pltpu.VMEM(modw.shape, full),
            pltpu.VMEM((total, width), low), pltpu.VMEM((total, width), low),
            pltpu.VMEM((packs, total, LANE), full), pltpu.VMEM((packs, total, LANE), full),
            pltpu.VMEM((packs, total, LANE), full),
            pltpu.VMEM((row_count, rows, 3 * heads * LANE), low),
            pltpu.VMEM((row_count, rows, slab - main), low),
            pltpu.VMEM((lines, width), full),
            pltpu.VMEM((row_count, lines, rows), full),
            pltpu.VMEM((row_count // 2, 2, lines, columns), full),
            pltpu.VMEM((row_count // 2, lines, columns), full),
            pltpu.VMEM((row_count // 2, lines, columns), full),
            pltpu.VMEM((row_count // 2, lines, columns), full),
            pltpu.VMEM((lines, columns), full),
            pltpu.VMEM((count, lines, columns), full),
            pltpu.VMEM((3, rows, slab), low),
            pltpu.VMEM((3, rows, slab), low),
            pltpu.VMEM((1, row_count, rows, cut), low),
            pltpu.VMEM((1, row_count, rows, block - cut), low),
            pltpu.VMEM((count, rows, chunk), low),
            pltpu.VMEM((count, hidden_rows, slab), low),
            pltpu.VMEM((count, hidden_rows, slab), low),
            dma((2, count - 1)), dma((2, count - 1)),
            dma((2, row_count - 1)), dma((2, row_count - 1)),
            dma((3, count - 1)), dma((3, count - 1)),
            dma((2, row_count // 2, 2)), dma((2, row_count // 2, 2)),
            dma((3,)), dma((3,)), dma((9 + row_count + 3 * packs,)),
        ],
        compiler_params=pltpu.CompilerParams(
            collective_id=0, has_side_effects=True, vmem_limit_bytes=62 * 1024 * 1024
        ),
        name="opening",
    )(lengths, widths, cond, bias, frequencies(size), qkv, out, tok, cot, pair, down, modw)


def attend_pack(
    heads, size, items, pack, hook, keep, tok_ref, ids_ref, rows_ref, cos_ref, lead_ref, trail_ref,
    gains_ref, wide_ref, normed_ref, raw_ref, query_ref, key_ref, value_ref, inverse_ref, mixed_a_ref,
    mixed_b_ref, value_t_ref, out_ref,
):
    total, width = tok_ref.shape
    span = heads * LANE
    tile = fit(total, PROJECT_TILE)
    lane = lax.broadcasted_iota(jnp.int32, (tile, LANE), 1)

    def project(index, carry):
        start = pl.multiple_of(index * tile, tile)
        here = pl.ds(start, tile)
        ids = ids_ref[here]
        normal, _ = normalized(tok_ref[here].astype(jnp.float32))
        normed = (
            normal * (1.0 + chosen(ids, rows_ref, 1, pack, items))
            + chosen(ids, rows_ref, 0, pack, items)
        ).astype(jnp.bfloat16)
        normed_ref[here] = normed
        cos, lead, trail = cos_ref[here], lead_ref[here], trail_ref[here]
        query_mark = jnp.where((lane >= size) & (lane < size + 8) & (lane - size != ids), -200.0, 0.0)
        key_mark = jnp.where(lane - size == ids, 1.0, 0.0)
        for part in range(3):
            projected = dot(normed, wide_ref[:, part * span : (part + 1) * span])
            for head in range(heads):
                raw = projected[:, head * LANE : (head + 1) * LANE]
                slot = slice(head * LANE, (head + 1) * LANE)
                if part == 2:
                    value_ref[here, slot] = raw.astype(jnp.bfloat16)
                    continue
                raw_ref[here, part * span + head * LANE : part * span + (head + 1) * LANE] = raw
                square = jnp.sum(raw * raw, axis=-1, keepdims=True) * (1.0 / size)
                unit = raw * lax.rsqrt(square + norm_eps) * gain_row(gains_ref, part, size)
                turned = (
                    unit * cos
                    + pltpu.roll(unit, LANE - size // 4, 1) * lead
                    + pltpu.roll(unit, size // 4, 1) * trail
                )
                if part == 0:
                    turned = turned * (1.0 / math.sqrt(size))
                    query_ref[here, slot] = (turned + query_mark).astype(jnp.bfloat16)
                else:
                    key_ref[here, slot] = (turned + key_mark).astype(jnp.bfloat16)
        return carry

    lax.fori_loop(0, total // tile, project, 0)
    keep()
    hook()
    block = fit(total, SCORE_TILE)
    value_lane = lax.broadcasted_iota(jnp.int32, (total, LANE), 1)
    for head in range(heads):
        slot = slice(head * LANE, (head + 1) * LANE)
        marked = jnp.where(value_lane == size, 1.0, value_ref[:, slot].astype(jnp.float32))
        value_t_ref[...] = marked.T.astype(jnp.bfloat16)

        def score(index, carry):
            here = pl.ds(pl.multiple_of(index * block, block), block)
            weights = jnp.exp(dot_t(key_ref[:, slot], query_ref[here, slot])).astype(jnp.bfloat16)
            mixed = dot(value_t_ref[...], weights)
            inverse = 1.0 / mixed[size : size + 1]
            inverse_ref[head : head + 1, here] = inverse
            out_ref[here, slot] = (mixed * inverse).T.astype(jnp.bfloat16)
            return carry

        lax.fori_loop(0, total // block, score, 0)
        hook()
    spread = spread_matrix(heads, size)

    blocks = mixed_b_ref.shape[0]
    length = total // blocks

    def narrow(index, carry):
        here = pl.ds(pl.multiple_of(index * length, length), length)
        values = dot_t(out_ref[here], spread).astype(jnp.bfloat16)
        mixed_a_ref[here], mixed_b_ref[index] = narrow_parts(values)
        return carry

    lax.fori_loop(0, blocks, narrow, 0)


def attend_kernel(
    heads, size, items, ids_ref, rows_ref, gains_ref, first_any, tok_any, cos_any, lead_any,
    trail_any, wide_any, out_a_any, out_b_any, pair_any, cot_any,
    normed_any, raw_any, query_any, key_any, value_any, inverse_ref,
    mixed_a_any, mixed_b_any, out_full_any, pair_all_any, cot_all_any,
    cos_ref, lead_ref, trail_ref, wide_ref, out_a_ref, out_b_ref, pair_ref,
    normed_ref, raw_ref, query_ref, key_ref, value_ref, mixed_a_ref, mixed_b_ref, out_full_ref,
    pair_all_ref, cot_all_ref,
    tok_ref, tok_own_ref, cot_own_ref,
    value_t_ref, wide_out_ref, own_a_ref, own_b_ref, slots_a_ref, slots_b_ref,
    ring_send, ring_recv, mixed_send, mixed_recv, out_send, out_recv,
    tok_send, tok_recv, cot_send, cot_recv, local,
):
    rank, count = lax.axis_index("seq"), lax.axis_size("seq")
    row_rank, row_count = lax.axis_index("dp"), lax.axis_size("dp")
    packs, total, width = tok_ref.shape
    length = total // count
    order = cube_order(count)
    mover = Mover(local)
    early = [
        mover.load(pair_any, pair_ref), mover.load(out_a_any, out_a_ref),
        mover.load(out_b_any, out_b_ref),
    ]
    for pack in range(1, packs):
        early.append(mover.load(tok_any.at[pack], tok_own_ref.at[pack - 1]))
        early.append(mover.load(cot_any.at[pack], cot_own_ref.at[pack - 1]))
    loads = [[mover.load(first_any, tok_ref.at[0])]] + [[] for _ in range(1, packs)]
    for pack in range(packs):
        for source, target in ((cos_any, cos_ref), (lead_any, lead_ref), (trail_any, trail_ref)):
            loads[pack].append(mover.load(source.at[pack], target.at[pack]))
        if pack == 0:
            wide_load = mover.load(wide_any, wide_ref)
    for copy in early:
        copy.wait()
    greet(ring_peers(row_rank, row_count) + seq_peers(rank, count))
    for lead in range(pair_ref.shape[0]):
        pair_all_ref[lead, row_rank] = pair_ref[lead]
    half = pair_ref.shape[0] // 2
    ring = RingGather(
        [pair_all_ref.at[pl.ds(0, half)], pair_all_ref.at[pl.ds(half, half)]], row_rank, row_count, ring_send, ring_recv
    )
    ring.advance()
    toks = []
    for pack in range(1, packs):
        toks.append(
            CubeGather(
                tok_own_ref.at[pack - 1], tok_ref.at[pack], rank, count, tok_send.at[pack - 1],
                tok_recv.at[pack - 1],
            )
        )
        tok_ref[pack, :length] = tok_own_ref[pack - 1]
        cot_all_ref[pack - 1, :length] = cot_own_ref[pack - 1]
    spreads, cots = [], []
    slots_a_ref[:row_count] = out_a_ref[...]
    slots_b_ref[: out_b_ref.shape[0]] = out_b_ref[...]
    per = row_count // out_b_ref.shape[0]
    rest = LANE // per
    marks = [0]
    turns = packs * (heads + 1)

    def hook():
        marks[0] += 1
        if marks[0] in (turns * 3 // 10, turns * 6 // 10, turns * 9 // 10) and ring.going:
            ring.advance()
        if marks[0] == 3:
            for gather in toks:
                gather.advance()
        if marks[0] == 2:
            spreads.append(
                CubeGather(out_a_ref, slots_a_ref, rank, count, out_send.at[0], out_recv.at[0])
            )
            spreads.append(
                CubeGather(out_b_ref, slots_b_ref, rank, count, out_send.at[1], out_recv.at[1])
            )
        if marks[0] == heads + 2:
            for pack in range(1, packs):
                cots.append(
                    CubeGather(
                        cot_own_ref.at[pack - 1], cot_all_ref.at[pack - 1], rank, count,
                        cot_send.at[pack - 1], cot_recv.at[pack - 1],
                    )
                )
        if marks[0] == turns:
            for gather in spreads:
                gather.advance()

    sends = []
    wide_load.wait()
    for pack in range(packs):
        for copy in loads[pack]:
            copy.wait()
        if pack:
            toks[pack - 1].finish()

        def keep():
            for source, target in (
                (normed_ref, normed_any), (raw_ref, raw_any), (query_ref, query_any),
                (key_ref, key_any), (value_ref, value_any),
            ):
                mover.store(source.at[pack], target.at[pack])

        attend_pack(
            heads, size, items, pack, hook, keep, tok_ref.at[pack], ids_ref.at[pack], rows_ref,
            cos_ref.at[pack], lead_ref.at[pack], trail_ref.at[pack], gains_ref, wide_ref,
            normed_ref.at[pack], raw_ref.at[pack], query_ref.at[pack], key_ref.at[pack],
            value_ref.at[pack], inverse_ref.at[pack], own_a_ref.at[pack], own_b_ref.at[pack],
            value_t_ref, wide_out_ref,
        )
        for slot in range(1, count):
            where = {"seq": xor(rank, order[slot])}
            sends.append(
                send(
                    own_a_ref.at[pack, pl.ds(slot * length, length)], mixed_a_ref.at[pack, rank],
                    mixed_send.at[0, pack, slot - 1], mixed_recv.at[0, pack, slot - 1], where,
                )
            )
            sends.append(
                send(
                    own_b_ref.at[pack, slot], mixed_b_ref.at[pack, rank],
                    mixed_send.at[1, pack, slot - 1], mixed_recv.at[1, pack, slot - 1], where,
                )
            )
        mixed_a_ref[pack, rank] = own_a_ref[pack, :length]
        mixed_b_ref[pack, rank] = own_b_ref[pack, 0]
    ring.finish()
    chunk = pair_ref.shape[2]
    for lead in range(pair_ref.shape[0]):
        mover.store(pair_all_ref.at[lead], pair_all_any.at[:, :, pl.ds(lead * chunk, chunk)])
    for gather in spreads:
        gather.finish()
    for gather in cots:
        gather.advance()
    for index in range(row_count):
        place = slice((index % per) * rest, (index % per + 1) * rest)
        pieces = []
        for owner in range(count):
            slot = cube_slot(xor(rank, owner), count)
            pieces.append(slots_a_ref[slot * row_count + index])
            pieces.append(slots_b_ref[slot * (row_count // per) + index // per][:, place])
        out_full_ref[index] = jnp.concatenate(pieces, axis=1)
    mover.store(out_full_ref, out_full_any)
    for gather in cots:
        gather.finish()
    mover.store(cot_all_ref, cot_all_any)
    for copy in sends:
        copy.wait_recv()
    mover.store(mixed_a_ref, mixed_a_any)
    mover.store(mixed_b_ref, mixed_b_any)
    for gather in spreads + toks + cots:
        gather.settle()
    for copy in sends:
        copy.wait_send()
    mover.finish()


def attend(first, tok, ids, rows, turns, gains, wide, out_a, out_b, pair, cot, items, heads, size):
    packs, length, width = tok.shape
    count, row_count = lax.axis_size("seq"), lax.axis_size("dp")
    total = first.shape[0]
    span, slab = heads * LANE, heads * size
    my_rows, main = out_a.shape[1:]
    per = row_count // out_b.shape[0]
    later = max(packs - 1, 1)
    low, full = jnp.bfloat16, jnp.float32
    shapes = [
        jax.ShapeDtypeStruct((packs, total, width), low),
        jax.ShapeDtypeStruct((packs, total, 2 * span), full),
        jax.ShapeDtypeStruct((packs, total, span), low),
        jax.ShapeDtypeStruct((packs, total, span), low),
        jax.ShapeDtypeStruct((packs, total, span), low),
        jax.ShapeDtypeStruct((packs, heads, total), full),
        jax.ShapeDtypeStruct((packs, count, length, main), low),
        jax.ShapeDtypeStruct((packs, count, length // per, LANE), low),
        jax.ShapeDtypeStruct((row_count, my_rows, count * slab), low),
        jax.ShapeDtypeStruct((row_count, my_rows, pair.shape[0] * pair.shape[2]), low),
        jax.ShapeDtypeStruct((later, total, width), low),
    ]
    staged = [pltpu.VMEM(shape.shape, shape.dtype) for index, shape in enumerate(shapes) if index != 5]
    staged[8] = pltpu.VMEM((pair.shape[0], row_count) + pair.shape[1:], low)
    inside = pl.BlockSpec(memory_space=pltpu.VMEM)
    anywhere = pl.BlockSpec(memory_space=pl.ANY)
    dma = pltpu.SemaphoreType.DMA
    direct = [*turns, wide, out_a, out_b, pair]
    return pl.pallas_call(
        partial(attend_kernel, heads, size, items),
        out_shape=shapes,
        in_specs=[inside] * 3 + [anywhere] * 10,
        out_specs=[anywhere] * 5 + [inside] + [anywhere] * 5,
        scratch_shapes=[pltpu.VMEM(entry.shape, entry.dtype) for entry in direct]
        + staged
        + [
            pltpu.VMEM((packs, total, width), low), pltpu.VMEM((later, length, width), low),
            pltpu.VMEM((later, length, width), low),
            pltpu.VMEM((LANE, total), low), pltpu.VMEM((total, span), low),
            pltpu.VMEM((packs, total, main), low),
            pltpu.VMEM((packs, count, length // per, LANE), low),
            pltpu.VMEM((count * row_count, my_rows, main), low),
            pltpu.VMEM((count * row_count // per, my_rows, LANE), low),
            dma((2, row_count // 2, 2)), dma((2, row_count // 2, 2)),
            dma((2, packs, count - 1)), dma((2, packs, count - 1)),
            dma((2, count - 1)), dma((2, count - 1)),
            dma((later, count - 1)), dma((later, count - 1)),
            dma((later, count - 1)), dma((later, count - 1)),
            dma((13 + 10 * packs,)),
        ],
        compiler_params=pltpu.CompilerParams(
            collective_id=1, has_side_effects=True, vmem_limit_bytes=62 * 1024 * 1024
        ),
        name="attend",
    )(ids, rows, gains, first, tok, *turns, wide, out_a, out_b, pair, cot)


def middle_kernel(
    items, ids_ref, rows_ref, down_ref, mixed_a_any, mixed_b_any, tok_any, own_cot_any, out_any,
    pair_any, cot_any, cot_later_any,
    middle_any, branch_own_ref, branch_move_ref, grad_a_any, grad_b_any, grad_middle_ref, part_ref, pair_grad_any, down_sum_ref,
    out_grad_any,
    mixed_a_ref, mixed_b_ref, tok_ref, own_cot_ref, out_ref, pair_ref, branch_in_ref,
    grad_a_ref, grad_b_ref, pair_grad_ref, out_grad_ref,
    down_a_ref, down_b_ref, own_ref, attended_ref, middle_ref, normed_ref, hidden_ref, gated_ref,
    partial_ref, landed_ref, total_ref, branch_ref, branch_landed_ref,
    gmix_a_ref, gmix_b_ref, coming_ref, down_grad_ref, down_total_ref,
    down_land_ref,
    ring_send, ring_recv, norm_send, norm_recv, grad_send, grad_recv, branch_send, branch_recv,
    mix_send, mix_recv, back_send, back_recv, local,
):
    rank, count = lax.axis_index("seq"), lax.axis_size("seq")
    row_rank, row_count = lax.axis_index("dp"), lax.axis_size("dp")
    packs, total, width = branch_in_ref.shape
    length = total // count
    slab = width // count
    chunk = pair_ref.shape[1] // count
    cut = down_a_ref.shape[3]
    hidden = row_count * down_ref.shape[0]
    order = cube_order(count)
    low, full = jnp.bfloat16, jnp.float32
    mover = Mover(local)
    first = [
        mover.load(mixed_a_any, mixed_a_ref), mover.load(mixed_b_any, mixed_b_ref),
        mover.load(out_any, out_ref), mover.load(tok_any, tok_ref),
    ]
    cot_loads = [
        mover.load(cot_later_any.at[pack - 1] if pack else cot_any, branch_in_ref.at[pack])
        for pack in range(packs)
    ]
    own_load, pair_load = mover.load(own_cot_any, own_cot_ref), mover.load(pair_any, pair_ref)
    greet(ring_peers(row_rank, row_count) + seq_peers(rank, count))
    down_a_ref[0, row_rank] = down_ref[:, :cut]
    down_b_ref[0, row_rank] = down_ref[:, cut:]
    ring = RingGather([down_a_ref, down_b_ref], row_rank, row_count, ring_send, ring_recv)
    ring.advance()
    part_ref[...] = jnp.zeros_like(part_ref)

    def own_ids(pack):
        return ids_ref[pack, :length]

    def pick(pack, which):
        return chosen(own_ids(pack), rows_ref, which, pack, items)

    def by_item(pack, which, values):
        for item in range(items):
            line = items * pack + item
            part_ref[which - 2, line : line + 1] = jnp.sum(
                jnp.where(own_ids(pack) == item, values, 0.0), axis=0, keepdims=True
            )

    gathers = []

    def start_gather(pack):
        gathers.append(
            CubeGather(
                coming_ref.at[pack], normed_ref.at[pack], rank, count, norm_send.at[pack],
                norm_recv.at[pack],
            )
        )

    for copy in first:
        copy.wait()
    for pack in range(packs):
        own = jnp.concatenate(
            [join_parts(mixed_a_ref[pack, index], mixed_b_ref[pack, index]) for index in range(count)],
            axis=1,
        )
        own_ref[pack] = own
        attended = dot(own, out_ref[...])
        attended_ref[pack] = attended.astype(low)
        middle = tok_ref[pack].astype(full) + pick(pack, 2) * attended
        middle_ref[pack] = middle
        mover.store(middle_ref.at[pack], middle_any.at[pack])
        normal, _ = normalized(middle)
        coming_ref[pack] = (normal * (1.0 + pick(pack, 4)) + pick(pack, 3)).astype(low)
        normed_ref[pack, :length] = coming_ref[pack]
        if pack == 0:
            start_gather(0)
        ring.advance()
    tile = fit(total, 2 * length)

    def scale_cotangent(pack):
        def step(index, carry):
            here = pl.ds(pl.multiple_of(index * length, length), length)
            gate = chosen(ids_ref[pack, here], rows_ref, 5, pack, items)
            branch_in_ref[pack, here] = (branch_in_ref[pack, here].astype(full) * gate).astype(low)
            return carry

        lax.fori_loop(0, count, step, 0)

    own_load.wait()
    gathers[0].advance()
    for pack in range(1, packs):
        start_gather(pack)
    cot_loads[0].wait()
    scale_cotangent(0)
    ring.advance()
    pair_load.wait()

    def down_part(which):
        ref = (down_a_ref, down_b_ref)[which]
        return ref[0].reshape(hidden, ref.shape[3])

    def forward(pack, start):
        here = pl.ds(start, tile)
        both = dot(normed_ref[pack, here], pair_ref[...])
        gate, up = both[:, :hidden], both[:, hidden:]
        hidden_ref[pack, here] = (gate / (1.0 + jnp.exp(-gate)) * up).astype(low)
        gated_ref[pack, here] = both.astype(low)

    def backward(pack, start):
        here = pl.ds(start, tile)
        coming = branch_in_ref[pack, here]
        grad = dot_t(coming[:, :cut], down_part(0)) + dot_t(coming[:, cut:], down_part(1))
        gate = gated_ref[pack, here, :hidden].astype(full)
        up = gated_ref[pack, here, hidden:].astype(full)
        sigmoid = 1.0 / (1.0 + jnp.exp(-gate))
        grad_gate = grad * up * sigmoid * (1.0 + gate * (1.0 - sigmoid))
        gated_ref[pack, here, :hidden] = grad_gate.astype(low)
        gated_ref[pack, here, hidden:] = (grad * gate * sigmoid).astype(low)
        partial_ref[pack, here] = dot_t(gated_ref[pack, here], pair_ref[...]).astype(low)

    reduces, branches = [], []
    for pack in range(packs):
        gathers[pack].finish()
        forward(pack, 0)
        forward(pack, total // 2)
        if pack == 0:
            for later in range(1, packs):
                cot_loads[later].wait()
                scale_cotangent(later)
            ring.finish()
        reduces.append(
            CubeReduce(
                partial_ref.at[pack], landed_ref.at[pack], total_ref.at[pack], rank, count,
                grad_send.at[pack], grad_recv.at[pack],
            )
        )
        backward(pack, total // 2)
        reduces[pack].near()
        backward(pack, 0)
        reduces[pack].across()

    def branch_part(pack, start):
        here = pl.ds(start, tile)
        values = hidden_ref[pack, here]
        branch_ref[here, :cut] = dot(values, down_part(0)).astype(low)
        branch_ref[here, cut:] = dot(values, down_part(1)).astype(low)

    def middle_back(pack):
        normal, inverse = normalized(middle_ref[pack])
        grad_normed = reduces[pack].result()
        grad_middle = own_cot_ref[pack].astype(full) + normalized_back(
            normal, inverse, grad_normed * (1.0 + pick(pack, 4))
        )
        grad_middle_ref[pack] = grad_middle
        by_item(pack, 2, grad_middle * attended_ref[pack].astype(full))
        by_item(pack, 3, grad_normed)
        by_item(pack, 4, grad_normed * normal)
        grad_attended = (grad_middle * pick(pack, 2)).astype(low)
        coming_ref[pack] = grad_attended
        grad_mixed = dot_t(grad_attended, out_ref[...]).astype(low)
        for index in range(count):
            gmix_a_ref[pack, index], gmix_b_ref[pack, index] = narrow_parts(
                grad_mixed[:, index * slab : (index + 1) * slab]
            )
        copies = []
        for slot in range(1, count):
            peer = xor(rank, order[slot])
            copies.append(
                send(
                    gmix_a_ref.at[pack, peer], grad_a_ref.at[pack, slot],
                    mix_send.at[0, pack, slot - 1], mix_recv.at[0, pack, slot - 1], {"seq": peer},
                )
            )
            copies.append(
                send(
                    gmix_b_ref.at[pack, peer], grad_b_ref.at[pack, slot],
                    mix_send.at[1, pack, slot - 1], mix_recv.at[1, pack, slot - 1], {"seq": peer},
                )
            )
        grad_a_ref[pack, 0], grad_b_ref[pack, 0] = (
            gmix_a_ref[pack, rank], gmix_b_ref[pack, rank]
        )
        return copies

    def branch_start(pack):
        branch_part(pack, total // 2)
        branches.append(
            send(
                branch_ref.at[pl.ds(total // 2, total // 2)], branch_landed_ref.at[pack],
                branch_send.at[pack], branch_recv.at[pack], {"seq": flip(rank, 1)},
            )
        )
        branch_part(pack, 0)

    def branch_finish(pack):
        branches[pack].wait_recv()
        own, move = slice(0, length), slice(length, 2 * length)
        branch_own_ref[pack] = (
            branch_ref[own].astype(full) + branch_landed_ref[pack, own].astype(full)
        )
        branch_move_ref[pack] = (
            branch_ref[move].astype(full) + branch_landed_ref[pack, move].astype(full)
        ).astype(low)
        branches[pack].wait_send()

    strip = fit(width, 384)
    hidden_rows = down_ref.shape[0]
    back = RingReduce(
        [down_grad_ref], [down_sum_ref], [down_total_ref], [down_land_ref], row_rank, row_count,
        back_send, back_recv,
    )

    def down_grads():
        for start in range(0, hidden, chunk):
            grad = sum(
                dot(hidden_ref[pack, :, start : start + chunk].T, branch_in_ref[pack])
                for pack in range(packs)
            ).astype(low)
            first_block = start // hidden_rows
            down_grad_ref[0, first_block : first_block + chunk // hidden_rows] = grad.reshape(
                chunk // hidden_rows, hidden_rows, width
            )

    def pair_grads(start):
        grad = sum(
            dot(normed_ref[pack, :, start : start + strip].T, gated_ref[pack]) for pack in range(packs)
        )
        here = pl.ds(start, strip)
        pair_grad_ref[here] = grad.astype(low)
        for index in range(count):
            mover.store(
                pair_grad_ref.at[here, pl.ds(index * chunk, chunk)], pair_grad_any.at[index, here]
            )

    mixes = []
    branch_start(0)
    for pack in range(packs):
        gathers[pack].settle()
    down_grads()
    back.advance()
    strips = list(range(0, width, strip))
    pair_grads(strips[0])
    back.advance()
    for pack in range(packs):
        mixes += middle_back(pack)
    for pack in range(1, packs):
        branch_finish(pack - 1)
        branch_start(pack)
    back.advance()
    for start in strips[1:]:
        pair_grads(start)
    back.advance()
    for start in range(0, width, strip):
        left = [own_ref[pack, :, start : start + strip].T for pack in range(packs)]
        grad = sum(dot(left[pack], coming_ref[pack]) for pack in range(packs)).astype(low)
        for index in range(count):
            out_grad_ref[index] = grad[:, index * slab : (index + 1) * slab]
        mover.load(out_grad_ref, out_grad_any.at[:, pl.ds(start, strip)]).wait()
    branch_finish(packs - 1)
    for copy in mixes:
        copy.wait_recv()
    mover.store(grad_a_ref, grad_a_any)
    mover.store(grad_b_ref, grad_b_any)
    back.finish()
    mover.finish()
    for group in reduces:
        group.settle()
    for copy in mixes:
        copy.wait_send()


def middle(
    mixed_a, mixed_b, tok, ids, rows, own_cot, cot, cot_later, out, pair, down, items
):
    packs, length, width = tok.shape
    count, row_count = lax.axis_size("seq"), lax.axis_size("dp")
    total, slab = count * length, width // count
    hidden_rows = down.shape[0]
    hidden = row_count * hidden_rows
    low, full = jnp.bfloat16, jnp.float32
    lines = rows.shape[1]
    cut = -(-width // (2 * LANE)) * LANE
    half = total // 2
    steps = row_count // 2
    shapes = [
        jax.ShapeDtypeStruct((packs, length, width), full),
        jax.ShapeDtypeStruct((packs, length, width), full),
        jax.ShapeDtypeStruct((packs, length, width), low),
        jax.ShapeDtypeStruct(mixed_a.shape, low),
        jax.ShapeDtypeStruct(mixed_b.shape, low),
        jax.ShapeDtypeStruct((packs, length, width), full),
        jax.ShapeDtypeStruct((3, lines, width), full),
        jax.ShapeDtypeStruct((count, width, 2 * hidden // count), low),
        jax.ShapeDtypeStruct((1, hidden_rows, width), full),
        jax.ShapeDtypeStruct((count, width, slab), low),
    ]
    inside = pl.BlockSpec(memory_space=pltpu.VMEM)
    anywhere = pl.BlockSpec(memory_space=pl.ANY)
    dma = pltpu.SemaphoreType.DMA
    inputs = [mixed_a, mixed_b, tok, own_cot, out, pair]
    strip = jax.ShapeDtypeStruct((count, fit(width, 384), slab), low)
    every = jax.ShapeDtypeStruct((packs, total, width), low)
    staged = [every, shapes[3], shapes[4], pair, strip]
    return pl.pallas_call(
        partial(middle_kernel, items),
        out_shape=shapes,
        in_specs=[inside] * 3 + [anywhere] * 8,
        out_specs=[anywhere] + [inside] * 2 + [anywhere] * 2 + [inside] * 2
        + [anywhere, inside, anywhere],
        scratch_shapes=[pltpu.VMEM(entry.shape, entry.dtype) for entry in inputs + staged]
        + [
            pltpu.VMEM((1, row_count, hidden_rows, cut), low),
            pltpu.VMEM((1, row_count, hidden_rows, width - cut), low),
            pltpu.VMEM((packs, length, width), low),
            pltpu.VMEM((packs, length, width), low),
            pltpu.VMEM((packs, length, width), full),
            pltpu.VMEM((packs, total, width), low),
            pltpu.VMEM((packs, total, hidden), low),
            pltpu.VMEM((packs, total, 2 * hidden), low),
            pltpu.VMEM((packs, total, width), low),
            pltpu.VMEM((packs, half + length, width), low),
            pltpu.VMEM((packs, length, width), low),
            pltpu.VMEM((total, width), low),
            pltpu.VMEM((packs, half, width), low),
            pltpu.VMEM(mixed_a.shape, low),
            pltpu.VMEM(mixed_b.shape, low),
            pltpu.VMEM((packs, length, width), low),
            pltpu.VMEM((1, row_count, hidden_rows, width), low),
            pltpu.VMEM((2, steps - 1, 1, hidden_rows, width), low),
            pltpu.VMEM((2, steps, 1, hidden_rows, width), low),
            dma((2, steps, 2)), dma((2, steps, 2)),
            dma((packs, count - 1)), dma((packs, count - 1)),
            dma((packs, 2)), dma((packs, 2)), dma((packs,)), dma((packs,)),
            dma((2, packs, count - 1)), dma((2, packs, count - 1)),
            dma((2, steps, 1)), dma((2, steps, 1)),
            dma((24 + 2 * packs,)),
        ],
        compiler_params=pltpu.CompilerParams(
            collective_id=2, has_side_effects=True, vmem_limit_bytes=62 * 1024 * 1024
        ),
        name="middle",
    )(ids, rows, down, *inputs, cot, cot_later)


def attend_back_pack(
    heads, size, hook, enter, ready, mixed_a_ref, mixed_b_ref, raw_ref, query_ref, key_ref, value_ref, inverse_ref,
    cos_ref, lead_ref, trail_ref, gains_ref, wide_ref,
    grad_ref, normed_ref, gain_ref,
    wide_mixed_ref, key_t_ref, dq_ref, dk_ref, dv_ref,
):
    blocks, length = mixed_a_ref.shape[:2]
    total = blocks * length
    span = heads * LANE
    tile = fit(total, BACK_TILE)
    block = fit(total, BACK_SCORE_TILE)
    spread = spread_matrix(heads, size)

    def widen(index, carry):
        here = pl.ds(pl.multiple_of(index * length, length), length)
        values = join_parts(mixed_a_ref[index], mixed_b_ref[index])
        wide_mixed_ref[here] = dot(values, spread).astype(jnp.bfloat16)
        return carry

    lax.fori_loop(0, blocks, widen, 0)
    for head in range(heads):
        slot = slice(head * LANE, (head + 1) * LANE)
        key_t_ref[...] = key_ref[:, slot].astype(jnp.float32).T.astype(jnp.bfloat16)
        dk_ref[...] = jnp.zeros_like(dk_ref)
        dv_ref[...] = jnp.zeros_like(dv_ref)

        def score(index, carry):
            start = pl.multiple_of(index * block, block)
            here = pl.ds(start, block)
            query, coming = query_ref[here, slot], wide_mixed_ref[here, slot]
            scores = lax.dot_general(
                key_ref[:, slot], query, (((1,), (1,)), ((), ())),
                preferred_element_type=jnp.float32,
            )
            probs = jnp.exp(scores) * inverse_ref[head : head + 1, here]
            grad_probs = lax.dot_general(
                value_ref[:, slot], coming, (((1,), (1,)), ((), ())),
                preferred_element_type=jnp.float32,
            )
            inner = jnp.sum(probs * grad_probs, axis=0, keepdims=True)
            grad_scores = (probs * (grad_probs - inner)).astype(jnp.bfloat16)
            dv_ref[...] += jnp.dot(
                probs.astype(jnp.bfloat16), coming, preferred_element_type=jnp.float32
            )
            dk_ref[...] += jnp.dot(grad_scores, query, preferred_element_type=jnp.float32)
            dq_ref[here] = jnp.dot(
                key_t_ref[...], grad_scores, preferred_element_type=jnp.float32
            ).T
            return carry

        lax.fori_loop(0, total // block, score, 0)

        def unturn(index, carry):
            here = pl.ds(pl.multiple_of(index * tile, tile), tile)
            cos, lead, trail = cos_ref[here], lead_ref[here], trail_ref[here]
            for part, source in ((0, dq_ref), (1, dk_ref)):
                coming = source[here]
                if part == 0:
                    coming = coming * (1.0 / math.sqrt(size))
                coming = (
                    coming * cos
                    - pltpu.roll(coming, LANE - size // 4, 1) * lead
                    - pltpu.roll(coming, size // 4, 1) * trail
                )
                start = part * span + head * LANE
                raw = raw_ref[here, start : start + LANE]
                square = jnp.sum(raw * raw, axis=-1, keepdims=True) * (1.0 / size)
                inverse = lax.rsqrt(square + norm_eps)
                unit = raw * inverse
                scaled = coming * gain_row(gains_ref, part, size)
                slope = jnp.sum(scaled * unit, axis=-1, keepdims=True) * (1.0 / size)
                grad_ref[here, start : start + LANE] = (
                    inverse * (scaled - unit * slope)
                ).astype(jnp.bfloat16)
                gain_ref[part : part + 1] += jnp.sum(coming * unit, axis=0, keepdims=True)
            start = 2 * span + head * LANE
            grad_ref[here, start : start + LANE] = dv_ref[here].astype(jnp.bfloat16)
            return carry

        if head == 0:
            enter()
        lax.fori_loop(0, total // tile, unturn, 0)
        hook()

    ready()

    def project(index, carry):
        here = pl.ds(pl.multiple_of(index * tile, tile), tile)
        normed_ref[here] = lax.dot_general(
            grad_ref[here], wide_ref[...], (((1,), (1,)), ((), ())),
            preferred_element_type=jnp.float32,
        ).astype(jnp.bfloat16)
        return carry

    lax.fori_loop(0, total // tile, project, 0)


def attend_back_kernel(
    heads, size, items, inverse_ref, gains_ref, ids_ref, rows_ref, branch_own_any, branch_move_any,
    middle_any, cot_any, mixed_a_any, mixed_b_any, query_any, key_any, value_any,
    raw_any, cos_any, lead_any, trail_any, wide_any, pair_any, out_any,
    grad_any, normed_any, gain_ref, reduced_ref, pair_sum_ref, out_sum_ref, layer_ref, gate_ref,
    branch_own_ref, branch_move_ref, middle_ref, cot_ref, mixed_a_ref, mixed_b_ref, query_ref, key_ref, value_ref, raw_ref, cos_ref, lead_ref, trail_ref,
    wide_ref, pair_ref, out_ref, grad_ref, normed_ref,
    wide_mixed_ref, key_t_ref, dq_ref, dk_ref, dv_ref,
    pair_total_ref, out_total_ref, pair_land_ref, out_land_ref,
    out_near_ref, out_move_a_ref, out_move_b_ref, out_far_a_ref, out_far_b_ref, out_own_ref, landed_ref, total_ref, branch_far_ref,
    ring_send, ring_recv, late_send, late_recv, out_send, out_recv, part_send, part_recv,
    branch_send, branch_recv, local,
):
    rank, count = lax.axis_index("seq"), lax.axis_size("seq")
    row_rank, row_count = lax.axis_index("dp"), lax.axis_size("dp")
    packs = mixed_a_ref.shape[0]
    mover = Mover(local)
    pair_load, out_load = mover.load(pair_any, pair_ref), mover.load(out_any, out_ref)
    move_load = mover.load(branch_move_any, branch_move_ref)
    loads = []
    for pack in range(packs):
        loads.append(
            [
                mover.load(source.at[pack], target.at[pack])
                for source, target in (
                    (mixed_a_any, mixed_a_ref), (mixed_b_any, mixed_b_ref),
                    (query_any, query_ref), (key_any, key_ref), (value_any, value_ref),
                    (cos_any, cos_ref), (lead_any, lead_ref),
                    (trail_any, trail_ref),
                )
            ]
        )
        if pack == 0:
            raw_loads = [mover.load(raw_any.at[0], raw_ref)]
            wide_load = mover.load(wide_any, wide_ref)
    late_loads = [
        mover.load(branch_own_any, branch_own_ref), mover.load(middle_any, middle_ref),
        mover.load(cot_any, cot_ref),
    ]
    pair_load.wait()
    out_load.wait()
    move_load.wait()
    greet(ring_peers(row_rank, row_count) + seq_peers(rank, count))
    half = pair_ref.shape[0] // 2
    sides = [pl.ds(0, half), pl.ds(half, half)]
    ring = RingReduce(
        [pair_ref.at[side] for side in sides], [pair_sum_ref.at[side] for side in sides],
        [pair_total_ref.at[:, :, side] for side in sides],
        [pair_land_ref.at[:, :, side] for side in sides], row_rank, row_count, ring_send, ring_recv,
    )
    ring.advance()
    mate, across = flip(rank, 1), flip(rank, 2)
    near = [
        send(
            out_ref.at[flip(mate, 2) if index else mate], out_near_ref.at[index],
            out_send.at[index], out_recv.at[index], {"seq": mate},
        )
        for index in range(2)
    ]
    late = RingReduce(
        [out_own_ref], [out_sum_ref], [out_total_ref], [out_land_ref], row_rank, row_count,
        late_send, late_recv,
    )
    marks, moved, reduces, branches = [0], [], [], []
    turns = packs * heads
    length, width = middle_ref.shape[1:]

    def send_branch(pack):
        branches.append(
            send(
                branch_move_ref.at[pack], branch_far_ref.at[pack], branch_send.at[pack],
                branch_recv.at[pack], {"seq": across},
            )
        )

    def finish_layer(pack):
        branches[pack].wait_recv()
        ids = ids_ref[pack, :length]
        branch = branch_own_ref[pack] + branch_far_ref[pack].astype(jnp.float32)
        layer_ref[pack] = (
            middle_ref[pack] + chosen(ids, rows_ref, 5, pack, items) * branch
        ).astype(jnp.bfloat16)
        values = cot_ref[pack].astype(jnp.float32) * branch
        for item in range(items):
            line = items * pack + item
            gate_ref[line : line + 1] = jnp.sum(
                jnp.where(ids == item, values, 0.0), axis=0, keepdims=True
            )


    def hook():
        marks[0] += 1
        if marks[0] == 1:
            near[1].wait_recv()
            out_move_a_ref[...], out_move_b_ref[...] = narrow_parts(
                (
                    out_ref[across].astype(jnp.float32) + out_near_ref[1].astype(jnp.float32)
                ).astype(jnp.bfloat16)
            )
            moved.append(
                send(out_move_a_ref, out_far_a_ref, out_send.at[2], out_recv.at[2], {"seq": across})
            )
            moved.append(
                send(out_move_b_ref, out_far_b_ref, out_send.at[3], out_recv.at[3], {"seq": across})
            )
        if marks[0] == turns // 2:
            for pack in range(packs):
                send_branch(pack)
        if marks[0] % heads == 1 and marks[0] > heads:
            reduces[-1].across()
        if marks[0] == turns // 2:
            near[0].wait_recv()
            for copy in moved:
                copy.wait_recv()
            own = (
                out_ref[rank].astype(jnp.float32)
                + out_near_ref[0].astype(jnp.float32)
                + join_parts(out_far_a_ref[...], out_far_b_ref[...]).astype(jnp.float32)
            )
            out_own_ref[0] = own.astype(jnp.bfloat16).reshape(out_own_ref.shape[1:])
            late.advance()
        elif marks[0] > turns // 2 and late.going:
            late.advance()
        if marks[0] % 2 == 0 and ring.going:
            ring.advance()

    gain_ref[...] = jnp.zeros_like(gain_ref)
    gate_ref[...] = jnp.zeros_like(gate_ref)
    grad_stores = []
    for pack in range(packs):
        for copy in loads[pack]:
            copy.wait()

        def enter():
            raw_loads[pack].wait()
            for copy in grad_stores[pack - 1 : pack]:
                copy.wait()

        def ready():
            grad_stores.append(mover.load(grad_ref, grad_any.at[pack]))
            if pack == 0:
                wide_load.wait()
            if pack < packs - 1:
                raw_loads.append(mover.load(raw_any.at[pack + 1], raw_ref))

        attend_back_pack(
            heads, size, hook, enter, ready, mixed_a_ref.at[pack], mixed_b_ref.at[pack],
            raw_ref, query_ref.at[pack], key_ref.at[pack], value_ref.at[pack],
            inverse_ref.at[pack], cos_ref.at[pack], lead_ref.at[pack], trail_ref.at[pack],
            gains_ref, wide_ref, grad_ref, normed_ref.at[pack], gain_ref,
            wide_mixed_ref, key_t_ref, dq_ref, dk_ref, dv_ref,
        )
        if pack < packs - 1:
            reduces.append(
                CubeReduce(
                    normed_ref.at[pack], landed_ref.at[pack], total_ref.at[pack], rank, count,
                    part_send.at[pack], part_recv.at[pack],
                )
            )
            reduces[pack].near()
    mover.store(normed_ref.at[packs - 1], normed_any)
    for copy in late_loads:
        copy.wait()
    for pack in range(packs):
        finish_layer(pack)
    for pack, reduce in enumerate(reduces):
        reduced_ref[pack] = reduce.result()
    ring.finish()
    late.finish()
    for copy in near + moved + branches:
        copy.wait_send()
    for reduce in reduces:
        reduce.settle()
    grad_stores[-1].wait()
    mover.finish()


def attend_back(
    mixed_a, mixed_b, saved, turns, gains, wide, pair, out, ids, rows_all, branch_own, branch_move,
    middle_all, cot, items, heads, size,
):
    packs, count, length = mixed_a.shape[:3]
    total = count * length
    row_count = lax.axis_size("dp")
    steps = row_count // 2
    span, slab = heads * LANE, heads * size
    width = wide.shape[0]
    rows = width // row_count
    main = slab // LANE * LANE
    per = LANE // (slab - main)
    low, full = jnp.bfloat16, jnp.float32
    raw, query, key, value, inverse = saved
    pair_block, out_block = (pair.shape[0],) + pair.shape[2:], (1, rows, slab)
    inside = pl.BlockSpec(memory_space=pltpu.VMEM)
    anywhere = pl.BlockSpec(memory_space=pl.ANY)
    dma = pltpu.SemaphoreType.DMA
    inputs = [
        branch_own, branch_move, middle_all, cot, mixed_a, mixed_b, query, key, value, raw, *turns,
        wide, pair, out,
    ]
    staged = [pltpu.VMEM(entry.shape, entry.dtype) for entry in inputs]
    staged[9] = pltpu.VMEM(raw.shape[1:], full)
    return pl.pallas_call(
        partial(attend_back_kernel, heads, size, items),
        out_shape=[
            jax.ShapeDtypeStruct((packs, total, 3 * span), low),
            jax.ShapeDtypeStruct((total, width), low),
            jax.ShapeDtypeStruct((2, LANE), full),
            jax.ShapeDtypeStruct((max(packs - 1, 1), length, width), full),
            jax.ShapeDtypeStruct(pair_block, full),
            jax.ShapeDtypeStruct(out_block, full),
            jax.ShapeDtypeStruct((packs, length, width), low),
            jax.ShapeDtypeStruct(rows_all.shape[1:], full),
        ],
        in_specs=[inside] * 4 + [anywhere] * 16,
        out_specs=[anywhere] * 2 + [inside] * 6,
        scratch_shapes=staged
        + [
            pltpu.VMEM((total, 3 * span), low),
            pltpu.VMEM((packs, total, width), low),
            pltpu.VMEM((total, span), low),
            pltpu.VMEM((LANE, total), low),
            pltpu.VMEM((total, LANE), full),
            pltpu.VMEM((total, LANE), full),
            pltpu.VMEM((total, LANE), full),
            pltpu.VMEM((2, steps - 1) + pair_block, low),
            pltpu.VMEM((2, steps - 1) + out_block, low),
            pltpu.VMEM((2, steps) + pair_block, low),
            pltpu.VMEM((2, steps) + out_block, low),
            pltpu.VMEM((2, width, slab), low),
            pltpu.VMEM((width, main), low), pltpu.VMEM((width // per, LANE), low),
            pltpu.VMEM((width, main), low), pltpu.VMEM((width // per, LANE), low),
            pltpu.VMEM((1, row_count, rows, slab), low),
            pltpu.VMEM((max(packs - 1, 1), total // 2 + length, width), low),
            pltpu.VMEM((max(packs - 1, 1), length, width), low),
            pltpu.VMEM((packs, length, width), low),
            dma((2, steps, 2)), dma((2, steps, 2)), dma((2, steps, 1)), dma((2, steps, 1)),
            dma((4,)), dma((4,)), dma((max(packs - 1, 1), 2)), dma((max(packs - 1, 1), 2)),
            dma((packs,)), dma((packs,)), dma((8 + 10 * packs,)),
        ],
        compiler_params=pltpu.CompilerParams(
            collective_id=3, has_side_effects=True, vmem_limit_bytes=62 * 1024 * 1024
        ),
        name="attend_back",
    )(inverse, gains, ids, rows_all, *inputs)


def closing_kernel(
    heads, size, items, ids_ref, rows_ref, mods_ref, gate_ref, cond_ref, gain_ref, pair_ref, down_ref, out_ref,
    reduced_ref, part_any, normed_any, wide_any, tok_any, middle_any,
    tokens_ref, qkv_sum_ref, gateup_sum_ref, down_sum_ref, mod_sum_ref, bias_sum_ref,
    gain_sum_ref, square_ref,
    part_ref, normed_ref, wide_ref, tok_ref, middle_ref,
    landed_ref, total_ref, grad_a_ref, grad_b_ref, sum_a_ref, sum_b_ref, tot_a_ref, tot_b_ref,
    land_a_ref, land_b_ref, head_src_ref, head_x_ref, pair_src_ref, pair_x_ref, down_src_ref, down_x_ref,
    first_ref, mod_src_ref, mod_x_ref, mod_own_ref, mod_all_ref, norm_own_ref, norm_x_ref,
    norm_mid_ref, norm_all_ref,
    part_send, part_recv, ring_send, ring_recv, head_send, head_recv, near_send, near_recv,
    far_send, far_recv, local,
):
    rank, count = lax.axis_index("seq"), lax.axis_size("seq")
    row_rank, row_count = lax.axis_index("dp"), lax.axis_size("dp")
    packs, total, width = normed_ref.shape
    length = total // count
    slab = heads * size
    span = heads * LANE
    rows = width // row_count
    low, full = jnp.bfloat16, jnp.float32
    mover = Mover(local)
    part_load = mover.load(part_any, part_ref)
    strip_loads = [mover.load(normed_any, normed_ref), mover.load(wide_any, wide_ref)]
    token_loads = [mover.load(tok_any, tok_ref), mover.load(middle_any, middle_ref)]
    far, near = far_peers(row_rank, row_count), seq_peers(rank, count)
    part_load.wait()
    greet(far + near)

    def exchange(kind, source, target):
        return [
            send(
                source(peer["seq"]), target.at[rank], near_send.at[kind, offset],
                near_recv.at[kind, offset], peer,
            )
            for offset, peer in enumerate(near)
        ]

    reduce = CubeReduce(
        part_ref, landed_ref, total_ref, rank, count, part_send.at[0], part_recv.at[0]
    )
    reduce.near()
    for copy in strip_loads:
        copy.wait()
    strip = 2 * rows
    cut = grad_a_ref.shape[3]
    for index in range(width // strip):
        start = index * strip
        left = [normed_ref[pack, :, start : start + strip].T for pack in range(packs)]
        pieces = []
        for part in range(3):
            grad = sum(
                dot(left[pack], wide_ref[pack, :, part * span : (part + 1) * span])
                for pack in range(packs)
            ).astype(low)
            pieces += [grad[:, head * LANE : head * LANE + size] for head in range(heads)]
        grad = jnp.concatenate(pieces, axis=1)
        for side in range(2):
            here = slice(side * rows, (side + 1) * rows)
            grad_a_ref[0, 2 * index + side] = grad[here, :cut]
            grad_b_ref[0, 2 * index + side] = grad[here, cut:]
        if index == 0:
            reduce.across()
    ring = RingReduce(
        [grad_a_ref, grad_b_ref], [sum_a_ref, sum_b_ref], [tot_a_ref, tot_b_ref],
        [land_a_ref, land_b_ref], row_rank, row_count, ring_send, ring_recv,
    )
    ring.advance()
    for copy in token_loads:
        copy.wait()
    pair_src_ref[...] = pair_ref[...].astype(low)
    for index in range(count):
        down_src_ref[index] = down_ref[0, :, index * slab : (index + 1) * slab].astype(low)

    first_ref[...] = jnp.zeros_like(first_ref)
    for pack in range(packs):
        ids = ids_ref[pack, :length]
        normal, inverse = normalized(tok_ref[pack].astype(full))
        grad_normed = reduced_ref[pack] if pack < packs - 1 else reduce.result()
        scale = chosen(ids, rows_ref, 1, pack, items)
        tokens_ref[pack] = (
            middle_ref[pack] + normalized_back(normal, inverse, grad_normed * (1.0 + scale))
        ).astype(low)
        for which, values in enumerate((grad_normed, grad_normed * normal)):
            for item in range(items):
                line = items * pack + item
                first_ref[which, line : line + 1] = jnp.sum(
                    jnp.where(ids == item, values, 0.0), axis=0, keepdims=True
                )
    used = items * packs
    columns = mod_src_ref.shape[2]
    full_rows = jnp.concatenate(
        [first_ref[0], first_ref[1]] + [mods_ref[index] for index in range(3)] + [gate_ref[...]],
        axis=1,
    )
    for index in range(count):
        mod_src_ref[index] = full_rows[:, index * columns : (index + 1) * columns]
        mod_src_ref[index, used : used + 2, :LANE] = gain_ref[...]
    mod_near = exchange(2, lambda peer: mod_src_ref.at[peer], mod_x_ref)
    mod_x_ref[rank] = mod_src_ref[rank]
    copies = exchange(0, lambda peer: pair_src_ref.at[peer], pair_x_ref)
    pair_x_ref[rank] = pair_src_ref[rank]
    copies += exchange(1, lambda peer: down_src_ref.at[peer], down_x_ref)
    down_x_ref[rank] = down_src_ref[rank]
    ring.advance()
    for copy in mod_near:
        copy.wait_recv()
    mod_sums = sum(mod_x_ref[index] for index in range(count))
    halfway = mod_own_ref.shape[1]
    mod_own_ref[...] = jnp.concatenate(
        [mod_sums[:, :halfway], mod_sums[:, halfway:]], axis=0
    ).astype(low)
    mod_far = [
        send(
            mod_own_ref, mod_all_ref.at[row_rank], far_send.at[0, offset], far_recv.at[0, offset],
            peer,
        )
        for offset, peer in enumerate(far)
    ]
    mod_all_ref[row_rank] = mod_own_ref[...]
    ring.advance()
    for copy in mod_far:
        copy.wait_recv()
    lines = mod_all_ref.shape[1] // 2
    every = [
        jnp.concatenate([mod_all_ref[index, :lines], mod_all_ref[index, lines:]], axis=1)
        for index in range(row_count)
    ]
    conditions = cond_ref[...].reshape(row_count * lines, rows).astype(low)
    mod_sum = t_dot(conditions, jnp.concatenate(every, axis=0))
    mod_sum_ref[...] = mod_sum
    square = jnp.sum(mod_sum * mod_sum)
    gains, bias = 0.0, 0.0
    for entry in every:
        gains += entry[used : used + 2, :LANE].astype(full)
        bias += jnp.sum(entry[:used].astype(full), axis=0, keepdims=True)
    gain_sum_ref[...] = gains
    bias_sum_ref[...] = bias.reshape(-1)
    square += jnp.sum(bias * bias) * (1.0 / row_count)
    ring.advance()
    for copy in copies:
        copy.wait_recv()
    hidden_rows = down_src_ref.shape[1]
    groups = pair_ref.shape[2] // hidden_rows
    pieces = []
    for group in range(groups):
        for index in range(count):
            pieces.append(pair_x_ref[index, :, group * hidden_rows : (group + 1) * hidden_rows])
    gateup = jnp.concatenate(pieces, axis=1).astype(full)
    gateup_sum_ref[...] = gateup
    square += jnp.sum(gateup * gateup)
    down_rows = []
    for index in range(count):
        block = down_x_ref[index].astype(full)
        down_rows.append(block)
        square += jnp.sum(block * block)
    down_sum_ref[...] = jnp.concatenate(down_rows, axis=0).T
    square += jnp.sum(out_ref[...] * out_ref[...])
    ring.finish()
    summed = jnp.concatenate([sum_a_ref[0], sum_b_ref[0]], axis=1)
    square += jnp.sum(summed * summed)
    norm_own_ref[...] = jnp.full(norm_own_ref.shape, square, full)
    norm_near = exchange(3, lambda peer: norm_own_ref, norm_x_ref)
    norm_x_ref[rank] = norm_own_ref[...]
    for slot in range(3):
        head_src_ref[slot] = summed[:, slot * slab : (slot + 1) * slab]

    def head_copy(slot, index, peer):
        return pltpu.make_async_remote_copy(
            src_ref=head_src_ref.at[slot], dst_ref=head_x_ref.at[index],
            send_sem=head_send.at[slot], recv_sem=head_recv.at[index],
            device_id={"seq": peer}, device_id_type=pl.DeviceIdType.MESH,
        )

    moves = []
    for slot in range(3):
        peer, index = (slot * count + rank) // 3, (slot * count + rank) % 3
        moves.append((peer, index))

        @pl.when(peer != rank)
        def _():
            head_copy(slot, index, peer).start()

        @pl.when(peer == rank)
        def _():
            head_x_ref[index] = head_src_ref[slot]

    for copy in norm_near:
        copy.wait_recv()
    norm_mid_ref[...] = sum(norm_x_ref[index] for index in range(count))
    norm_far = [
        send(
            norm_mid_ref, norm_all_ref.at[row_rank], far_send.at[1, offset],
            far_recv.at[1, offset], peer,
        )
        for offset, peer in enumerate(far)
    ]
    norm_all_ref[row_rank] = norm_mid_ref[...]
    for index in range(3):
        source = (3 * rank + index) % count

        @pl.when(source != rank)
        def _():
            head_copy(index, index, source).wait_recv()

    qkv_sum_ref[...] = jnp.concatenate([head_x_ref[index] for index in range(3)], axis=1)
    for copy in norm_far:
        copy.wait_recv()
    squares = sum(norm_all_ref[index] for index in range(row_count))
    square_ref[...] = squares + jnp.sum(gains * gains)
    for slot, (peer, index) in enumerate(moves):
        @pl.when(peer != rank)
        def _():
            head_copy(slot, index, peer).wait_send()

    reduce.settle()
    for copy in copies + mod_near + mod_far + norm_near + norm_far:
        copy.wait_send()


def closing(
    normed, wide, part, reduced, tok, ids, rows, middle_grad, mods, gate, cond, gain, pair, down,
    out, items, heads, size,
):
    packs, total, width = normed.shape
    count, row_count = lax.axis_size("seq"), lax.axis_size("dp")
    length, slab = total // count, heads * size
    my_rows = width // row_count
    steps = row_count // 2
    low, full = jnp.bfloat16, jnp.float32
    lines = rows.shape[1]
    columns = 6 * width // count
    hidden_rows = down.shape[1]
    cut = -(-3 * slab // (2 * LANE)) * LANE
    sides = [(1, my_rows, cut), (1, my_rows, 3 * slab - cut)]
    shapes = [
        jax.ShapeDtypeStruct((packs, length, width), low),
        jax.ShapeDtypeStruct((my_rows, 3 * slab), full),
        jax.ShapeDtypeStruct((my_rows, pair.shape[0] * pair.shape[2]), full),
        jax.ShapeDtypeStruct((slab, count * hidden_rows), full),
        jax.ShapeDtypeStruct((my_rows, columns), full),
        jax.ShapeDtypeStruct((columns,), full),
        jax.ShapeDtypeStruct((2, LANE), full),
        jax.ShapeDtypeStruct((8, LANE), full),
    ]
    inside = pl.BlockSpec(memory_space=pltpu.VMEM)
    anywhere = pl.BlockSpec(memory_space=pl.ANY)
    dma = pltpu.SemaphoreType.DMA
    inputs = [part, normed, wide, tok, middle_grad]
    return pl.pallas_call(
        partial(closing_kernel, heads, size, items),
        out_shape=shapes,
        in_specs=[inside] * 10 + [anywhere] * 5,
        out_specs=[inside] * len(shapes),
        scratch_shapes=[pltpu.VMEM(entry.shape, entry.dtype) for entry in inputs]
        + [
            pltpu.VMEM((total // 2 + length, width), low),
            pltpu.VMEM((length, width), low),
        ]
        + [pltpu.VMEM((1, row_count) + side[1:], low) for side in sides]
        + [pltpu.VMEM(side, full) for side in sides]
        + [pltpu.VMEM((2, steps - 1) + side, low) for side in sides]
        + [pltpu.VMEM((2, steps) + side, low) for side in sides]
        + [
            pltpu.VMEM((3, my_rows, slab), full),
            pltpu.VMEM((3, my_rows, slab), full),
            pltpu.VMEM(pair.shape, low),
            pltpu.VMEM(pair.shape, low),
            pltpu.VMEM((count, hidden_rows, slab), low),
            pltpu.VMEM((count, hidden_rows, slab), low),
            pltpu.VMEM((2, lines, width), full),
            pltpu.VMEM((count, lines, columns), full),
            pltpu.VMEM((count, lines, columns), full),
            pltpu.VMEM((2 * lines, columns // 2), low),
            pltpu.VMEM((row_count, 2 * lines, columns // 2), low),
            pltpu.VMEM((8, LANE), full),
            pltpu.VMEM((count, 8, LANE), full),
            pltpu.VMEM((8, LANE), full),
            pltpu.VMEM((row_count, 8, LANE), full),
            dma((1, 2)), dma((1, 2)),
            dma((2, steps, 2)), dma((2, steps, 2)),
            dma((3,)), dma((3,)), dma((4, count - 1)), dma((4, count - 1)),
            dma((2, row_count - 1)), dma((2, row_count - 1)), dma((5,)),
        ],
        compiler_params=pltpu.CompilerParams(
            collective_id=4, has_side_effects=True, vmem_limit_bytes=62 * 1024 * 1024
        ),
        name="closing",
    )(ids, rows, mods, gate, cond, gain, pair, down, out, reduced, *inputs)


def adam_kernel(many, square_ref, *refs):
    grads_any, refs = refs[:many], refs[many:]
    olds_any, refs = refs[: 3 * many], refs[3 * many :]
    passed_any, refs = refs[:2], refs[2:]
    news_any, refs = refs[: 3 * many], refs[3 * many :]
    handed_any, norm_ref, refs = refs[:2], refs[2], refs[3:]
    grads, refs = refs[:many], refs[many:]
    values, refs = refs[: 3 * many], refs[3 * many :]
    held, local = refs[:2], refs[2]
    mover = Mover(local)
    loads = []
    for index in range(many):
        loads.append([mover.load(grads_any[index], grads[index])])
        for part in range(3 * index, 3 * index + 3):
            loads[index].append(mover.load(olds_any[part], values[part]))
    passing = [mover.load(source, target) for source, target in zip(passed_any, held)]
    norm = jnp.sqrt(square_ref[0:1, 0:1])
    norm_ref[0, 0] = jnp.sum(norm)
    factor = clip_limit / jnp.maximum(norm, clip_limit)
    for index in range(many):
        for copy in loads[index]:
            copy.wait()
        mine = values[3 * index : 3 * index + 3]
        if len(mine[0].shape) == 1:
            flat = [entry[...].reshape(1, -1) for entry in mine]
            updated = adam_update(*flat, grads[index][...].reshape(1, -1), factor)
            for part, value in enumerate(updated):
                mine[part][...] = value.reshape(-1)
                mover.store(mine[part], news_any[3 * index + part])
            continue
        rows, columns = mine[0].shape
        tile = 16 if rows % 16 == 0 else rows

        def step(place, carry):
            here = pl.ds(pl.multiple_of(place * tile, tile), tile)
            updated = adam_update(*(entry[here] for entry in mine), grads[index][here, :columns], factor)
            for target, value in zip(mine, updated):
                target[here] = value
            return carry

        lax.fori_loop(0, rows // tile, step, 0)
        for part in range(3):
            mover.store(mine[part], news_any[3 * index + part])
    for copy, source, target in zip(passing, held, handed_any):
        copy.wait()
        mover.store(source, target)
    mover.finish()


def adam(square, grads, olds, passed):
    many = len(grads)
    inside = pl.BlockSpec(memory_space=pltpu.VMEM)
    anywhere = pl.BlockSpec(memory_space=pl.ANY)
    flat = [entry for old in olds for entry in old]
    shape = lambda entry: jax.ShapeDtypeStruct(entry.shape, entry.dtype)
    results = pl.pallas_call(
        partial(adam_kernel, many),
        out_shape=[shape(entry) for entry in flat + passed]
        + [jax.ShapeDtypeStruct((1, 1), jnp.float32)],
        in_specs=[inside] + [anywhere] * (4 * many + 2),
        out_specs=[anywhere] * (3 * many + 2) + [pl.BlockSpec(memory_space=pltpu.SMEM)],
        scratch_shapes=[pltpu.VMEM(entry.shape, entry.dtype) for entry in grads + flat + passed]
        + [pltpu.SemaphoreType.DMA((7 * many + 4,))],
        compiler_params=pltpu.CompilerParams(vmem_limit_bytes=62 * 1024 * 1024),
        name="adam",
    )(square, *grads, *flat, *passed)
    return list(results[: 3 * many]), results[3 * many : 3 * many + 2], results[-1]


def on_device(
    tokens,
    cotangent,
    condition,
    item_lengths,
    item_widths,
    qkv_weight,
    qkv_first,
    qkv_second,
    out_weight,
    out_first,
    out_second,
    gateup_weight,
    gateup_first,
    gateup_second,
    down_weight,
    down_first,
    down_second,
    mod_weight,
    mod_first,
    mod_second,
    mod_bias,
    bias_first,
    bias_second,
    qk_gains,
    gains_first,
    gains_second,
):
    packs, length, width = tokens.shape
    items = condition.shape[1]
    size = width // HEADS
    count, row_count = lax.axis_size("seq"), lax.axis_size("dp")
    heads = HEADS // count
    rows = qkv_weight.shape[0]

    lines = -(-(packs * items + 2) // 8) * 8
    (
        tok_first, cot_first, ids, cos, lead, trail, mod_rows, cond_rows, wide, out_a, out_b, pair_own,
        down_own,
    ) = opening(
        item_lengths, item_widths, tokens, cotangent, jnp.swapaxes(condition, 0, 1), qkv_weight,
        out_weight, gateup_weight, down_weight.T, mod_weight, mod_bias, lines, heads, size,
    )
    turns = (cos, lead, trail)
    wide = wide.reshape(width, wide.shape[2])
    (
        normed, raw, query, key, value, inverse, mixed_a, mixed_b, out_full, pair_all, cot_later,
    ) = attend(
        tok_first, tokens, ids, mod_rows, turns, qk_gains, wide, out_a, out_b, pair_own, cotangent, items,
        heads, size,
    )
    (
        middle_all, branch_own, branch_move, grad_a, grad_b, grad_middle, mod_part, pair_grad,
        down_sum, out_grad,
    ) = middle(
        mixed_a, mixed_b, tokens, ids, mod_rows, cotangent, cot_first, cot_later,
        out_full.reshape(width, width), pair_all.reshape(width, -1), down_own, items,
    )
    grad_wide, grad_part, gain_part, reduced, pair_sum, out_sum, layer_out, gate_part = attend_back(
        grad_a, grad_b, (raw, query, key, value, inverse), turns, qk_gains, wide,
        pair_grad.reshape(count, row_count, rows, -1), out_grad, ids, mod_rows, branch_own,
        branch_move, middle_all, cotangent, items, heads, size,
    )
    tokens_grad, qkv_sum, gateup_sum, down_sum, mod_sum, bias_sum, gain_sum, square = closing(
        normed, grad_wide, grad_part, reduced, tokens, ids, mod_rows, grad_middle, mod_part,
        gate_part, cond_rows, gain_part, pair_sum, down_sum, out_sum, items, heads, size,
    )
    news, outs, norm = adam(
        square, [qkv_sum, out_sum[0], gateup_sum, down_sum, mod_sum, bias_sum, gain_sum],
        [
            (qkv_weight, qkv_first, qkv_second), (out_weight, out_first, out_second),
            (gateup_weight, gateup_first, gateup_second),
            (down_weight.T, down_first.T, down_second.T), (mod_weight, mod_first, mod_second),
            (mod_bias, bias_first, bias_second),
            (qk_gains, gains_first, gains_second),
        ],
        [layer_out, tokens_grad],
    )
    news[9:12] = [entry.T for entry in news[9:12]]
    return tuple(list(outs) + [norm.reshape(())] + list(news))


def solution(mesh):
    return jax.shard_map(
        on_device,
        mesh=mesh,
        in_specs=(
            P("dp", "seq", None),
            P("dp", "seq", None),
            P("dp", None, None),
            P("dp", None),
            P("dp", None),
            P("dp", "seq"),
            P("dp", "seq"),
            P("dp", "seq"),
            P("dp", "seq"),
            P("dp", "seq"),
            P("dp", "seq"),
            P("dp", "seq"),
            P("dp", "seq"),
            P("dp", "seq"),
            P("dp", "seq"),
            P("dp", "seq"),
            P("dp", "seq"),
            P("dp", "seq"),
            P("dp", "seq"),
            P("dp", "seq"),
            P("seq"),
            P("seq"),
            P("seq"),
            P(),
            P(),
            P(),
        ),
        out_specs=(
            P("dp", "seq", None),
            P("dp", "seq", None),
            P(),
            P("dp", "seq"),
            P("dp", "seq"),
            P("dp", "seq"),
            P("dp", "seq"),
            P("dp", "seq"),
            P("dp", "seq"),
            P("dp", "seq"),
            P("dp", "seq"),
            P("dp", "seq"),
            P("dp", "seq"),
            P("dp", "seq"),
            P("dp", "seq"),
            P("dp", "seq"),
            P("dp", "seq"),
            P("dp", "seq"),
            P("seq"),
            P("seq"),
            P("seq"),
            P(),
            P(),
            P(),
        ),
        check_vma=False,
    )
```

```python
from functools import partial
import math

import jax
import jax.numpy as jnp
import numpy as np
from jax import lax
from jax.experimental import pallas as pl
from jax.experimental.pallas import tpu as pltpu
from jax.sharding import PartitionSpec as P

HEADS = 16
OPT_STEP = 10


norm_eps = 1e-06
clip_limit = 1.0
beta_one = 0.9
beta_two = 0.95
adam_eps = 1e-08
learn_rate = 0.06
decay_rate = 0.01


def adam_update(master, moment, square, gradient, factor):
    clipped = gradient * factor
    moment_new = beta_one * moment + (1.0 - beta_one) * clipped
    square_new = beta_two * square + (1.0 - beta_two) * clipped * clipped
    moment_hat = moment_new * (1.0 / (1.0 - beta_one**OPT_STEP))
    square_hat = square_new * (1.0 / (1.0 - beta_two**OPT_STEP))
    master_new = master - learn_rate * (
        moment_hat / (jnp.sqrt(square_hat) + adam_eps) + decay_rate * master
    )
    return (master_new, moment_new, square_new)


LANE = 128
PROJECT_TILE = 384
SCORE_TILE = 768
BACK_TILE = 384
BACK_SCORE_TILE = 768


def fit(total, wanted):
    size = min(total, wanted)
    while total % size:
        size -= 8
    return size


def spread_matrix(heads, size):
    row = lax.broadcasted_iota(jnp.int32, (heads * size, heads * LANE), 0)
    column = lax.broadcasted_iota(jnp.int32, (heads * size, heads * LANE), 1)
    hit = row < 0
    for head in range(heads):
        inside = (column >= head * LANE) & (column < head * LANE + size)
        hit = hit | (inside & (row - column == head * (size - LANE)))
    return jnp.where(hit, 1.0, 0.0).astype(jnp.bfloat16)


def cube_slot(offset, count):
    bits = count.bit_length() - 1
    return sum(((offset // 2**bit) % 2) * 2 ** (bits - 1 - bit) for bit in range(bits))


def chosen(ids, rows_ref, which, pack, items):
    first = items * pack
    choice = rows_ref[which, first + items - 1 : first + items]
    for item in range(items - 2, -1, -1):
        choice = jnp.where(ids == item, rows_ref[which, first + item : first + item + 1], choice)
    return choice


def dot(left, right):
    return jnp.dot(left, right, preferred_element_type=jnp.float32)


def dot_t(left, right):
    return lax.dot_general(left, right, (((1,), (1,)), ((), ())), preferred_element_type=jnp.float32)


def t_dot(left, right):
    return lax.dot_general(left, right, (((0,), (0,)), ((), ())), preferred_element_type=jnp.float32)


def normalized(values):
    centered = values - jnp.mean(values, axis=-1, keepdims=True)
    inverse = lax.rsqrt(jnp.mean(centered * centered, axis=-1, keepdims=True) + norm_eps)
    return centered * inverse, inverse


def normalized_back(normal, inverse, incoming):
    return inverse * (
        incoming
        - jnp.mean(incoming, axis=-1, keepdims=True)
        - normal * jnp.mean(incoming * normal, axis=-1, keepdims=True)
    )


def gain_row(gains_ref, part, size):
    return jnp.concatenate(
        [1.0 + gains_ref[part : part + 1], jnp.zeros((1, LANE - size), jnp.float32)], axis=1
    )


def flip(rank, step):
    return rank + step - 2 * step * ((rank // step) % 2)


def xor(rank, offset):
    step = 1
    while step <= offset:
        if offset & step:
            rank = flip(rank, step)
        step *= 2
    return rank


def cube_order(count):
    order, step = [0], count // 2
    while step:
        order = order + [place ^ step for place in order]
        step //= 2
    return order


def ring_place(rank, count):
    side = rank % 2
    return (rank // 2) * (1 - 2 * side) + (count - 1) * side


def ring_rank(place, count):
    place = (place + count) % count
    side = place // (count // 2)
    return 2 * place * (1 - side) + (2 * (count - 1 - place) + 1) * side


def send(source, target, send_sem, recv_sem, where):
    copy = pltpu.make_async_remote_copy(
        src_ref=source, dst_ref=target, send_sem=send_sem, recv_sem=recv_sem,
        device_id=where, device_id_type=pl.DeviceIdType.MESH,
    )
    copy.start()
    return copy


def greet(targets):
    barrier = pltpu.get_barrier_semaphore()
    for target in targets:
        pl.semaphore_signal(
            barrier, inc=1, device_id=target, device_id_type=pl.DeviceIdType.MESH
        )
    pl.semaphore_wait(barrier, len(targets))


def seq_peers(rank, count):
    return [{"seq": xor(rank, offset)} for offset in range(1, count)]


def far_peers(rank, count):
    return [{"dp": (rank + offset) % count} for offset in range(1, count)]


def ring_peers(rank, count):
    place = ring_place(rank, count)
    return [{"dp": ring_rank(place + 1, count)}, {"dp": ring_rank(place - 1, count)}]


def far_part(index, lead, way):
    if lead == 1:
        return (0, 1) if index % 2 == way else (0, 0)
    cut = (lead + 1) // 2
    return (cut, lead) if way else (0, cut)


class RingGather:
    def __init__(self, buffers, rank, count, send_sems, recv_sems, use=None):
        self.buffers, self.count, self.use = buffers, count, use
        self.place = ring_place(rank, count)
        self.send_sems, self.recv_sems = send_sems, recv_sems
        self.steps = count // 2
        self.sent, self.going = [], []
        self.step = 0

    def launch_first(self):
        self.advance_links()

    def use_first(self):
        self.use(ring_rank(self.place, self.count))

    def advance_links(self):
        step = self.step
        if step > self.steps:
            return
        self.step += 1
        arriving, self.going = self.going, []
        for index in range(len(self.buffers)):
            for place, copy in arriving:
                if place == index:
                    copy.wait_recv()
                    self.sent.append(copy)
            if step < self.steps:
                self.launch(step, index)

    def advance(self):
        step = self.step
        self.advance_links()
        if self.use is not None and step <= self.steps:
            self.use(ring_rank(self.place - step, self.count))
            if 0 < step < self.steps:
                self.use(ring_rank(self.place + step, self.count))

    def launch(self, step, index):
        buffer = self.buffers[index]
        for way in range(2):
            sign = 1 - 2 * way
            block = ring_rank(self.place - sign * step, self.count)
            where = {"dp": ring_rank(self.place + sign, self.count)}
            low, high = 0, buffer.shape[0]
            if step == self.steps - 1:
                low, high = far_part(index, high, way)
                if low == high:
                    continue
            view = buffer.at[pl.ds(low, high - low), block]
            copy = send(
                view, view, self.send_sems.at[way, step, index],
                self.recv_sems.at[way, step, index], where,
            )
            self.going.append((index, copy))

    def finish(self):
        while self.step <= self.steps:
            self.advance()
        for copy in self.sent:
            copy.wait_send()


class RingReduce:
    def __init__(self, sources, results, totals, landed, rank, count, send_sems, recv_sems):
        self.sources, self.results, self.totals, self.landed = sources, results, totals, landed
        self.count, self.steps = count, count // 2
        self.place = ring_place(rank, count)
        self.send_sems, self.recv_sems = send_sems, recv_sems
        self.sent, self.going = [], []
        self.step = 0

    def advance(self):
        step = self.step
        if step > self.steps:
            return
        self.step += 1
        arriving, self.going = self.going, []
        for index in range(len(self.sources)):
            for place, copy in arriving:
                if place == index:
                    copy.wait_recv()
                    self.sent.append(copy)
            if step < self.steps:
                self.launch(step, index)
            else:
                self.total(step, index)

    def total(self, step, index):
        source = self.sources[index]
        mine = ring_rank(self.place, self.count)
        for lead in range(source.shape[0]):
            total = source[lead, mine].astype(jnp.float32)
            for way in range(2):
                total += self.landed[index][way, step - 1, lead].astype(jnp.float32)
            self.results[index][lead] = total

    def launch(self, step, index):
        source = self.sources[index]
        size = source.shape[0]
        for way in range(2):
            sign = 1 - 2 * way
            block = ring_rank(self.place + sign * (self.steps - step), self.count)
            where = {"dp": ring_rank(self.place + sign, self.count)}
            low, high = far_part(index, size, way)
            if step == 0:
                if low == high:
                    continue
                view = source.at[pl.ds(low, high - low), block]
                target = self.landed[index].at[way, step, pl.ds(low, high - low)]
            else:
                for lead in range(size):
                    total = source[lead, block]
                    if step > 1 or low <= lead < high:
                        total = (
                            total.astype(jnp.float32)
                            + self.landed[index][way, step - 1, lead].astype(jnp.float32)
                        ).astype(total.dtype)
                    self.totals[index][way, step - 1, lead] = total
                view = self.totals[index].at[way, step - 1]
                target = self.landed[index].at[way, step]
            copy = send(
                view, target, self.send_sems.at[way, step, index],
                self.recv_sems.at[way, step, index], where,
            )
            self.going.append((index, copy))

    def finish(self):
        while self.step <= self.steps:
            self.advance()
        for copy in self.sent:
            copy.wait_send()


class CubeGather:
    def __init__(self, source, target, rank, count, send_sems, recv_sems):
        self.source, self.target, self.rank = source, target, rank
        self.length = source.shape[0]
        self.send_sems, self.recv_sems = send_sems, recv_sems
        self.steps = [count >> (level + 1) for level in range(count.bit_length() - 1)]
        self.copies = {}
        self.level = 0
        for level in range(len(self.steps)):
            self.launch(0, level)

    def launch(self, slot, level):
        landing = slot + 2**level
        view = self.source
        if slot:
            view = self.target.at[pl.ds(slot * self.length, self.length)]
        self.copies[slot, level] = send(
            view, self.target.at[pl.ds(landing * self.length, self.length)],
            self.send_sems.at[landing - 1], self.recv_sems.at[landing - 1],
            {"seq": flip(self.rank, self.steps[level])},
        )

    def advance(self):
        level = self.level
        if level >= len(self.steps):
            return
        self.level += 1
        for slot in range(2**level):
            self.copies[slot, level].wait_recv()
        for later in range(level + 1, len(self.steps)):
            for slot in range(2**level, 2 ** (level + 1)):
                self.launch(slot, later)

    def finish(self):
        while self.level < len(self.steps):
            self.advance()

    def settle(self):
        for copy in self.copies.values():
            copy.wait_send()


class CubeReduce:
    def __init__(self, parts, landed, total, rank, count, send_sems, recv_sems):
        self.parts, self.landed, self.total, self.rank = parts, landed, total, rank
        self.length = parts.shape[0] // count
        self.half = parts.shape[0] // 2
        self.send_sems, self.recv_sems = send_sems, recv_sems
        self.copies = []

    def near(self):
        view = self.parts.at[pl.ds(self.half, self.half)]
        self.copies.append(
            send(
                view, self.landed.at[pl.ds(0, self.half)], self.send_sems.at[0],
                self.recv_sems.at[0], {"seq": flip(self.rank, 1)},
            )
        )

    def across(self):
        self.copies[0].wait_recv()
        here = pl.ds(self.length, self.length)
        self.total[...] = (
            self.parts[here].astype(jnp.float32) + self.landed[here].astype(jnp.float32)
        ).astype(self.total.dtype)
        self.copies.append(
            send(
                self.total, self.landed.at[pl.ds(self.half, self.length)], self.send_sems.at[1],
                self.recv_sems.at[1], {"seq": flip(self.rank, 2)},
            )
        )

    def result(self):
        self.copies[1].wait_recv()
        own = pl.ds(0, self.length)
        return (
            self.parts[own].astype(jnp.float32)
            + self.landed[own].astype(jnp.float32)
            + self.landed[pl.ds(self.half, self.length)].astype(jnp.float32)
        )

    def settle(self):
        for copy in self.copies:
            copy.wait_send()


class Mover:
    def __init__(self, sems):
        self.sems, self.used, self.stores = sems, 0, []

    def load(self, source, target):
        copy = pltpu.make_async_copy(source, target, self.sems.at[self.used])
        self.used += 1
        copy.start()
        return copy

    def store(self, source, target):
        self.stores.append(self.load(source, target))

    def finish(self):
        for copy in self.stores:
            copy.wait()


def narrow_parts(values):
    slab = values.shape[1]
    cut = slab // LANE * LANE
    per = LANE // (slab - cut)
    step = values.shape[0] // per
    tail = [values[index * step : (index + 1) * step, cut:] for index in range(per)]
    return values[:, :cut], jnp.concatenate(tail, axis=1)


def join_parts(wide, packed):
    per = wide.shape[0] // packed.shape[0]
    rest = LANE // per
    tail = [packed[:, index * rest : (index + 1) * rest] for index in range(per)]
    return jnp.concatenate([wide, jnp.concatenate(tail, axis=0)], axis=1)


def token_layout(pack, slot_rank, length, lengths_ref, widths_ref):
    items = lengths_ref.shape[1]
    place = lax.broadcasted_iota(jnp.int32, (length, 1), 0) + slot_rank * length
    ids = jnp.zeros_like(place)
    start = jnp.zeros_like(place)
    width = jnp.zeros_like(place) + widths_ref[pack, 0]
    end = 0
    for item in range(1, items):
        end = end + lengths_ref[pack, item - 1]
        inside = place >= end
        ids = jnp.where(inside, item, ids)
        start = jnp.where(inside, end, start)
        width = jnp.where(inside, widths_ref[pack, item], width)
    offset = (place - start).astype(jnp.float32)
    width = width.astype(jnp.float32)
    row = jnp.floor((offset + 0.5) / width)
    return ids, row, offset - row * width


def frequencies(size):
    quarter = size // 4
    lane = np.arange(LANE)
    table = np.where(lane < size, 10000.0 ** (-(lane % quarter) / quarter), 0.0)
    return table.astype(np.float32)[None]


def open_kernel(
    heads, size, items,
    lengths_ref, widths_ref, cond_ref, bias_ref, freq_ref, qkv_any, out_any, tok_any, cot_any, pair_any,
    down_any, modw_any,
    tok_all_any, cot_all_any, ids_ref, cos_any, lead_any, trail_any, mod_ref, cond_all_ref,
    wide_any, out_a_ref, out_b_ref, pair_x_ref, down_own_ref,
    qkv_ref, out_ref, tok_ref, cot_ref, pair_ref, down_ref, modw_ref,
    tok_all_ref, cot_all_ref, cos_ref, lead_ref, trail_ref, wide_ref, out_tail_ref,
    act_ref, cond_own_ref, part_ref, half_ref, half_own_ref, sums_ref, mod_own_ref, mod_all_ref, head_src_ref, head_x_ref,
    ring_a_ref, ring_b_ref, pair_src_ref, down_src_ref, down_x_ref,
    tok_send, tok_recv, far_send, far_recv, near_send, near_recv, ring_send, ring_recv,
    head_send, head_recv, local,
):
    rank, count = lax.axis_index("seq"), lax.axis_size("seq")
    row_rank, row_count = lax.axis_index("dp"), lax.axis_size("dp")
    packs = ids_ref.shape[0]
    length, width = tok_ref.shape
    rows = qkv_ref.shape[0]
    slab = heads * size
    low = jnp.bfloat16
    mover = Mover(local)
    qkv_load, out_load = mover.load(qkv_any, qkv_ref), mover.load(out_any, out_ref)
    modw_load = mover.load(modw_any, modw_ref)
    down_load, pair_load = mover.load(down_any, down_ref), mover.load(pair_any, pair_ref)
    tok_loads = [mover.load(tok_any.at[0], tok_ref), mover.load(cot_any.at[0], cot_ref)]
    far, near = far_peers(row_rank, row_count), seq_peers(rank, count)
    act_ref[...] = jnp.zeros_like(act_ref)
    for item in range(items):
        cond = cond_ref[item].astype(jnp.float32)
        act = (cond / (1.0 + jnp.exp(-cond))).astype(low).astype(jnp.float32)
        for pack in range(packs):
            line = items * pack + item
            act_ref[line : line + 1] = act[pack : pack + 1]
    for index in range(row_count):
        cond_own_ref[index] = act_ref[:, index * rows : (index + 1) * rows]
    cond_all_ref[row_rank] = cond_own_ref[row_rank]
    qkv_load.wait()
    for index in range(3):
        head_src_ref[index] = qkv_ref[:, index * slab : (index + 1) * slab].astype(low)
    greet(far + near)

    def head_copy(index, slot, peer):
        return pltpu.make_async_remote_copy(
            src_ref=head_src_ref.at[index], dst_ref=head_x_ref.at[slot],
            send_sem=head_send.at[index], recv_sem=head_recv.at[slot],
            device_id={"seq": peer}, device_id_type=pl.DeviceIdType.MESH,
        )

    moves = []
    for index in range(3):
        peer, slot = (3 * rank + index) % count, (3 * rank + index) // count
        owner = (pow(3, -1, count) * (rank - index + 3 * count)) % count
        moves.append((peer, slot, owner, (3 * owner + index) // count))

        @pl.when(peer != rank)
        def _():
            head_copy(index, slot, peer).start()

        @pl.when(peer == rank)
        def _():
            head_x_ref[slot] = head_src_ref[index]

    conds = []
    for offset, peer in enumerate(far):
        conds.append(
            send(
                cond_own_ref.at[peer["dp"]], cond_all_ref.at[row_rank],
                far_send.at[0, offset], far_recv.at[0, offset], peer,
            )
        )
    hidden_rows = down_ref.shape[1] // count
    groups = pair_ref.shape[1] // (count * hidden_rows)
    down_load.wait()
    down = down_ref[...].T.astype(low)
    pair_load.wait()
    for target in range(count):
        pieces = []
        for group in range(groups):
            start = (group * count + target) * hidden_rows
            pieces.append(pair_ref[:, start : start + hidden_rows])
        pair_src_ref[target] = jnp.concatenate(pieces, axis=1).astype(low)
        down_src_ref[target] = down[target * hidden_rows : (target + 1) * hidden_rows]
    pair_x_ref[rank] = pair_src_ref[rank]
    down_x_ref[rank] = down_src_ref[rank]

    for index, (peer, slot, owner, landed) in enumerate(moves):
        @pl.when(peer != rank)
        def _():
            head_copy(index, slot, peer).wait_send()

        @pl.when(owner != rank)
        def _():
            head_copy(index, landed, owner).wait_recv()

    cut = ring_a_ref.shape[3]
    out_load.wait()
    block = jnp.concatenate(
        [head_x_ref[index] for index in range(3)] + [out_ref[...].astype(low)], axis=1
    )
    ring_a_ref[0, row_rank] = block[:, :cut]
    ring_b_ref[0, row_rank] = block[:, cut:]
    spread = spread_matrix(heads, size)
    main = slab // LANE * LANE

    def use(index):
        whole_block = jnp.concatenate([ring_a_ref[0, index], ring_b_ref[0, index]], axis=1)
        for part in range(3):
            wide_ref[index, :, part * heads * LANE : (part + 1) * heads * LANE] = jnp.dot(
                whole_block[:, part * slab : (part + 1) * slab], spread,
                preferred_element_type=jnp.float32,
            ).astype(low)
        mover.store(wide_ref.at[index], wide_any.at[index])
        out_a_ref[index] = whole_block[:, 3 * slab : 3 * slab + main]
        out_tail_ref[index] = whole_block[:, 3 * slab + main :]

    ring = RingGather([ring_a_ref, ring_b_ref], row_rank, row_count, ring_send, ring_recv, use)
    ring.launch_first()
    for copy in tok_loads:
        copy.wait()
    toks = [CubeGather(tok_ref, tok_all_ref, rank, count, tok_send.at[0], tok_recv.at[0])]
    tok_all_ref[:length] = tok_ref[...]
    cot_all_ref[:length] = cot_ref[...]
    weights = []
    for offset, peer in enumerate(near):
        weights.append(
            send(
                pair_src_ref.at[peer["seq"]], pair_x_ref.at[rank], near_send.at[0, offset],
                near_recv.at[0, offset], peer,
            )
        )
        weights.append(
            send(
                down_src_ref.at[peer["seq"]], down_x_ref.at[rank], near_send.at[1, offset],
                near_recv.at[1, offset], peer,
            )
        )
    toks.append(CubeGather(cot_ref, cot_all_ref, rank, count, tok_send.at[1], tok_recv.at[1]))
    modw_load.wait()
    modw = modw_ref[...].astype(low)
    for copy in conds:
        copy.wait_recv()
    lines = cond_all_ref.shape[1]
    conditions = cond_all_ref[...].reshape(row_count * lines, rows).astype(low)
    products = jnp.dot(conditions, modw, preferred_element_type=jnp.float32)
    part_ref[...] = products.reshape(part_ref.shape)
    side, group = row_rank % 2, row_rank // 2
    paired = send(
        part_ref.at[:, 1 - side], half_ref, far_send.at[1, row_count - 2],
        far_recv.at[1, row_count - 2], {"dp": flip(row_rank, 1)},
    )
    ring.use_first()
    ring.advance()

    order = cube_order(count)
    lane = lax.broadcasted_iota(jnp.int32, (length, LANE), 1)
    quarter = size // 4
    leading = (lane < quarter) | ((lane >= 2 * quarter) & (lane < 3 * quarter))

    def tables(pack):
        for slot in range(count):
            here = slice(slot * length, (slot + 1) * length)
            ids, row, col = token_layout(
                pack, xor(rank, order[slot]), length, lengths_ref, widths_ref
            )
            ids_ref[pack, here] = ids
            angle = jnp.where(lane < 2 * quarter, row, col) * freq_ref[...]
            sine = jnp.where(lane < size, jnp.sin(angle), 0.0)
            cos_ref[pack, here] = jnp.where(lane < size, jnp.cos(angle), 0.0)
            lead_ref[pack, here] = jnp.where(leading, -sine, 0.0)
            trail_ref[pack, here] = jnp.where(leading, 0.0, sine)
        mover.store(cos_ref.at[pack], cos_any.at[pack])
        mover.store(lead_ref.at[pack], lead_any.at[pack])
        mover.store(trail_ref.at[pack], trail_any.at[pack])

    paired.wait_recv()
    half_own_ref[...] = part_ref[:, side] + half_ref[...]
    parts = []
    for offset in range(1, row_count // 2):
        target = (group + offset) % (row_count // 2)
        parts.append(
            send(
                half_own_ref.at[target], sums_ref.at[group], far_send.at[1, offset - 1],
                far_recv.at[1, offset - 1], {"dp": 2 * target + side},
            )
        )
    sums_ref[group] = half_own_ref[group]
    tables(0)
    ring.advance()
    for copy in parts:
        copy.wait_recv()
    total = bias_ref[...].reshape(1, -1) + sums_ref[0]
    for index in range(1, row_count // 2):
        total += sums_ref[index]
    mod_own_ref[...] = total.astype(low).astype(jnp.float32)
    mods = []
    for offset, peer in enumerate(near):
        mods.append(
            send(
                mod_own_ref, mod_all_ref.at[rank], near_send.at[2, offset],
                near_recv.at[2, offset], peer,
            )
        )
    mod_all_ref[rank] = mod_own_ref[...]
    for pack in range(1, packs):
        tables(pack)
    ring.advance()
    for gather in toks:
        gather.advance()
    for copy in mods:
        copy.wait_recv()
    everything = jnp.concatenate([mod_all_ref[index] for index in range(count)], axis=1)
    for which in range(6):
        mod_ref[which] = everything[:, which * width : (which + 1) * width]
    for copy in weights:
        copy.wait_recv()
    down_own_ref[...] = jnp.concatenate([down_x_ref[index] for index in range(count)], axis=1)
    ring.finish()
    for gather, source, target in zip(
        toks, (tok_all_ref, cot_all_ref), (tok_all_any, cot_all_any)
    ):
        gather.finish()
        mover.store(source, target)
    per = LANE // (slab - main)
    for index in range(row_count // per):
        out_b_ref[index] = jnp.concatenate(
            [out_tail_ref[per * index + place] for place in range(per)], axis=1
        )
    for gather in toks:
        gather.settle()
    for copy in conds + [paired] + parts + weights + mods:
        copy.wait_send()
    mover.finish()


def opening(
    lengths, widths, tok, cot, cond, qkv, out, pair, down, modw, bias, lines, heads, size
):
    packs, length, width = tok.shape
    items = lengths.shape[1]
    count, row_count = lax.axis_size("seq"), lax.axis_size("dp")
    total = count * length
    low, full = jnp.bfloat16, jnp.float32
    rows, slab = qkv.shape[0], heads * size
    columns = modw.shape[1]
    hidden_rows = down.shape[1] // count
    chunk = pair.shape[1] // count
    block = 4 * slab
    main = slab // LANE * LANE
    per = LANE // (slab - main)
    cut = -(-block // (2 * LANE)) * LANE
    table = jax.ShapeDtypeStruct((packs, total, LANE), full)
    shapes = [
        jax.ShapeDtypeStruct((total, width), low),
        jax.ShapeDtypeStruct((total, width), low),
        jax.ShapeDtypeStruct((packs, total, 1), jnp.int32),
        table, table, table,
        jax.ShapeDtypeStruct((6, lines, width), full),
        jax.ShapeDtypeStruct((row_count, lines, rows), full),
        jax.ShapeDtypeStruct((row_count, rows, 3 * heads * LANE), low),
        jax.ShapeDtypeStruct((row_count, rows, main), low),
        jax.ShapeDtypeStruct((row_count // per, rows, LANE), low),
        jax.ShapeDtypeStruct((count, rows, chunk), low),
        jax.ShapeDtypeStruct((hidden_rows, count * slab), low),
    ]
    inside = pl.BlockSpec(memory_space=pltpu.VMEM)
    anywhere = pl.BlockSpec(memory_space=pl.ANY)
    scalars = pl.BlockSpec(memory_space=pltpu.SMEM)
    dma = pltpu.SemaphoreType.DMA
    return pl.pallas_call(
        partial(open_kernel, heads, size, items),
        out_shape=shapes,
        in_specs=[scalars] * 2 + [inside] * 3 + [anywhere] * 7,
        out_specs=[anywhere] * 2 + [inside] + [anywhere] * 3 + [inside] * 2 + [anywhere]
        + [inside] * 4,
        scratch_shapes=[
            pltpu.VMEM(qkv.shape, full), pltpu.VMEM(out.shape, full),
            pltpu.VMEM((length, width), low),
            pltpu.VMEM((length, width), low), pltpu.VMEM(pair.shape, full),
            pltpu.VMEM(down.shape, full), pltpu.VMEM(modw.shape, full),
            pltpu.VMEM((total, width), low), pltpu.VMEM((total, width), low),
            pltpu.VMEM((packs, total, LANE), full), pltpu.VMEM((packs, total, LANE), full),
            pltpu.VMEM((packs, total, LANE), full),
            pltpu.VMEM((row_count, rows, 3 * heads * LANE), low),
            pltpu.VMEM((row_count, rows, slab - main), low),
            pltpu.VMEM((lines, width), full),
            pltpu.VMEM((row_count, lines, rows), full),
            pltpu.VMEM((row_count // 2, 2, lines, columns), full),
            pltpu.VMEM((row_count // 2, lines, columns), full),
            pltpu.VMEM((row_count // 2, lines, columns), full),
            pltpu.VMEM((row_count // 2, lines, columns), full),
            pltpu.VMEM((lines, columns), full),
            pltpu.VMEM((count, lines, columns), full),
            pltpu.VMEM((3, rows, slab), low),
            pltpu.VMEM((3, rows, slab), low),
            pltpu.VMEM((1, row_count, rows, cut), low),
            pltpu.VMEM((1, row_count, rows, block - cut), low),
            pltpu.VMEM((count, rows, chunk), low),
            pltpu.VMEM((count, hidden_rows, slab), low),
            pltpu.VMEM((count, hidden_rows, slab), low),
            dma((2, count - 1)), dma((2, count - 1)),
            dma((2, row_count - 1)), dma((2, row_count - 1)),
            dma((3, count - 1)), dma((3, count - 1)),
            dma((2, row_count // 2, 2)), dma((2, row_count // 2, 2)),
            dma((3,)), dma((3,)), dma((9 + row_count + 3 * packs,)),
        ],
        compiler_params=pltpu.CompilerParams(
            collective_id=0, has_side_effects=True, vmem_limit_bytes=62 * 1024 * 1024
        ),
        name="opening",
    )(lengths, widths, cond, bias, frequencies(size), qkv, out, tok, cot, pair, down, modw)


def attend_pack(
    heads, size, items, pack, hook, keep, tok_ref, ids_ref, rows_ref, cos_ref, lead_ref, trail_ref,
    gains_ref, wide_ref, normed_ref, raw_ref, query_ref, key_ref, value_ref, inverse_ref, mixed_a_ref,
    mixed_b_ref, value_t_ref, out_ref,
):
    total, width = tok_ref.shape
    span = heads * LANE
    tile = fit(total, PROJECT_TILE)
    lane = lax.broadcasted_iota(jnp.int32, (tile, LANE), 1)

    def project(index, carry):
        start = pl.multiple_of(index * tile, tile)
        here = pl.ds(start, tile)
        ids = ids_ref[here]
        normal, _ = normalized(tok_ref[here].astype(jnp.float32))
        normed = (
            normal * (1.0 + chosen(ids, rows_ref, 1, pack, items))
            + chosen(ids, rows_ref, 0, pack, items)
        ).astype(jnp.bfloat16)
        normed_ref[here] = normed
        cos, lead, trail = cos_ref[here], lead_ref[here], trail_ref[here]
        query_mark = jnp.where((lane >= size) & (lane < size + 8) & (lane - size != ids), -200.0, 0.0)
        key_mark = jnp.where(lane - size == ids, 1.0, 0.0)
        for part in range(3):
            projected = dot(normed, wide_ref[:, part * span : (part + 1) * span])
            for head in range(heads):
                raw = projected[:, head * LANE : (head + 1) * LANE]
                slot = slice(head * LANE, (head + 1) * LANE)
                if part == 2:
                    value_ref[here, slot] = raw.astype(jnp.bfloat16)
                    continue
                raw_ref[here, part * span + head * LANE : part * span + (head + 1) * LANE] = raw
                square = jnp.sum(raw * raw, axis=-1, keepdims=True) * (1.0 / size)
                unit = raw * lax.rsqrt(square + norm_eps) * gain_row(gains_ref, part, size)
                turned = (
                    unit * cos
                    + pltpu.roll(unit, LANE - size // 4, 1) * lead
                    + pltpu.roll(unit, size // 4, 1) * trail
                )
                if part == 0:
                    turned = turned * (1.0 / math.sqrt(size))
                    query_ref[here, slot] = (turned + query_mark).astype(jnp.bfloat16)
                else:
                    key_ref[here, slot] = (turned + key_mark).astype(jnp.bfloat16)
        return carry

    lax.fori_loop(0, total // tile, project, 0)
    keep()
    hook()
    block = fit(total, SCORE_TILE)
    value_lane = lax.broadcasted_iota(jnp.int32, (total, LANE), 1)
    for head in range(heads):
        slot = slice(head * LANE, (head + 1) * LANE)
        marked = jnp.where(value_lane == size, 1.0, value_ref[:, slot].astype(jnp.float32))
        value_t_ref[...] = marked.T.astype(jnp.bfloat16)

        def score(index, carry):
            here = pl.ds(pl.multiple_of(index * block, block), block)
            weights = jnp.exp(dot_t(key_ref[:, slot], query_ref[here, slot])).astype(jnp.bfloat16)
            mixed = dot(value_t_ref[...], weights)
            inverse = 1.0 / mixed[size : size + 1]
            inverse_ref[head : head + 1, here] = inverse
            out_ref[here, slot] = (mixed * inverse).T.astype(jnp.bfloat16)
            return carry

        lax.fori_loop(0, total // block, score, 0)
        hook()
    spread = spread_matrix(heads, size)

    blocks = mixed_b_ref.shape[0]
    length = total // blocks

    def narrow(index, carry):
        here = pl.ds(pl.multiple_of(index * length, length), length)
        values = dot_t(out_ref[here], spread).astype(jnp.bfloat16)
        mixed_a_ref[here], mixed_b_ref[index] = narrow_parts(values)
        return carry

    lax.fori_loop(0, blocks, narrow, 0)


def attend_kernel(
    heads, size, items, ids_ref, rows_ref, gains_ref, first_any, tok_any, cos_any, lead_any,
    trail_any, wide_any, out_a_any, out_b_any, pair_any, cot_any,
    normed_any, raw_any, query_any, key_any, value_any, inverse_ref,
    mixed_a_any, mixed_b_any, out_full_any, pair_all_any, cot_all_any,
    cos_ref, lead_ref, trail_ref, wide_ref, out_a_ref, out_b_ref, pair_ref,
    normed_ref, raw_ref, query_ref, key_ref, value_ref, mixed_a_ref, mixed_b_ref, out_full_ref,
    pair_all_ref, cot_all_ref,
    tok_ref, tok_own_ref, cot_own_ref,
    value_t_ref, wide_out_ref, own_a_ref, own_b_ref, slots_a_ref, slots_b_ref,
    ring_send, ring_recv, mixed_send, mixed_recv, out_send, out_recv,
    tok_send, tok_recv, cot_send, cot_recv, local,
):
    rank, count = lax.axis_index("seq"), lax.axis_size("seq")
    row_rank, row_count = lax.axis_index("dp"), lax.axis_size("dp")
    packs, total, width = tok_ref.shape
    length = total // count
    order = cube_order(count)
    mover = Mover(local)
    early = [
        mover.load(pair_any, pair_ref), mover.load(out_a_any, out_a_ref),
        mover.load(out_b_any, out_b_ref),
    ]
    for pack in range(1, packs):
        early.append(mover.load(tok_any.at[pack], tok_own_ref.at[pack - 1]))
        early.append(mover.load(cot_any.at[pack], cot_own_ref.at[pack - 1]))
    loads = [[mover.load(first_any, tok_ref.at[0])]] + [[] for _ in range(1, packs)]
    for pack in range(packs):
        for source, target in ((cos_any, cos_ref), (lead_any, lead_ref), (trail_any, trail_ref)):
            loads[pack].append(mover.load(source.at[pack], target.at[pack]))
        if pack == 0:
            wide_load = mover.load(wide_any, wide_ref)
    for copy in early:
        copy.wait()
    greet(ring_peers(row_rank, row_count) + seq_peers(rank, count))
    for lead in range(pair_ref.shape[0]):
        pair_all_ref[lead, row_rank] = pair_ref[lead]
    half = pair_ref.shape[0] // 2
    ring = RingGather(
        [pair_all_ref.at[pl.ds(0, half)], pair_all_ref.at[pl.ds(half, half)]], row_rank, row_count, ring_send, ring_recv
    )
    ring.advance()
    toks = []
    for pack in range(1, packs):
        toks.append(
            CubeGather(
                tok_own_ref.at[pack - 1], tok_ref.at[pack], rank, count, tok_send.at[pack - 1],
                tok_recv.at[pack - 1],
            )
        )
        tok_ref[pack, :length] = tok_own_ref[pack - 1]
        cot_all_ref[pack - 1, :length] = cot_own_ref[pack - 1]
    spreads, cots = [], []
    slots_a_ref[:row_count] = out_a_ref[...]
    slots_b_ref[: out_b_ref.shape[0]] = out_b_ref[...]
    per = row_count // out_b_ref.shape[0]
    rest = LANE // per
    marks = [0]
    turns = packs * (heads + 1)

    def hook():
        marks[0] += 1
        if marks[0] in (turns * 3 // 10, turns * 6 // 10, turns * 9 // 10) and ring.going:
            ring.advance()
        if marks[0] == 3:
            for gather in toks:
                gather.advance()
        if marks[0] == 2:
            spreads.append(
                CubeGather(out_a_ref, slots_a_ref, rank, count, out_send.at[0], out_recv.at[0])
            )
            spreads.append(
                CubeGather(out_b_ref, slots_b_ref, rank, count, out_send.at[1], out_recv.at[1])
            )
        if marks[0] == heads + 2:
            for pack in range(1, packs):
                cots.append(
                    CubeGather(
                        cot_own_ref.at[pack - 1], cot_all_ref.at[pack - 1], rank, count,
                        cot_send.at[pack - 1], cot_recv.at[pack - 1],
                    )
                )
        if marks[0] == turns:
            for gather in spreads:
                gather.advance()

    sends = []
    wide_load.wait()
    for pack in range(packs):
        for copy in loads[pack]:
            copy.wait()
        if pack:
            toks[pack - 1].finish()

        def keep():
            for source, target in (
                (normed_ref, normed_any), (raw_ref, raw_any), (query_ref, query_any),
                (key_ref, key_any), (value_ref, value_any),
            ):
                mover.store(source.at[pack], target.at[pack])

        attend_pack(
            heads, size, items, pack, hook, keep, tok_ref.at[pack], ids_ref.at[pack], rows_ref,
            cos_ref.at[pack], lead_ref.at[pack], trail_ref.at[pack], gains_ref, wide_ref,
            normed_ref.at[pack], raw_ref.at[pack], query_ref.at[pack], key_ref.at[pack],
            value_ref.at[pack], inverse_ref.at[pack], own_a_ref.at[pack], own_b_ref.at[pack],
            value_t_ref, wide_out_ref,
        )
        for slot in range(1, count):
            where = {"seq": xor(rank, order[slot])}
            sends.append(
                send(
                    own_a_ref.at[pack, pl.ds(slot * length, length)], mixed_a_ref.at[pack, rank],
                    mixed_send.at[0, pack, slot - 1], mixed_recv.at[0, pack, slot - 1], where,
                )
            )
            sends.append(
                send(
                    own_b_ref.at[pack, slot], mixed_b_ref.at[pack, rank],
                    mixed_send.at[1, pack, slot - 1], mixed_recv.at[1, pack, slot - 1], where,
                )
            )
        mixed_a_ref[pack, rank] = own_a_ref[pack, :length]
        mixed_b_ref[pack, rank] = own_b_ref[pack, 0]
    ring.finish()
    chunk = pair_ref.shape[2]
    for lead in range(pair_ref.shape[0]):
        mover.store(pair_all_ref.at[lead], pair_all_any.at[:, :, pl.ds(lead * chunk, chunk)])
    for gather in spreads:
        gather.finish()
    for gather in cots:
        gather.advance()
    for index in range(row_count):
        place = slice((index % per) * rest, (index % per + 1) * rest)
        pieces = []
        for owner in range(count):
            slot = cube_slot(xor(rank, owner), count)
            pieces.append(slots_a_ref[slot * row_count + index])
            pieces.append(slots_b_ref[slot * (row_count // per) + index // per][:, place])
        out_full_ref[index] = jnp.concatenate(pieces, axis=1)
    mover.store(out_full_ref, out_full_any)
    for gather in cots:
        gather.finish()
    mover.store(cot_all_ref, cot_all_any)
    for copy in sends:
        copy.wait_recv()
    mover.store(mixed_a_ref, mixed_a_any)
    mover.store(mixed_b_ref, mixed_b_any)
    for gather in spreads + toks + cots:
        gather.settle()
    for copy in sends:
        copy.wait_send()
    mover.finish()


def attend(first, tok, ids, rows, turns, gains, wide, out_a, out_b, pair, cot, items, heads, size):
    packs, length, width = tok.shape
    count, row_count = lax.axis_size("seq"), lax.axis_size("dp")
    total = first.shape[0]
    span, slab = heads * LANE, heads * size
    my_rows, main = out_a.shape[1:]
    per = row_count // out_b.shape[0]
    later = max(packs - 1, 1)
    low, full = jnp.bfloat16, jnp.float32
    shapes = [
        jax.ShapeDtypeStruct((packs, total, width), low),
        jax.ShapeDtypeStruct((packs, total, 2 * span), full),
        jax.ShapeDtypeStruct((packs, total, span), low),
        jax.ShapeDtypeStruct((packs, total, span), low),
        jax.ShapeDtypeStruct((packs, total, span), low),
        jax.ShapeDtypeStruct((packs, heads, total), full),
        jax.ShapeDtypeStruct((packs, count, length, main), low),
        jax.ShapeDtypeStruct((packs, count, length // per, LANE), low),
        jax.ShapeDtypeStruct((row_count, my_rows, count * slab), low),
        jax.ShapeDtypeStruct((row_count, my_rows, pair.shape[0] * pair.shape[2]), low),
        jax.ShapeDtypeStruct((later, total, width), low),
    ]
    staged = [pltpu.VMEM(shape.shape, shape.dtype) for index, shape in enumerate(shapes) if index != 5]
    staged[8] = pltpu.VMEM((pair.shape[0], row_count) + pair.shape[1:], low)
    inside = pl.BlockSpec(memory_space=pltpu.VMEM)
    anywhere = pl.BlockSpec(memory_space=pl.ANY)
    dma = pltpu.SemaphoreType.DMA
    direct = [*turns, wide, out_a, out_b, pair]
    return pl.pallas_call(
        partial(attend_kernel, heads, size, items),
        out_shape=shapes,
        in_specs=[inside] * 3 + [anywhere] * 10,
        out_specs=[anywhere] * 5 + [inside] + [anywhere] * 5,
        scratch_shapes=[pltpu.VMEM(entry.shape, entry.dtype) for entry in direct]
        + staged
        + [
            pltpu.VMEM((packs, total, width), low), pltpu.VMEM((later, length, width), low),
            pltpu.VMEM((later, length, width), low),
            pltpu.VMEM((LANE, total), low), pltpu.VMEM((total, span), low),
            pltpu.VMEM((packs, total, main), low),
            pltpu.VMEM((packs, count, length // per, LANE), low),
            pltpu.VMEM((count * row_count, my_rows, main), low),
            pltpu.VMEM((count * row_count // per, my_rows, LANE), low),
            dma((2, row_count // 2, 2)), dma((2, row_count // 2, 2)),
            dma((2, packs, count - 1)), dma((2, packs, count - 1)),
            dma((2, count - 1)), dma((2, count - 1)),
            dma((later, count - 1)), dma((later, count - 1)),
            dma((later, count - 1)), dma((later, count - 1)),
            dma((13 + 10 * packs,)),
        ],
        compiler_params=pltpu.CompilerParams(
            collective_id=1, has_side_effects=True, vmem_limit_bytes=62 * 1024 * 1024
        ),
        name="attend",
    )(ids, rows, gains, first, tok, *turns, wide, out_a, out_b, pair, cot)


def middle_kernel(
    items, ids_ref, rows_ref, down_ref, mixed_a_any, mixed_b_any, tok_any, own_cot_any, out_any,
    pair_any, cot_any, cot_later_any,
    middle_any, branch_own_ref, branch_move_ref, grad_a_any, grad_b_any, grad_middle_ref, part_ref, pair_grad_any, down_sum_ref,
    out_grad_any,
    mixed_a_ref, mixed_b_ref, tok_ref, own_cot_ref, out_ref, pair_ref, branch_in_ref,
    grad_a_ref, grad_b_ref, pair_grad_ref, out_grad_ref,
    down_a_ref, down_b_ref, own_ref, attended_ref, middle_ref, normed_ref, hidden_ref, gated_ref,
    partial_ref, landed_ref, total_ref, branch_ref, branch_landed_ref,
    gmix_a_ref, gmix_b_ref, coming_ref, down_grad_ref, down_total_ref,
    down_land_ref,
    ring_send, ring_recv, norm_send, norm_recv, grad_send, grad_recv, branch_send, branch_recv,
    mix_send, mix_recv, back_send, back_recv, local,
):
    rank, count = lax.axis_index("seq"), lax.axis_size("seq")
    row_rank, row_count = lax.axis_index("dp"), lax.axis_size("dp")
    packs, total, width = branch_in_ref.shape
    length = total // count
    slab = width // count
    chunk = pair_ref.shape[1] // count
    cut = down_a_ref.shape[3]
    hidden = row_count * down_ref.shape[0]
    order = cube_order(count)
    low, full = jnp.bfloat16, jnp.float32
    mover = Mover(local)
    first = [
        mover.load(mixed_a_any, mixed_a_ref), mover.load(mixed_b_any, mixed_b_ref),
        mover.load(out_any, out_ref), mover.load(tok_any, tok_ref),
    ]
    cot_loads = [
        mover.load(cot_later_any.at[pack - 1] if pack else cot_any, branch_in_ref.at[pack])
        for pack in range(packs)
    ]
    own_load, pair_load = mover.load(own_cot_any, own_cot_ref), mover.load(pair_any, pair_ref)
    greet(ring_peers(row_rank, row_count) + seq_peers(rank, count))
    down_a_ref[0, row_rank] = down_ref[:, :cut]
    down_b_ref[0, row_rank] = down_ref[:, cut:]
    ring = RingGather([down_a_ref, down_b_ref], row_rank, row_count, ring_send, ring_recv)
    ring.advance()
    part_ref[...] = jnp.zeros_like(part_ref)

    def own_ids(pack):
        return ids_ref[pack, :length]

    def pick(pack, which):
        return chosen(own_ids(pack), rows_ref, which, pack, items)

    def by_item(pack, which, values):
        for item in range(items):
            line = items * pack + item
            part_ref[which - 2, line : line + 1] = jnp.sum(
                jnp.where(own_ids(pack) == item, values, 0.0), axis=0, keepdims=True
            )

    gathers = []

    def start_gather(pack):
        gathers.append(
            CubeGather(
                coming_ref.at[pack], normed_ref.at[pack], rank, count, norm_send.at[pack],
                norm_recv.at[pack],
            )
        )

    for copy in first:
        copy.wait()
    for pack in range(packs):
        own = jnp.concatenate(
            [join_parts(mixed_a_ref[pack, index], mixed_b_ref[pack, index]) for index in range(count)],
            axis=1,
        )
        own_ref[pack] = own
        attended = dot(own, out_ref[...])
        attended_ref[pack] = attended.astype(low)
        middle = tok_ref[pack].astype(full) + pick(pack, 2) * attended
        middle_ref[pack] = middle
        mover.store(middle_ref.at[pack], middle_any.at[pack])
        normal, _ = normalized(middle)
        coming_ref[pack] = (normal * (1.0 + pick(pack, 4)) + pick(pack, 3)).astype(low)
        normed_ref[pack, :length] = coming_ref[pack]
        if pack == 0:
            start_gather(0)
        ring.advance()
    tile = fit(total, 2 * length)

    def scale_cotangent(pack):
        def step(index, carry):
            here = pl.ds(pl.multiple_of(index * length, length), length)
            gate = chosen(ids_ref[pack, here], rows_ref, 5, pack, items)
            branch_in_ref[pack, here] = (branch_in_ref[pack, here].astype(full) * gate).astype(low)
            return carry

        lax.fori_loop(0, count, step, 0)

    own_load.wait()
    gathers[0].advance()
    for pack in range(1, packs):
        start_gather(pack)
    cot_loads[0].wait()
    scale_cotangent(0)
    ring.advance()
    pair_load.wait()

    def down_part(which):
        ref = (down_a_ref, down_b_ref)[which]
        return ref[0].reshape(hidden, ref.shape[3])

    def forward(pack, start):
        here = pl.ds(start, tile)
        both = dot(normed_ref[pack, here], pair_ref[...])
        gate, up = both[:, :hidden], both[:, hidden:]
        hidden_ref[pack, here] = (gate / (1.0 + jnp.exp(-gate)) * up).astype(low)
        gated_ref[pack, here] = both.astype(low)

    def backward(pack, start):
        here = pl.ds(start, tile)
        coming = branch_in_ref[pack, here]
        grad = dot_t(coming[:, :cut], down_part(0)) + dot_t(coming[:, cut:], down_part(1))
        gate = gated_ref[pack, here, :hidden].astype(full)
        up = gated_ref[pack, here, hidden:].astype(full)
        sigmoid = 1.0 / (1.0 + jnp.exp(-gate))
        grad_gate = grad * up * sigmoid * (1.0 + gate * (1.0 - sigmoid))
        gated_ref[pack, here, :hidden] = grad_gate.astype(low)
        gated_ref[pack, here, hidden:] = (grad * gate * sigmoid).astype(low)
        partial_ref[pack, here] = dot_t(gated_ref[pack, here], pair_ref[...]).astype(low)

    reduces, branches = [], []
    for pack in range(packs):
        gathers[pack].finish()
        forward(pack, 0)
        forward(pack, total // 2)
        if pack == 0:
            for later in range(1, packs):
                cot_loads[later].wait()
                scale_cotangent(later)
            ring.finish()
        reduces.append(
            CubeReduce(
                partial_ref.at[pack], landed_ref.at[pack], total_ref.at[pack], rank, count,
                grad_send.at[pack], grad_recv.at[pack],
            )
        )
        backward(pack, total // 2)
        reduces[pack].near()
        backward(pack, 0)
        reduces[pack].across()

    def branch_part(pack, start):
        here = pl.ds(start, tile)
        values = hidden_ref[pack, here]
        branch_ref[here, :cut] = dot(values, down_part(0)).astype(low)
        branch_ref[here, cut:] = dot(values, down_part(1)).astype(low)

    def middle_back(pack):
        normal, inverse = normalized(middle_ref[pack])
        grad_normed = reduces[pack].result()
        grad_middle = own_cot_ref[pack].astype(full) + normalized_back(
            normal, inverse, grad_normed * (1.0 + pick(pack, 4))
        )
        grad_middle_ref[pack] = grad_middle
        by_item(pack, 2, grad_middle * attended_ref[pack].astype(full))
        by_item(pack, 3, grad_normed)
        by_item(pack, 4, grad_normed * normal)
        grad_attended = (grad_middle * pick(pack, 2)).astype(low)
        coming_ref[pack] = grad_attended
        grad_mixed = dot_t(grad_attended, out_ref[...]).astype(low)
        for index in range(count):
            gmix_a_ref[pack, index], gmix_b_ref[pack, index] = narrow_parts(
                grad_mixed[:, index * slab : (index + 1) * slab]
            )
        copies = []
        for slot in range(1, count):
            peer = xor(rank, order[slot])
            copies.append(
                send(
                    gmix_a_ref.at[pack, peer], grad_a_ref.at[pack, slot],
                    mix_send.at[0, pack, slot - 1], mix_recv.at[0, pack, slot - 1], {"seq": peer},
                )
            )
            copies.append(
                send(
                    gmix_b_ref.at[pack, peer], grad_b_ref.at[pack, slot],
                    mix_send.at[1, pack, slot - 1], mix_recv.at[1, pack, slot - 1], {"seq": peer},
                )
            )
        grad_a_ref[pack, 0], grad_b_ref[pack, 0] = (
            gmix_a_ref[pack, rank], gmix_b_ref[pack, rank]
        )
        return copies

    def branch_start(pack):
        branch_part(pack, total // 2)
        branches.append(
            send(
                branch_ref.at[pl.ds(total // 2, total // 2)], branch_landed_ref.at[pack],
                branch_send.at[pack], branch_recv.at[pack], {"seq": flip(rank, 1)},
            )
        )
        branch_part(pack, 0)

    def branch_finish(pack):
        branches[pack].wait_recv()
        own, move = slice(0, length), slice(length, 2 * length)
        branch_own_ref[pack] = (
            branch_ref[own].astype(full) + branch_landed_ref[pack, own].astype(full)
        )
        branch_move_ref[pack] = (
            branch_ref[move].astype(full) + branch_landed_ref[pack, move].astype(full)
        ).astype(low)
        branches[pack].wait_send()

    strip = fit(width, 384)
    hidden_rows = down_ref.shape[0]
    back = RingReduce(
        [down_grad_ref], [down_sum_ref], [down_total_ref], [down_land_ref], row_rank, row_count,
        back_send, back_recv,
    )

    def down_grads():
        for start in range(0, hidden, chunk):
            grad = sum(
                dot(hidden_ref[pack, :, start : start + chunk].T, branch_in_ref[pack])
                for pack in range(packs)
            ).astype(low)
            first_block = start // hidden_rows
            down_grad_ref[0, first_block : first_block + chunk // hidden_rows] = grad.reshape(
                chunk // hidden_rows, hidden_rows, width
            )

    def pair_grads(start):
        grad = sum(
            dot(normed_ref[pack, :, start : start + strip].T, gated_ref[pack]) for pack in range(packs)
        )
        here = pl.ds(start, strip)
        pair_grad_ref[here] = grad.astype(low)
        for index in range(count):
            mover.store(
                pair_grad_ref.at[here, pl.ds(index * chunk, chunk)], pair_grad_any.at[index, here]
            )

    mixes = []
    branch_start(0)
    for pack in range(packs):
        gathers[pack].settle()
    down_grads()
    back.advance()
    strips = list(range(0, width, strip))
    pair_grads(strips[0])
    back.advance()
    for pack in range(packs):
        mixes += middle_back(pack)
    for pack in range(1, packs):
        branch_finish(pack - 1)
        branch_start(pack)
    back.advance()
    for start in strips[1:]:
        pair_grads(start)
    back.advance()
    for start in range(0, width, strip):
        left = [own_ref[pack, :, start : start + strip].T for pack in range(packs)]
        grad = sum(dot(left[pack], coming_ref[pack]) for pack in range(packs)).astype(low)
        for index in range(count):
            out_grad_ref[index] = grad[:, index * slab : (index + 1) * slab]
        mover.load(out_grad_ref, out_grad_any.at[:, pl.ds(start, strip)]).wait()
    branch_finish(packs - 1)
    for copy in mixes:
        copy.wait_recv()
    mover.store(grad_a_ref, grad_a_any)
    mover.store(grad_b_ref, grad_b_any)
    back.finish()
    mover.finish()
    for group in reduces:
        group.settle()
    for copy in mixes:
        copy.wait_send()


def middle(
    mixed_a, mixed_b, tok, ids, rows, own_cot, cot, cot_later, out, pair, down, items
):
    packs, length, width = tok.shape
    count, row_count = lax.axis_size("seq"), lax.axis_size("dp")
    total, slab = count * length, width // count
    hidden_rows = down.shape[0]
    hidden = row_count * hidden_rows
    low, full = jnp.bfloat16, jnp.float32
    lines = rows.shape[1]
    cut = -(-width // (2 * LANE)) * LANE
    half = total // 2
    steps = row_count // 2
    shapes = [
        jax.ShapeDtypeStruct((packs, length, width), full),
        jax.ShapeDtypeStruct((packs, length, width), full),
        jax.ShapeDtypeStruct((packs, length, width), low),
        jax.ShapeDtypeStruct(mixed_a.shape, low),
        jax.ShapeDtypeStruct(mixed_b.shape, low),
        jax.ShapeDtypeStruct((packs, length, width), full),
        jax.ShapeDtypeStruct((3, lines, width), full),
        jax.ShapeDtypeStruct((count, width, 2 * hidden // count), low),
        jax.ShapeDtypeStruct((1, hidden_rows, width), full),
        jax.ShapeDtypeStruct((count, width, slab), low),
    ]
    inside = pl.BlockSpec(memory_space=pltpu.VMEM)
    anywhere = pl.BlockSpec(memory_space=pl.ANY)
    dma = pltpu.SemaphoreType.DMA
    inputs = [mixed_a, mixed_b, tok, own_cot, out, pair]
    strip = jax.ShapeDtypeStruct((count, fit(width, 384), slab), low)
    every = jax.ShapeDtypeStruct((packs, total, width), low)
    staged = [every, shapes[3], shapes[4], pair, strip]
    return pl.pallas_call(
        partial(middle_kernel, items),
        out_shape=shapes,
        in_specs=[inside] * 3 + [anywhere] * 8,
        out_specs=[anywhere] + [inside] * 2 + [anywhere] * 2 + [inside] * 2
        + [anywhere, inside, anywhere],
        scratch_shapes=[pltpu.VMEM(entry.shape, entry.dtype) for entry in inputs + staged]
        + [
            pltpu.VMEM((1, row_count, hidden_rows, cut), low),
            pltpu.VMEM((1, row_count, hidden_rows, width - cut), low),
            pltpu.VMEM((packs, length, width), low),
            pltpu.VMEM((packs, length, width), low),
            pltpu.VMEM((packs, length, width), full),
            pltpu.VMEM((packs, total, width), low),
            pltpu.VMEM((packs, total, hidden), low),
            pltpu.VMEM((packs, total, 2 * hidden), low),
            pltpu.VMEM((packs, total, width), low),
            pltpu.VMEM((packs, half + length, width), low),
            pltpu.VMEM((packs, length, width), low),
            pltpu.VMEM((total, width), low),
            pltpu.VMEM((packs, half, width), low),
            pltpu.VMEM(mixed_a.shape, low),
            pltpu.VMEM(mixed_b.shape, low),
            pltpu.VMEM((packs, length, width), low),
            pltpu.VMEM((1, row_count, hidden_rows, width), low),
            pltpu.VMEM((2, steps - 1, 1, hidden_rows, width), low),
            pltpu.VMEM((2, steps, 1, hidden_rows, width), low),
            dma((2, steps, 2)), dma((2, steps, 2)),
            dma((packs, count - 1)), dma((packs, count - 1)),
            dma((packs, 2)), dma((packs, 2)), dma((packs,)), dma((packs,)),
            dma((2, packs, count - 1)), dma((2, packs, count - 1)),
            dma((2, steps, 1)), dma((2, steps, 1)),
            dma((24 + 2 * packs,)),
        ],
        compiler_params=pltpu.CompilerParams(
            collective_id=2, has_side_effects=True, vmem_limit_bytes=62 * 1024 * 1024
        ),
        name="middle",
    )(ids, rows, down, *inputs, cot, cot_later)


def attend_back_pack(
    heads, size, hook, enter, ready, mixed_a_ref, mixed_b_ref, raw_ref, query_ref, key_ref, value_ref, inverse_ref,
    cos_ref, lead_ref, trail_ref, gains_ref, wide_ref,
    grad_ref, normed_ref, gain_ref,
    wide_mixed_ref, key_t_ref, dq_ref, dk_ref, dv_ref,
):
    blocks, length = mixed_a_ref.shape[:2]
    total = blocks * length
    span = heads * LANE
    tile = fit(total, BACK_TILE)
    block = fit(total, BACK_SCORE_TILE)
    spread = spread_matrix(heads, size)

    def widen(index, carry):
        here = pl.ds(pl.multiple_of(index * length, length), length)
        values = join_parts(mixed_a_ref[index], mixed_b_ref[index])
        wide_mixed_ref[here] = dot(values, spread).astype(jnp.bfloat16)
        return carry

    lax.fori_loop(0, blocks, widen, 0)
    for head in range(heads):
        slot = slice(head * LANE, (head + 1) * LANE)
        key_t_ref[...] = key_ref[:, slot].astype(jnp.float32).T.astype(jnp.bfloat16)
        dk_ref[...] = jnp.zeros_like(dk_ref)
        dv_ref[...] = jnp.zeros_like(dv_ref)

        def score(index, carry):
            start = pl.multiple_of(index * block, block)
            here = pl.ds(start, block)
            query, coming = query_ref[here, slot], wide_mixed_ref[here, slot]
            scores = lax.dot_general(
                key_ref[:, slot], query, (((1,), (1,)), ((), ())),
                preferred_element_type=jnp.float32,
            )
            probs = jnp.exp(scores) * inverse_ref[head : head + 1, here]
            grad_probs = lax.dot_general(
                value_ref[:, slot], coming, (((1,), (1,)), ((), ())),
                preferred_element_type=jnp.float32,
            )
            inner = jnp.sum(probs * grad_probs, axis=0, keepdims=True)
            grad_scores = (probs * (grad_probs - inner)).astype(jnp.bfloat16)
            dv_ref[...] += jnp.dot(
                probs.astype(jnp.bfloat16), coming, preferred_element_type=jnp.float32
            )
            dk_ref[...] += jnp.dot(grad_scores, query, preferred_element_type=jnp.float32)
            dq_ref[here] = jnp.dot(
                key_t_ref[...], grad_scores, preferred_element_type=jnp.float32
            ).T
            return carry

        lax.fori_loop(0, total // block, score, 0)

        def unturn(index, carry):
            here = pl.ds(pl.multiple_of(index * tile, tile), tile)
            cos, lead, trail = cos_ref[here], lead_ref[here], trail_ref[here]
            for part, source in ((0, dq_ref), (1, dk_ref)):
                coming = source[here]
                if part == 0:
                    coming = coming * (1.0 / math.sqrt(size))
                coming = (
                    coming * cos
                    - pltpu.roll(coming, LANE - size // 4, 1) * lead
                    - pltpu.roll(coming, size // 4, 1) * trail
                )
                start = part * span + head * LANE
                raw = raw_ref[here, start : start + LANE]
                square = jnp.sum(raw * raw, axis=-1, keepdims=True) * (1.0 / size)
                inverse = lax.rsqrt(square + norm_eps)
                unit = raw * inverse
                scaled = coming * gain_row(gains_ref, part, size)
                slope = jnp.sum(scaled * unit, axis=-1, keepdims=True) * (1.0 / size)
                grad_ref[here, start : start + LANE] = (
                    inverse * (scaled - unit * slope)
                ).astype(jnp.bfloat16)
                gain_ref[part : part + 1] += jnp.sum(coming * unit, axis=0, keepdims=True)
            start = 2 * span + head * LANE
            grad_ref[here, start : start + LANE] = dv_ref[here].astype(jnp.bfloat16)
            return carry

        if head == 0:
            enter()
        lax.fori_loop(0, total // tile, unturn, 0)
        hook()

    ready()

    def project(index, carry):
        here = pl.ds(pl.multiple_of(index * tile, tile), tile)
        normed_ref[here] = lax.dot_general(
            grad_ref[here], wide_ref[...], (((1,), (1,)), ((), ())),
            preferred_element_type=jnp.float32,
        ).astype(jnp.bfloat16)
        return carry

    lax.fori_loop(0, total // tile, project, 0)


def attend_back_kernel(
    heads, size, items, inverse_ref, gains_ref, ids_ref, rows_ref, branch_own_any, branch_move_any,
    middle_any, cot_any, mixed_a_any, mixed_b_any, query_any, key_any, value_any,
    raw_any, cos_any, lead_any, trail_any, wide_any, pair_any, out_any,
    grad_any, normed_any, gain_ref, reduced_ref, pair_sum_ref, out_sum_ref, layer_ref, gate_ref,
    branch_own_ref, branch_move_ref, middle_ref, cot_ref, mixed_a_ref, mixed_b_ref, query_ref, key_ref, value_ref, raw_ref, cos_ref, lead_ref, trail_ref,
    wide_ref, pair_ref, out_ref, grad_ref, normed_ref,
    wide_mixed_ref, key_t_ref, dq_ref, dk_ref, dv_ref,
    pair_total_ref, out_total_ref, pair_land_ref, out_land_ref,
    out_near_ref, out_move_a_ref, out_move_b_ref, out_far_a_ref, out_far_b_ref, out_own_ref, landed_ref, total_ref, branch_far_ref,
    ring_send, ring_recv, late_send, late_recv, out_send, out_recv, part_send, part_recv,
    branch_send, branch_recv, local,
):
    rank, count = lax.axis_index("seq"), lax.axis_size("seq")
    row_rank, row_count = lax.axis_index("dp"), lax.axis_size("dp")
    packs = mixed_a_ref.shape[0]
    mover = Mover(local)
    pair_load, out_load = mover.load(pair_any, pair_ref), mover.load(out_any, out_ref)
    move_load = mover.load(branch_move_any, branch_move_ref)
    loads = []
    for pack in range(packs):
        loads.append(
            [
                mover.load(source.at[pack], target.at[pack])
                for source, target in (
                    (mixed_a_any, mixed_a_ref), (mixed_b_any, mixed_b_ref),
                    (query_any, query_ref), (key_any, key_ref), (value_any, value_ref),
                    (cos_any, cos_ref), (lead_any, lead_ref),
                    (trail_any, trail_ref),
                )
            ]
        )
        if pack == 0:
            raw_loads = [mover.load(raw_any.at[0], raw_ref)]
            wide_load = mover.load(wide_any, wide_ref)
    late_loads = [
        mover.load(branch_own_any, branch_own_ref), mover.load(middle_any, middle_ref),
        mover.load(cot_any, cot_ref),
    ]
    pair_load.wait()
    out_load.wait()
    move_load.wait()
    greet(ring_peers(row_rank, row_count) + seq_peers(rank, count))
    half = pair_ref.shape[0] // 2
    sides = [pl.ds(0, half), pl.ds(half, half)]
    ring = RingReduce(
        [pair_ref.at[side] for side in sides], [pair_sum_ref.at[side] for side in sides],
        [pair_total_ref.at[:, :, side] for side in sides],
        [pair_land_ref.at[:, :, side] for side in sides], row_rank, row_count, ring_send, ring_recv,
    )
    ring.advance()
    mate, across = flip(rank, 1), flip(rank, 2)
    near = [
        send(
            out_ref.at[flip(mate, 2) if index else mate], out_near_ref.at[index],
            out_send.at[index], out_recv.at[index], {"seq": mate},
        )
        for index in range(2)
    ]
    late = RingReduce(
        [out_own_ref], [out_sum_ref], [out_total_ref], [out_land_ref], row_rank, row_count,
        late_send, late_recv,
    )
    marks, moved, reduces, branches = [0], [], [], []
    turns = packs * heads
    length, width = middle_ref.shape[1:]

    def send_branch(pack):
        branches.append(
            send(
                branch_move_ref.at[pack], branch_far_ref.at[pack], branch_send.at[pack],
                branch_recv.at[pack], {"seq": across},
            )
        )

    def finish_layer(pack):
        branches[pack].wait_recv()
        ids = ids_ref[pack, :length]
        branch = branch_own_ref[pack] + branch_far_ref[pack].astype(jnp.float32)
        layer_ref[pack] = (
            middle_ref[pack] + chosen(ids, rows_ref, 5, pack, items) * branch
        ).astype(jnp.bfloat16)
        values = cot_ref[pack].astype(jnp.float32) * branch
        for item in range(items):
            line = items * pack + item
            gate_ref[line : line + 1] = jnp.sum(
                jnp.where(ids == item, values, 0.0), axis=0, keepdims=True
            )


    def hook():
        marks[0] += 1
        if marks[0] == 1:
            near[1].wait_recv()
            out_move_a_ref[...], out_move_b_ref[...] = narrow_parts(
                (
                    out_ref[across].astype(jnp.float32) + out_near_ref[1].astype(jnp.float32)
                ).astype(jnp.bfloat16)
            )
            moved.append(
                send(out_move_a_ref, out_far_a_ref, out_send.at[2], out_recv.at[2], {"seq": across})
            )
            moved.append(
                send(out_move_b_ref, out_far_b_ref, out_send.at[3], out_recv.at[3], {"seq": across})
            )
        if marks[0] == turns // 2:
            for pack in range(packs):
                send_branch(pack)
        if marks[0] % heads == 1 and marks[0] > heads:
            reduces[-1].across()
        if marks[0] == turns // 2:
            near[0].wait_recv()
            for copy in moved:
                copy.wait_recv()
            own = (
                out_ref[rank].astype(jnp.float32)
                + out_near_ref[0].astype(jnp.float32)
                + join_parts(out_far_a_ref[...], out_far_b_ref[...]).astype(jnp.float32)
            )
            out_own_ref[0] = own.astype(jnp.bfloat16).reshape(out_own_ref.shape[1:])
            late.advance()
        elif marks[0] > turns // 2 and late.going:
            late.advance()
        if marks[0] % 2 == 0 and ring.going:
            ring.advance()

    gain_ref[...] = jnp.zeros_like(gain_ref)
    gate_ref[...] = jnp.zeros_like(gate_ref)
    grad_stores = []
    for pack in range(packs):
        for copy in loads[pack]:
            copy.wait()

        def enter():
            raw_loads[pack].wait()
            for copy in grad_stores[pack - 1 : pack]:
                copy.wait()

        def ready():
            grad_stores.append(mover.load(grad_ref, grad_any.at[pack]))
            if pack == 0:
                wide_load.wait()
            if pack < packs - 1:
                raw_loads.append(mover.load(raw_any.at[pack + 1], raw_ref))

        attend_back_pack(
            heads, size, hook, enter, ready, mixed_a_ref.at[pack], mixed_b_ref.at[pack],
            raw_ref, query_ref.at[pack], key_ref.at[pack], value_ref.at[pack],
            inverse_ref.at[pack], cos_ref.at[pack], lead_ref.at[pack], trail_ref.at[pack],
            gains_ref, wide_ref, grad_ref, normed_ref.at[pack], gain_ref,
            wide_mixed_ref, key_t_ref, dq_ref, dk_ref, dv_ref,
        )
        if pack < packs - 1:
            reduces.append(
                CubeReduce(
                    normed_ref.at[pack], landed_ref.at[pack], total_ref.at[pack], rank, count,
                    part_send.at[pack], part_recv.at[pack],
                )
            )
            reduces[pack].near()
    mover.store(normed_ref.at[packs - 1], normed_any)
    for copy in late_loads:
        copy.wait()
    for pack in range(packs):
        finish_layer(pack)
    for pack, reduce in enumerate(reduces):
        reduced_ref[pack] = reduce.result()
    ring.finish()
    late.finish()
    for copy in near + moved + branches:
        copy.wait_send()
    for reduce in reduces:
        reduce.settle()
    grad_stores[-1].wait()
    mover.finish()


def attend_back(
    mixed_a, mixed_b, saved, turns, gains, wide, pair, out, ids, rows_all, branch_own, branch_move,
    middle_all, cot, items, heads, size,
):
    packs, count, length = mixed_a.shape[:3]
    total = count * length
    row_count = lax.axis_size("dp")
    steps = row_count // 2
    span, slab = heads * LANE, heads * size
    width = wide.shape[0]
    rows = width // row_count
    main = slab // LANE * LANE
    per = LANE // (slab - main)
    low, full = jnp.bfloat16, jnp.float32
    raw, query, key, value, inverse = saved
    pair_block, out_block = (pair.shape[0],) + pair.shape[2:], (1, rows, slab)
    inside = pl.BlockSpec(memory_space=pltpu.VMEM)
    anywhere = pl.BlockSpec(memory_space=pl.ANY)
    dma = pltpu.SemaphoreType.DMA
    inputs = [
        branch_own, branch_move, middle_all, cot, mixed_a, mixed_b, query, key, value, raw, *turns,
        wide, pair, out,
    ]
    staged = [pltpu.VMEM(entry.shape, entry.dtype) for entry in inputs]
    staged[9] = pltpu.VMEM(raw.shape[1:], full)
    return pl.pallas_call(
        partial(attend_back_kernel, heads, size, items),
        out_shape=[
            jax.ShapeDtypeStruct((packs, total, 3 * span), low),
            jax.ShapeDtypeStruct((total, width), low),
            jax.ShapeDtypeStruct((2, LANE), full),
            jax.ShapeDtypeStruct((max(packs - 1, 1), length, width), full),
            jax.ShapeDtypeStruct(pair_block, full),
            jax.ShapeDtypeStruct(out_block, full),
            jax.ShapeDtypeStruct((packs, length, width), low),
            jax.ShapeDtypeStruct(rows_all.shape[1:], full),
        ],
        in_specs=[inside] * 4 + [anywhere] * 16,
        out_specs=[anywhere] * 2 + [inside] * 6,
        scratch_shapes=staged
        + [
            pltpu.VMEM((total, 3 * span), low),
            pltpu.VMEM((packs, total, width), low),
            pltpu.VMEM((total, span), low),
            pltpu.VMEM((LANE, total), low),
            pltpu.VMEM((total, LANE), full),
            pltpu.VMEM((total, LANE), full),
            pltpu.VMEM((total, LANE), full),
            pltpu.VMEM((2, steps - 1) + pair_block, low),
            pltpu.VMEM((2, steps - 1) + out_block, low),
            pltpu.VMEM((2, steps) + pair_block, low),
            pltpu.VMEM((2, steps) + out_block, low),
            pltpu.VMEM((2, width, slab), low),
            pltpu.VMEM((width, main), low), pltpu.VMEM((width // per, LANE), low),
            pltpu.VMEM((width, main), low), pltpu.VMEM((width // per, LANE), low),
            pltpu.VMEM((1, row_count, rows, slab), low),
            pltpu.VMEM((max(packs - 1, 1), total // 2 + length, width), low),
            pltpu.VMEM((max(packs - 1, 1), length, width), low),
            pltpu.VMEM((packs, length, width), low),
            dma((2, steps, 2)), dma((2, steps, 2)), dma((2, steps, 1)), dma((2, steps, 1)),
            dma((4,)), dma((4,)), dma((max(packs - 1, 1), 2)), dma((max(packs - 1, 1), 2)),
            dma((packs,)), dma((packs,)), dma((8 + 10 * packs,)),
        ],
        compiler_params=pltpu.CompilerParams(
            collective_id=3, has_side_effects=True, vmem_limit_bytes=62 * 1024 * 1024
        ),
        name="attend_back",
    )(inverse, gains, ids, rows_all, *inputs)


def closing_kernel(
    heads, size, items, ids_ref, rows_ref, mods_ref, gate_ref, cond_ref, gain_ref, pair_ref, down_ref, out_ref,
    reduced_ref, part_any, normed_any, wide_any, tok_any, middle_any,
    tokens_ref, qkv_sum_ref, gateup_sum_ref, down_sum_ref, mod_sum_ref, bias_sum_ref,
    gain_sum_ref, square_ref,
    part_ref, normed_ref, wide_ref, tok_ref, middle_ref,
    landed_ref, total_ref, grad_a_ref, grad_b_ref, sum_a_ref, sum_b_ref, tot_a_ref, tot_b_ref,
    land_a_ref, land_b_ref, head_src_ref, head_x_ref, pair_src_ref, pair_x_ref, down_src_ref, down_x_ref,
    first_ref, mod_src_ref, mod_x_ref, mod_own_ref, mod_all_ref, norm_own_ref, norm_x_ref,
    norm_mid_ref, norm_all_ref,
    part_send, part_recv, ring_send, ring_recv, head_send, head_recv, near_send, near_recv,
    far_send, far_recv, local,
):
    rank, count = lax.axis_index("seq"), lax.axis_size("seq")
    row_rank, row_count = lax.axis_index("dp"), lax.axis_size("dp")
    packs, total, width = normed_ref.shape
    length = total // count
    slab = heads * size
    span = heads * LANE
    rows = width // row_count
    low, full = jnp.bfloat16, jnp.float32
    mover = Mover(local)
    part_load = mover.load(part_any, part_ref)
    strip_loads = [mover.load(normed_any, normed_ref), mover.load(wide_any, wide_ref)]
    token_loads = [mover.load(tok_any, tok_ref), mover.load(middle_any, middle_ref)]
    far, near = far_peers(row_rank, row_count), seq_peers(rank, count)
    part_load.wait()
    greet(far + near)

    def exchange(kind, source, target):
        return [
            send(
                source(peer["seq"]), target.at[rank], near_send.at[kind, offset],
                near_recv.at[kind, offset], peer,
            )
            for offset, peer in enumerate(near)
        ]

    reduce = CubeReduce(
        part_ref, landed_ref, total_ref, rank, count, part_send.at[0], part_recv.at[0]
    )
    reduce.near()
    for copy in strip_loads:
        copy.wait()
    strip = 2 * rows
    spread = spread_matrix(heads, size)
    cut = grad_a_ref.shape[3]
    for index in range(width // strip):
        start = index * strip
        left = [normed_ref[pack, :, start : start + strip].T for pack in range(packs)]
        pieces = []
        for part in range(3):
            grad = sum(
                dot(left[pack], wide_ref[pack, :, part * span : (part + 1) * span])
                for pack in range(packs)
            ).astype(low)
            pieces.append(dot_t(grad, spread).astype(low))
        grad = jnp.concatenate(pieces, axis=1)
        for side in range(2):
            here = slice(side * rows, (side + 1) * rows)
            grad_a_ref[0, 2 * index + side] = grad[here, :cut]
            grad_b_ref[0, 2 * index + side] = grad[here, cut:]
        if index == 0:
            reduce.across()
    ring = RingReduce(
        [grad_a_ref, grad_b_ref], [sum_a_ref, sum_b_ref], [tot_a_ref, tot_b_ref],
        [land_a_ref, land_b_ref], row_rank, row_count, ring_send, ring_recv,
    )
    ring.advance()
    for copy in token_loads:
        copy.wait()
    pair_src_ref[...] = pair_ref[...].astype(low)
    for index in range(count):
        down_src_ref[index] = down_ref[0, :, index * slab : (index + 1) * slab].astype(low)

    first_ref[...] = jnp.zeros_like(first_ref)
    for pack in range(packs):
        ids = ids_ref[pack, :length]
        normal, inverse = normalized(tok_ref[pack].astype(full))
        grad_normed = reduced_ref[pack] if pack < packs - 1 else reduce.result()
        scale = chosen(ids, rows_ref, 1, pack, items)
        tokens_ref[pack] = (
            middle_ref[pack] + normalized_back(normal, inverse, grad_normed * (1.0 + scale))
        ).astype(low)
        for which, values in enumerate((grad_normed, grad_normed * normal)):
            for item in range(items):
                line = items * pack + item
                first_ref[which, line : line + 1] = jnp.sum(
                    jnp.where(ids == item, values, 0.0), axis=0, keepdims=True
                )
    used = items * packs
    columns = mod_src_ref.shape[2]
    full_rows = jnp.concatenate(
        [first_ref[0], first_ref[1]] + [mods_ref[index] for index in range(3)] + [gate_ref[...]],
        axis=1,
    )
    for index in range(count):
        mod_src_ref[index] = full_rows[:, index * columns : (index + 1) * columns]
        mod_src_ref[index, used : used + 2, :LANE] = gain_ref[...]
    mod_near = exchange(2, lambda peer: mod_src_ref.at[peer], mod_x_ref)
    mod_x_ref[rank] = mod_src_ref[rank]
    copies = exchange(0, lambda peer: pair_src_ref.at[peer], pair_x_ref)
    pair_x_ref[rank] = pair_src_ref[rank]
    copies += exchange(1, lambda peer: down_src_ref.at[peer], down_x_ref)
    down_x_ref[rank] = down_src_ref[rank]
    ring.advance()
    for copy in mod_near:
        copy.wait_recv()
    mod_sums = sum(mod_x_ref[index] for index in range(count))
    halfway = mod_own_ref.shape[1]
    mod_own_ref[...] = jnp.concatenate(
        [mod_sums[:, :halfway], mod_sums[:, halfway:]], axis=0
    ).astype(low)
    mod_far = [
        send(
            mod_own_ref, mod_all_ref.at[row_rank], far_send.at[0, offset], far_recv.at[0, offset],
            peer,
        )
        for offset, peer in enumerate(far)
    ]
    mod_all_ref[row_rank] = mod_own_ref[...]
    ring.advance()
    for copy in mod_far:
        copy.wait_recv()
    lines = mod_all_ref.shape[1] // 2
    every = [
        jnp.concatenate([mod_all_ref[index, :lines], mod_all_ref[index, lines:]], axis=1)
        for index in range(row_count)
    ]
    conditions = cond_ref[...].reshape(row_count * lines, rows).astype(low)
    mod_sum = t_dot(conditions, jnp.concatenate(every, axis=0))
    mod_sum_ref[...] = mod_sum
    square = jnp.sum(mod_sum * mod_sum)
    gains, bias = 0.0, 0.0
    for entry in every:
        gains += entry[used : used + 2, :LANE].astype(full)
        bias += jnp.sum(entry[:used].astype(full), axis=0, keepdims=True)
    gain_sum_ref[...] = gains
    bias_sum_ref[...] = bias.reshape(-1)
    square += jnp.sum(bias * bias) * (1.0 / row_count)
    ring.advance()
    for copy in copies:
        copy.wait_recv()
    hidden_rows = down_src_ref.shape[1]
    groups = pair_ref.shape[2] // hidden_rows
    pieces = []
    for group in range(groups):
        for index in range(count):
            pieces.append(pair_x_ref[index, :, group * hidden_rows : (group + 1) * hidden_rows])
    gateup = jnp.concatenate(pieces, axis=1).astype(full)
    gateup_sum_ref[...] = gateup
    square += jnp.sum(gateup * gateup)
    down_rows = []
    for index in range(count):
        block = down_x_ref[index].astype(full)
        down_rows.append(block)
        square += jnp.sum(block * block)
    down_sum_ref[...] = jnp.concatenate(down_rows, axis=0).T
    square += jnp.sum(out_ref[...] * out_ref[...])
    ring.finish()
    summed = jnp.concatenate([sum_a_ref[0], sum_b_ref[0]], axis=1)
    square += jnp.sum(summed * summed)
    norm_own_ref[...] = jnp.full(norm_own_ref.shape, square, full)
    norm_near = exchange(3, lambda peer: norm_own_ref, norm_x_ref)
    norm_x_ref[rank] = norm_own_ref[...]
    for slot in range(3):
        head_src_ref[slot] = summed[:, slot * slab : (slot + 1) * slab]

    def head_copy(slot, index, peer):
        return pltpu.make_async_remote_copy(
            src_ref=head_src_ref.at[slot], dst_ref=head_x_ref.at[index],
            send_sem=head_send.at[slot], recv_sem=head_recv.at[index],
            device_id={"seq": peer}, device_id_type=pl.DeviceIdType.MESH,
        )

    moves = []
    for slot in range(3):
        peer, index = (slot * count + rank) // 3, (slot * count + rank) % 3
        moves.append((peer, index))

        @pl.when(peer != rank)
        def _():
            head_copy(slot, index, peer).start()

        @pl.when(peer == rank)
        def _():
            head_x_ref[index] = head_src_ref[slot]

    for copy in norm_near:
        copy.wait_recv()
    norm_mid_ref[...] = sum(norm_x_ref[index] for index in range(count))
    norm_far = [
        send(
            norm_mid_ref, norm_all_ref.at[row_rank], far_send.at[1, offset],
            far_recv.at[1, offset], peer,
        )
        for offset, peer in enumerate(far)
    ]
    norm_all_ref[row_rank] = norm_mid_ref[...]
    for index in range(3):
        source = (3 * rank + index) % count

        @pl.when(source != rank)
        def _():
            head_copy(index, index, source).wait_recv()

    qkv_sum_ref[...] = jnp.concatenate([head_x_ref[index] for index in range(3)], axis=1)
    for copy in norm_far:
        copy.wait_recv()
    squares = sum(norm_all_ref[index] for index in range(row_count))
    square_ref[...] = squares + jnp.sum(gains * gains)
    for slot, (peer, index) in enumerate(moves):
        @pl.when(peer != rank)
        def _():
            head_copy(slot, index, peer).wait_send()

    reduce.settle()
    for copy in copies + mod_near + mod_far + norm_near + norm_far:
        copy.wait_send()


def closing(
    normed, wide, part, reduced, tok, ids, rows, middle_grad, mods, gate, cond, gain, pair, down,
    out, items, heads, size,
):
    packs, total, width = normed.shape
    count, row_count = lax.axis_size("seq"), lax.axis_size("dp")
    length, slab = total // count, heads * size
    my_rows = width // row_count
    steps = row_count // 2
    low, full = jnp.bfloat16, jnp.float32
    lines = rows.shape[1]
    columns = 6 * width // count
    hidden_rows = down.shape[1]
    cut = -(-3 * slab // (2 * LANE)) * LANE
    sides = [(1, my_rows, cut), (1, my_rows, 3 * slab - cut)]
    shapes = [
        jax.ShapeDtypeStruct((packs, length, width), low),
        jax.ShapeDtypeStruct((my_rows, 3 * slab), full),
        jax.ShapeDtypeStruct((my_rows, pair.shape[0] * pair.shape[2]), full),
        jax.ShapeDtypeStruct((slab, count * hidden_rows), full),
        jax.ShapeDtypeStruct((my_rows, columns), full),
        jax.ShapeDtypeStruct((columns,), full),
        jax.ShapeDtypeStruct((2, LANE), full),
        jax.ShapeDtypeStruct((8, LANE), full),
    ]
    inside = pl.BlockSpec(memory_space=pltpu.VMEM)
    anywhere = pl.BlockSpec(memory_space=pl.ANY)
    dma = pltpu.SemaphoreType.DMA
    inputs = [part, normed, wide, tok, middle_grad]
    return pl.pallas_call(
        partial(closing_kernel, heads, size, items),
        out_shape=shapes,
        in_specs=[inside] * 10 + [anywhere] * 5,
        out_specs=[inside] * len(shapes),
        scratch_shapes=[pltpu.VMEM(entry.shape, entry.dtype) for entry in inputs]
        + [
            pltpu.VMEM((total // 2 + length, width), low),
            pltpu.VMEM((length, width), low),
        ]
        + [pltpu.VMEM((1, row_count) + side[1:], low) for side in sides]
        + [pltpu.VMEM(side, full) for side in sides]
        + [pltpu.VMEM((2, steps - 1) + side, low) for side in sides]
        + [pltpu.VMEM((2, steps) + side, low) for side in sides]
        + [
            pltpu.VMEM((3, my_rows, slab), full),
            pltpu.VMEM((3, my_rows, slab), full),
            pltpu.VMEM(pair.shape, low),
            pltpu.VMEM(pair.shape, low),
            pltpu.VMEM((count, hidden_rows, slab), low),
            pltpu.VMEM((count, hidden_rows, slab), low),
            pltpu.VMEM((2, lines, width), full),
            pltpu.VMEM((count, lines, columns), full),
            pltpu.VMEM((count, lines, columns), full),
            pltpu.VMEM((2 * lines, columns // 2), low),
            pltpu.VMEM((row_count, 2 * lines, columns // 2), low),
            pltpu.VMEM((8, LANE), full),
            pltpu.VMEM((count, 8, LANE), full),
            pltpu.VMEM((8, LANE), full),
            pltpu.VMEM((row_count, 8, LANE), full),
            dma((1, 2)), dma((1, 2)),
            dma((2, steps, 2)), dma((2, steps, 2)),
            dma((3,)), dma((3,)), dma((4, count - 1)), dma((4, count - 1)),
            dma((2, row_count - 1)), dma((2, row_count - 1)), dma((5,)),
        ],
        compiler_params=pltpu.CompilerParams(
            collective_id=4, has_side_effects=True, vmem_limit_bytes=62 * 1024 * 1024
        ),
        name="closing",
    )(ids, rows, mods, gate, cond, gain, pair, down, out, reduced, *inputs)


def adam_kernel(many, square_ref, *refs):
    grads_any, refs = refs[:many], refs[many:]
    olds_any, refs = refs[: 3 * many], refs[3 * many :]
    passed_any, refs = refs[:2], refs[2:]
    news_any, refs = refs[: 3 * many], refs[3 * many :]
    handed_any, norm_ref, refs = refs[:2], refs[2], refs[3:]
    grads, refs = refs[:many], refs[many:]
    values, refs = refs[: 3 * many], refs[3 * many :]
    held, local = refs[:2], refs[2]
    mover = Mover(local)
    loads = []
    for index in range(many):
        loads.append([mover.load(grads_any[index], grads[index])])
        for part in range(3 * index, 3 * index + 3):
            loads[index].append(mover.load(olds_any[part], values[part]))
    passing = [mover.load(source, target) for source, target in zip(passed_any, held)]
    norm = jnp.sqrt(square_ref[0:1, 0:1])
    norm_ref[0, 0] = jnp.sum(norm)
    factor = clip_limit / jnp.maximum(norm, clip_limit)
    for index in range(many):
        for copy in loads[index]:
            copy.wait()
        mine = values[3 * index : 3 * index + 3]
        if len(mine[0].shape) == 1:
            flat = [entry[...].reshape(1, -1) for entry in mine]
            updated = adam_update(*flat, grads[index][...].reshape(1, -1), factor)
            for part, value in enumerate(updated):
                mine[part][...] = value.reshape(-1)
                mover.store(mine[part], news_any[3 * index + part])
            continue
        rows, columns = mine[0].shape
        tile = 48 if rows % 48 == 0 else rows

        def step(place, carry):
            here = pl.ds(pl.multiple_of(place * tile, tile), tile)
            updated = adam_update(*(entry[here] for entry in mine), grads[index][here, :columns], factor)
            for target, value in zip(mine, updated):
                target[here] = value
            return carry

        lax.fori_loop(0, rows // tile, step, 0)
        for part in range(3):
            mover.store(mine[part], news_any[3 * index + part])
    for copy, source, target in zip(passing, held, handed_any):
        copy.wait()
        mover.store(source, target)
    mover.finish()


def adam(square, grads, olds, passed):
    many = len(grads)
    inside = pl.BlockSpec(memory_space=pltpu.VMEM)
    anywhere = pl.BlockSpec(memory_space=pl.ANY)
    flat = [entry for old in olds for entry in old]
    shape = lambda entry: jax.ShapeDtypeStruct(entry.shape, entry.dtype)
    results = pl.pallas_call(
        partial(adam_kernel, many),
        out_shape=[shape(entry) for entry in flat + passed]
        + [jax.ShapeDtypeStruct((1, 1), jnp.float32)],
        in_specs=[inside] + [anywhere] * (4 * many + 2),
        out_specs=[anywhere] * (3 * many + 2) + [pl.BlockSpec(memory_space=pltpu.SMEM)],
        scratch_shapes=[pltpu.VMEM(entry.shape, entry.dtype) for entry in grads + flat + passed]
        + [pltpu.SemaphoreType.DMA((7 * many + 4,))],
        compiler_params=pltpu.CompilerParams(vmem_limit_bytes=62 * 1024 * 1024),
        name="adam",
    )(square, *grads, *flat, *passed)
    return list(results[: 3 * many]), results[3 * many : 3 * many + 2], results[-1]


def on_device(
    tokens,
    cotangent,
    condition,
    item_lengths,
    item_widths,
    qkv_weight,
    qkv_first,
    qkv_second,
    out_weight,
    out_first,
    out_second,
    gateup_weight,
    gateup_first,
    gateup_second,
    down_weight,
    down_first,
    down_second,
    mod_weight,
    mod_first,
    mod_second,
    mod_bias,
    bias_first,
    bias_second,
    qk_gains,
    gains_first,
    gains_second,
):
    packs, length, width = tokens.shape
    items = condition.shape[1]
    size = width // HEADS
    count, row_count = lax.axis_size("seq"), lax.axis_size("dp")
    heads = HEADS // count
    rows = qkv_weight.shape[0]

    lines = -(-(packs * items + 2) // 8) * 8
    (
        tok_first, cot_first, ids, cos, lead, trail, mod_rows, cond_rows, wide, out_a, out_b, pair_own,
        down_own,
    ) = opening(
        item_lengths, item_widths, tokens, cotangent, jnp.swapaxes(condition, 0, 1), qkv_weight,
        out_weight, gateup_weight, down_weight.T, mod_weight, mod_bias, lines, heads, size,
    )
    turns = (cos, lead, trail)
    wide = wide.reshape(width, wide.shape[2])
    (
        normed, raw, query, key, value, inverse, mixed_a, mixed_b, out_full, pair_all, cot_later,
    ) = attend(
        tok_first, tokens, ids, mod_rows, turns, qk_gains, wide, out_a, out_b, pair_own, cotangent, items,
        heads, size,
    )
    (
        middle_all, branch_own, branch_move, grad_a, grad_b, grad_middle, mod_part, pair_grad,
        down_sum, out_grad,
    ) = middle(
        mixed_a, mixed_b, tokens, ids, mod_rows, cotangent, cot_first, cot_later,
        out_full.reshape(width, width), pair_all.reshape(width, -1), down_own, items,
    )
    grad_wide, grad_part, gain_part, reduced, pair_sum, out_sum, layer_out, gate_part = attend_back(
        grad_a, grad_b, (raw, query, key, value, inverse), turns, qk_gains, wide,
        pair_grad.reshape(count, row_count, rows, -1), out_grad, ids, mod_rows, branch_own,
        branch_move, middle_all, cotangent, items, heads, size,
    )
    tokens_grad, qkv_sum, gateup_sum, down_sum, mod_sum, bias_sum, gain_sum, square = closing(
        normed, grad_wide, grad_part, reduced, tokens, ids, mod_rows, grad_middle, mod_part,
        gate_part, cond_rows, gain_part, pair_sum, down_sum, out_sum, items, heads, size,
    )
    news, outs, norm = adam(
        square, [qkv_sum, out_sum[0], gateup_sum, down_sum, mod_sum, bias_sum, gain_sum],
        [
            (qkv_weight, qkv_first, qkv_second), (out_weight, out_first, out_second),
            (gateup_weight, gateup_first, gateup_second),
            (down_weight.T, down_first.T, down_second.T), (mod_weight, mod_first, mod_second),
            (mod_bias, bias_first, bias_second),
            (qk_gains, gains_first, gains_second),
        ],
        [layer_out, tokens_grad],
    )
    news[9:12] = [entry.T for entry in news[9:12]]
    return tuple(list(outs) + [norm.reshape(())] + list(news))


def solution(mesh):
    return jax.shard_map(
        on_device,
        mesh=mesh,
        in_specs=(
            P("dp", "seq", None),
            P("dp", "seq", None),
            P("dp", None, None),
            P("dp", None),
            P("dp", None),
            P("dp", "seq"),
            P("dp", "seq"),
            P("dp", "seq"),
            P("dp", "seq"),
            P("dp", "seq"),
            P("dp", "seq"),
            P("dp", "seq"),
            P("dp", "seq"),
            P("dp", "seq"),
            P("dp", "seq"),
            P("dp", "seq"),
            P("dp", "seq"),
            P("dp", "seq"),
            P("dp", "seq"),
            P("dp", "seq"),
            P("seq"),
            P("seq"),
            P("seq"),
            P(),
            P(),
            P(),
        ),
        out_specs=(
            P("dp", "seq", None),
            P("dp", "seq", None),
            P(),
            P("dp", "seq"),
            P("dp", "seq"),
            P("dp", "seq"),
            P("dp", "seq"),
            P("dp", "seq"),
            P("dp", "seq"),
            P("dp", "seq"),
            P("dp", "seq"),
            P("dp", "seq"),
            P("dp", "seq"),
            P("dp", "seq"),
            P("dp", "seq"),
            P("dp", "seq"),
            P("dp", "seq"),
            P("dp", "seq"),
            P("seq"),
            P("seq"),
            P("seq"),
            P(),
            P(),
            P(),
        ),
        check_vma=False,
    )
```
